32 devices in a mesh: batch: 8 (over z, x), mp: 4 (over y, core).
Axes of the slice: x: 2, y: 2, z: 4, core: 2. Of those that a mesh axis runs over, the one named last changes fastest.
Arguments:
- query_hidden: bfloat16 [8192, 768], P(('batch', 'mp')), may hold values from -28 to 28
- passage_hidden: bfloat16 [40960, 768], P(('batch', 'mp')), may hold values from -28 to 28
- projection: bfloat16 [768, 128], replicated, may hold values from -0.21875 to 0.21875
- query_lengths: int32 [256], P(('batch', 'mp')), may hold values from 8 to 32, as said below
- passage_lengths: int32 [320], P(('batch', 'mp')), may hold values from 64 to 128, as said below
- positives: int32 [256], P(('batch', 'mp')), may hold values from 0 to 9
Outputs:
- query_loss: float32 [256], P(('batch', 'mp'))
- grad_query_hidden: bfloat16 [8192, 768], P(('batch', 'mp'))
- grad_passage_hidden: bfloat16 [40960, 768], P(('batch', 'mp'))
- grad_projection: float32 [768, 128], replicated
The draws below stay inside these ranges and needn't reach their ends.
Inputs may be any that keep to these rules, and one draw needn't show every extreme that they name: `query_lengths`: the first query of each block of 8 queries has all 32 tokens. `passage_lengths`: the first passage of each block of 10 passages has all 128 tokens.
All inputs are finite; a program needn't handle non-finite values.
Results may differ from the reference program's by a relative error of at most 0.012.
The reference program's roundings to bfloat16 on the way (of `query_embed`, `passage_embed`, `grad_sim`, `query_pre_grad` and `passage_pre_grad`) count: a program that leaves them out, or rounds other values in their place, can miss the bound.
Values may be sent and summed in bfloat16 or wider, within the bound.
No kernel may reach another device: no remote copies, remote signals or barrier semaphores. Data moves between devices by JAX's collectives and lax.ppermute only.
A program may use at most 64 MiB of HBM per device.

```python
import jax
import jax.numpy as jnp
from jax import lax

H = 768
DIM = 128
QL = 32
PL = 128
BQ = 8
BP = 10
BLOCKS = 32
STRIDE = 4
NQ = 256
NP = 320
N_BATCH = 8
N_MP = 4


def query_rows(key):
    rows = NQ * QL
    noise = jnp.clip(jax.random.normal(jax.random.fold_in(key, 101), (rows, H), jnp.float32), -4.0, 4.0)
    return noise


def draw_query_hidden(key, part):
    values = query_rows(key)
    return values.astype(jnp.bfloat16)


def draw_passage_hidden(key, part):
    rows = NP * PL
    noise = jnp.clip(jax.random.normal(jax.random.fold_in(key, 201), (rows, H), jnp.float32), -4.0, 4.0)
    values = noise
    return values.astype(jnp.bfloat16)


def draw_query_lengths(key, part):
    lengths = jax.random.randint(jax.random.fold_in(key, 301), (NQ // BQ, BQ), QL // 4, QL + 1, jnp.int32)
    lengths = lengths.at[:, 0].set(QL)
    return lengths.reshape(NQ)


def draw_passage_lengths(key, part):
    lengths = jax.random.randint(jax.random.fold_in(key, 302), (NP // BP, BP), PL // 2, PL + 1, jnp.int32)
    lengths = lengths.at[:, 0].set(PL)
    return lengths.reshape(NP)


def place_ends(result, own_key, low, high):
    longest = result.shape.index(max(result.shape))
    spots = []
    for shift in (0, 1):
        where = [jax.random.randint(jax.random.fold_in(own_key, axis), (), 0, length) for axis, length in enumerate(result.shape)]
        where[longest] = (where[longest] + shift) % result.shape[longest]
        spots.append(tuple(where))
    return result.at[spots[0]].set(low).at[spots[1]].set(high)


def bell_draw(own_key, shape, spread, bound, held_as=jnp.bfloat16):
    drawn = jax.random.normal(own_key, shape, jnp.float32) * spread
    return jnp.minimum(jnp.maximum(drawn, -bound), bound).astype(held_as)


def setup_inputs(seed: int = 0) -> dict:
    keys = jax.random.split(jax.random.key(seed), 7)
    query_hidden = draw_query_hidden(jax.random.fold_in(keys[6], 71), 0)
    passage_hidden = draw_passage_hidden(jax.random.fold_in(keys[6], 71), 0)
    projection = bell_draw(keys[2], (H, DIM), H ** -0.5, 0.21875)
    query_lengths = draw_query_lengths(jax.random.fold_in(keys[6], 71), 0)
    passage_lengths = draw_passage_lengths(jax.random.fold_in(keys[6], 71), 0)
    positives = place_ends(jax.random.randint(keys[5], (NQ,), 0, BP), jax.random.fold_in(keys[5], 1), 0, BP - 1).astype(jnp.int32)
    return {"query_hidden": query_hidden, "passage_hidden": passage_hidden, "projection": projection, "query_lengths": query_lengths, "passage_lengths": passage_lengths, "positives": positives}


inner_scale = 128.0
outer_scale = 8.0
loss_scale = 32.0
norm_eps = 1e-06

def embed_rows(hidden, projection):
    before = jnp.dot(hidden, projection, preferred_element_type=jnp.float32)
    radius = jnp.sqrt(lax.optimization_barrier(jnp.sum(before * before, axis=-1, keepdims=True)) + norm_eps)
    return (before / radius, radius)

def candidate_block(query_embed, passage_embed, passage_valid, query_keep):
    queries, query_tokens = query_keep.shape
    passages, passage_tokens = passage_valid.shape
    sims = jnp.dot(query_embed, passage_embed.T, preferred_element_type=jnp.float32)
    sims = sims.reshape(queries, query_tokens, passages, passage_tokens)
    logits = jnp.where(passage_valid[None, None], sims * inner_scale, -jnp.inf)
    row_top = lax.optimization_barrier(jnp.max(logits, axis=-1, keepdims=True))
    powers = jnp.exp(logits - row_top)
    totals = lax.optimization_barrier(jnp.sum(powers, axis=-1, keepdims=True))
    weights = powers / totals
    best = (jnp.log(totals[..., 0]) + row_top[..., 0]) / inner_scale
    scores = outer_scale * lax.optimization_barrier(jnp.sum(query_keep[:, :, None] * best, axis=1))
    return (scores, weights)

def softmax_loss(scores, positives):
    row_top = lax.optimization_barrier(jnp.max(scores, axis=1, keepdims=True))
    totals = lax.optimization_barrier(jnp.sum(jnp.exp(scores - row_top), axis=1, keepdims=True))
    log_total = row_top + jnp.log(totals)
    probs = jnp.exp(scores - log_total)
    columns = jnp.arange(scores.shape[1], dtype=jnp.int32)
    onehot = (columns[None, :] == positives[:, None]).astype(jnp.float32)
    losses = log_total[:, 0] - lax.optimization_barrier(jnp.sum(onehot * scores, axis=1))
    return (losses, loss_scale * (probs - onehot))

def block_grads(dscores, query_keep, weights, query_embed, passage_embed):
    grad_sim = (outer_scale * dscores[:, None, :, None] * query_keep[:, :, None, None] * weights).astype(jnp.bfloat16)
    flat = grad_sim.reshape(query_embed.shape[0], passage_embed.shape[0])
    to_query = jnp.dot(flat, passage_embed, preferred_element_type=jnp.float32)
    to_passage = lax.dot_general(flat, query_embed, (((0,), (0,)), ((), ())), preferred_element_type=jnp.float32)
    return (to_query, to_passage)

def back_norm(grad, unit, radius):
    return ((grad - unit * lax.optimization_barrier(jnp.sum(unit * grad, axis=-1, keepdims=True))) / radius).astype(jnp.bfloat16)

def contract_rows(left, right):
    return lax.dot_general(left, right, (((0,), (0,)), ((), ())), preferred_element_type=jnp.float32)

def reference(query_hidden, passage_hidden, projection, query_lengths, passage_lengths, positives):
    query_unit, query_radius = embed_rows(query_hidden, projection)
    passage_unit, passage_radius = embed_rows(passage_hidden, projection)
    query_embed = query_unit.astype(jnp.bfloat16).reshape(BLOCKS, BQ * QL, DIM)
    passage_embed = passage_unit.astype(jnp.bfloat16).reshape(BLOCKS, BP * PL, DIM)
    block_lengths = passage_lengths.reshape(BLOCKS, BP)
    windows = [jnp.roll(passage_embed, -column * STRIDE, axis=0) for column in range(3)]
    window_lengths = [jnp.roll(block_lengths, -column * STRIDE, axis=0) for column in range(3)]

    def one_block(items):
        query_block, first, second, third, len_first, len_second, len_third, lengths_block, positive_block = items
        query_keep = (jnp.arange(QL, dtype=jnp.int32)[None, :] < lengths_block[:, None]).astype(jnp.float32)
        slots = jnp.arange(PL, dtype=jnp.int32)
        members = [(first, len_first), (second, len_second), (third, len_third)]
        score_list = []
        weight_list = []
        for member in members:
            valid = slots[None, :] < member[1][:, None]
            scores, weights = candidate_block(query_block, member[0], valid, query_keep)
            score_list.append(scores)
            weight_list.append(weights)
        losses, dscores = softmax_loss(jnp.concatenate(score_list, axis=1), positive_block)
        query_grad = jnp.zeros((BQ * QL, DIM), jnp.float32)
        passage_terms = []
        for column in range(3):
            to_query, to_passage = block_grads(dscores[:, column * BP:(column + 1) * BP], query_keep, weight_list[column], query_block, members[column][0])
            query_grad = query_grad + to_query
            passage_terms.append(to_passage)
        return (query_grad, jnp.stack(passage_terms), losses)
    query_grad, terms, losses = lax.map(one_block, (query_embed, windows[0], windows[1], windows[2], window_lengths[0], window_lengths[1], window_lengths[2], query_lengths.reshape(BLOCKS, BQ), positives.reshape(BLOCKS, BQ)))
    passage_grad = terms[:, 0] + jnp.roll(terms[:, 1], STRIDE, axis=0) + jnp.roll(terms[:, 2], 2 * STRIDE, axis=0)
    query_pre_grad = back_norm(query_grad.reshape(NQ * QL, DIM), query_unit, query_radius)
    passage_pre_grad = back_norm(passage_grad.reshape(NP * PL, DIM), passage_unit, passage_radius)
    grad_query_hidden = jnp.dot(query_pre_grad, projection.T, preferred_element_type=jnp.float32).astype(jnp.bfloat16)
    grad_passage_hidden = jnp.dot(passage_pre_grad, projection.T, preferred_element_type=jnp.float32).astype(jnp.bfloat16)
    grad_projection = (contract_rows(query_hidden, query_pre_grad) + contract_rows(passage_hidden, passage_pre_grad)) / (N_BATCH * N_MP)
    return (losses.reshape(NQ), grad_query_hidden, grad_passage_hidden, grad_projection)
```

```python
import jax
import jax.numpy as jnp
from jax import lax
from jax.sharding import PartitionSpec as P

inner_scale = 128.0
outer_scale = 8.0
loss_scale = 32.0
norm_eps = 1e-06


def shifted(block, axis, distance):
    devices = range(lax.axis_size(axis))
    route = [((i - distance) % len(devices), i) for i in devices]
    return lax.ppermute(block, axis, route)


def embed_rows(hidden, projection):
    before = jnp.dot(hidden, projection, preferred_element_type=jnp.float32)
    radius = jnp.sqrt(jnp.sum(before * before, axis=-1, keepdims=True) + norm_eps)
    return (before / radius, radius)


def candidate_block(query_embed, passage_embed, passage_valid, query_keep):
    queries, query_tokens = query_keep.shape
    passages, passage_tokens = passage_valid.shape
    sims = jnp.dot(query_embed, passage_embed.T, preferred_element_type=jnp.float32)
    sims = sims.reshape(queries, query_tokens, passages, passage_tokens)
    logits = jnp.where(passage_valid[None, None], sims * inner_scale, -jnp.inf)
    row_top = jnp.max(logits, axis=-1, keepdims=True)
    powers = jnp.exp(logits - row_top)
    totals = jnp.sum(powers, axis=-1, keepdims=True)
    weights = powers / totals
    best = (jnp.log(totals[..., 0]) + row_top[..., 0]) / inner_scale
    scores = outer_scale * jnp.sum(query_keep[:, :, None] * best, axis=1)
    return (scores, weights)


def softmax_loss(scores, positives):
    row_top = jnp.max(scores, axis=1, keepdims=True)
    totals = jnp.sum(jnp.exp(scores - row_top), axis=1, keepdims=True)
    log_total = row_top + jnp.log(totals)
    probs = jnp.exp(scores - log_total)
    columns = jnp.arange(scores.shape[1], dtype=jnp.int32)
    onehot = (columns[None, :] == positives[:, None]).astype(jnp.float32)
    losses = log_total[:, 0] - jnp.sum(onehot * scores, axis=1)
    return (losses, loss_scale * (probs - onehot))


def block_grads(dscores, query_keep, weights, query_embed, passage_embed):
    grad_sim = (
        outer_scale * dscores[:, None, :, None] * query_keep[:, :, None, None] * weights
    ).astype(jnp.bfloat16)
    flat = grad_sim.reshape(query_embed.shape[0], passage_embed.shape[0])
    to_query = jnp.dot(flat, passage_embed, preferred_element_type=jnp.float32)
    to_passage = lax.dot_general(
        flat, query_embed, (((0,), (0,)), ((), ())), preferred_element_type=jnp.float32
    )
    return (to_query, to_passage)


def back_norm(grad, unit, radius):
    return ((grad - unit * jnp.sum(unit * grad, axis=-1, keepdims=True)) / radius).astype(
        jnp.bfloat16
    )


def contract_rows(left, right):
    return lax.dot_general(
        left, right, (((0,), (0,)), ((), ())), preferred_element_type=jnp.float32
    )


def mean_over_devices(partial):
    axes = ("batch", "mp")
    devices = lax.axis_size("batch") * lax.axis_size("mp")
    rows, columns = partial.shape
    share = -(-rows // (devices * 8)) * 8
    padded = jnp.pad(partial.astype(jnp.bfloat16), ((0, share * devices - rows), (0, 0)))
    pieces = padded.reshape(devices, share, columns)
    pieces = lax.all_to_all(pieces, axes, 0, 0)
    mean = (jnp.sum(pieces.astype(jnp.float32), axis=0) / devices).astype(jnp.bfloat16)
    whole = lax.all_to_all(jnp.broadcast_to(mean[None], (devices, share, columns)), axes, 0, 0)
    return whole.reshape(devices * share, columns)[:rows].astype(jnp.float32)


def per_device(query_hidden, passage_hidden, projection, query_lengths, passage_lengths, positives):
    queries = query_lengths.shape[0]
    passages = passage_lengths.shape[0]
    query_tokens = query_hidden.shape[0] // queries
    passage_tokens = passage_hidden.shape[0] // passages
    query_unit, query_radius = embed_rows(query_hidden, projection)
    passage_unit, passage_radius = embed_rows(passage_hidden, projection)
    query_embed = query_unit.astype(jnp.bfloat16)
    passage_embed = passage_unit.astype(jnp.bfloat16)
    length_values = passage_lengths.astype(jnp.bfloat16)
    query_keep = (
        jnp.arange(query_tokens, dtype=jnp.int32)[None, :] < query_lengths[:, None]
    ).astype(jnp.float32)
    slots = jnp.arange(passage_tokens, dtype=jnp.float32)
    members = [(passage_embed, length_values)]
    current = (passage_embed, length_values)
    for repeat in range(2):
        current = shifted((current[0], current[1]), "batch", -1)
        members.append(current)
    score_list = []
    weight_list = []
    for member in members:
        valid = slots[None, :] < member[1].astype(jnp.float32)[:, None]
        scores, weights = candidate_block(query_embed, member[0], valid, query_keep)
        score_list.append(scores)
        weight_list.append(weights)
    losses, dscores = softmax_loss(jnp.concatenate(score_list, axis=1), positives)
    query_grad = jnp.zeros(query_unit.shape, jnp.float32)
    passage_terms = []
    for column in range(3):
        to_query, to_passage = block_grads(
            dscores[:, column * passages : (column + 1) * passages],
            query_keep,
            weight_list[column],
            query_embed,
            members[column][0],
        )
        query_grad = query_grad + to_query
        passage_terms.append(to_passage)
    query_pre_grad = back_norm(query_grad, query_unit, query_radius)
    query_partial = contract_rows(query_hidden, query_pre_grad)
    carried = passage_terms[2]
    for repeat in range(2):
        carried = (
            shifted(carried.astype(jnp.bfloat16), "batch", 1).astype(carried.dtype)
            + passage_terms[1 - repeat]
        )
    passage_pre_grad = back_norm(carried, passage_unit, passage_radius)
    grad_query_hidden = jnp.dot(
        query_pre_grad, projection.T, preferred_element_type=jnp.float32
    ).astype(jnp.bfloat16)
    grad_passage_hidden = jnp.dot(
        passage_pre_grad, projection.T, preferred_element_type=jnp.float32
    ).astype(jnp.bfloat16)
    passage_partial = contract_rows(passage_hidden, passage_pre_grad)
    grad_projection = mean_over_devices(query_partial + passage_partial)
    return (losses, grad_query_hidden, grad_passage_hidden, grad_projection)


def solution(mesh):
    in_specs = (
        P(("batch", "mp"), None),
        P(("batch", "mp"), None),
        P(),
        P(("batch", "mp")),
        P(("batch", "mp")),
        P(("batch", "mp")),
    )
    out_specs = (P(("batch", "mp")), P(("batch", "mp"), None), P(("batch", "mp"), None), P())
    return jax.shard_map(
        per_device, mesh=mesh, in_specs=in_specs, out_specs=out_specs, check_vma=False
    )
```

```python
import functools
import math

import jax
import jax.numpy as jnp
from jax import lax
from jax.experimental import pallas as pl
from jax.experimental.pallas import tpu as pltpu
from jax.sharding import PartitionSpec as P

inner_scale = 128.0
outer_scale = 8.0
loss_scale = 32.0
norm_eps = 1e-06

LANES = 128
ROWS = 16
LOG2E = 1.0 / math.log(2.0)
NT = (((1,), (1,)), ((), ()))

vmem = pl.BlockSpec(memory_space=pltpu.VMEM)
smem = pl.BlockSpec(memory_space=pltpu.SMEM)


def shifted(block, axis, distance):
    devices = range(lax.axis_size(axis))
    route = [((i - distance) % len(devices), i) for i in devices]
    return lax.ppermute(block, axis, route)


def dot32(left, right, dims=(((1,), (0,)), ((), ()))):
    return lax.dot_general(left, right, dims, preferred_element_type=jnp.float32)


def call(body, outs, in_specs, args, scratch=(), flops=0, trans=0):
    moved = sum(a.size * a.dtype.itemsize for a in args)
    moved += sum(math.prod(o.shape) * o.dtype.itemsize for o in outs)
    return pl.pallas_call(
        body,
        out_shape=tuple(outs),
        in_specs=list(in_specs),
        out_specs=tuple(vmem for _ in outs),
        scratch_shapes=list(scratch),
        compiler_params=pltpu.CompilerParams(vmem_limit_bytes=24 * 2**20),
        cost_estimate=pl.CostEstimate(flops=flops, bytes_accessed=moved, transcendentals=trans),
    )(*args)


def spread(values, count, group):
    lane = lax.broadcasted_iota(jnp.int32, (1, count * group), 1) // group
    row = jnp.zeros((1, count * group), jnp.int32)
    for item in range(count):
        row = jnp.where(lane == item, values[item], row)
    return row


def keep_row(lengths, queries, tokens):
    slot = lax.broadcasted_iota(jnp.int32, (1, queries * tokens), 1) % tokens
    return (slot < spread(lengths, queries, tokens)).astype(jnp.float32)


def unit_rows(before):
    inverse = lax.rsqrt(jnp.sum(before * before, axis=1, keepdims=True) + norm_eps)
    return before * inverse, inverse


def back_rows(grad, before):
    unit, inverse = unit_rows(before)
    inner = jnp.sum(unit * grad, axis=1, keepdims=True)
    return ((grad - unit * inner) * inverse).astype(jnp.bfloat16)


def query_embed_body(queries, lengths, hidden, projection, before_out, sent_out):
    rows = hidden.shape[0]
    before = dot32(hidden[...], projection[...])
    before_out[...] = before
    sent_out[:rows, :] = unit_rows(before)[0].astype(jnp.bfloat16)
    keep = keep_row(lengths, queries, rows // queries)
    row = lax.broadcasted_iota(jnp.int32, (ROWS, LANES), 0)
    tail = jnp.zeros((ROWS, LANES), jnp.float32)
    for piece in range(rows // LANES):
        tail = jnp.where(row == piece, keep[:, piece * LANES : (piece + 1) * LANES], tail)
    sent_out[rows:, :] = tail.astype(jnp.bfloat16)


def sent_keep(sent, rows):
    tail = sent[rows:, :].astype(jnp.float32)
    return jnp.concatenate([tail[i : i + 1, :] for i in range(rows // LANES)], axis=1)


def score_block(queries, passages, lengths, embed, sent, powers, totals, scores, tops):
    rows = sent.shape[0] - ROWS
    tokens = embed.shape[0] // passages
    query = sent[:rows, :]
    slot = lax.broadcasted_iota(jnp.int32, (tokens, rows), 0)
    totals[...] = jnp.ones(totals.shape, jnp.float32)
    tops[...] = jnp.zeros(tops.shape, jnp.float32)
    for c in range(passages):
        part = slice(c * tokens, (c + 1) * tokens)
        sims = dot32(embed[part, :], query, NT)
        sims = jnp.where(slot < lengths[c], sims, -jnp.inf)
        top = jnp.max(sims, axis=0, keepdims=True)
        power = jnp.exp2((sims - top) * (inner_scale * LOG2E))
        powers[part, :] = power
        tops[c : c + 1, :] = top
        totals[c : c + 1, :] = jnp.sum(power, axis=0, keepdims=True)
    best = tops[...] + jnp.log(totals[...]) / inner_scale
    best = best * sent_keep(sent, rows)
    group = rows // queries
    same = lax.broadcasted_iota(jnp.int32, (rows, rows), 0) // group
    same = (same == lax.broadcasted_iota(jnp.int32, (rows, rows), 1) // group).astype(jnp.bfloat16)
    high = best.astype(jnp.bfloat16)
    rest = best - high.astype(jnp.float32)
    middle = rest.astype(jnp.bfloat16)
    low = (rest - middle.astype(jnp.float32)).astype(jnp.bfloat16)
    total = dot32(high, same) + dot32(middle, same) + dot32(low, same)
    c = lax.broadcasted_iota(jnp.int32, total.shape, 0)
    scores[...] = jnp.where(c < passages, outer_scale * total, -jnp.inf)


def own_score_body(
    queries, lengths, hidden, projection, sent, before_out, embed_out, powers, totals, scores, tops
):
    before = dot32(hidden[...], projection[...])
    before_out[...] = before
    embed_out[...] = unit_rows(before)[0].astype(jnp.bfloat16)
    score_block(
        queries, lengths.shape[0], lengths, embed_out, sent, powers, totals, scores, tops
    )


def other_score_body(
    queries, lengths, embed, sent1, sent2, powers1, powers2, totals1, totals2, scores1, scores2, tops
):
    passages = lengths.shape[0]
    score_block(queries, passages, lengths, embed, sent1, powers1, totals1, scores1, tops)
    score_block(queries, passages, lengths, embed, sent2, powers2, totals2, scores2, tops)


def score_softmax(first, second, third):
    parts = (first, second, third)
    top = functools.reduce(
        jnp.maximum, [jnp.max(part, axis=0, keepdims=True) for part in parts]
    )
    total = sum(jnp.sum(jnp.exp(part - top), axis=0, keepdims=True) for part in parts)
    return top + jnp.log(total)


def fill_grad_sim(passages, coefficient, powers, out, column):
    tokens = powers.shape[0] // passages
    rows = powers.shape[1]
    for c in range(passages):
        part = slice(c * tokens, (c + 1) * tokens)
        out[part, column : column + rows] = (powers[part, :] * coefficient[c : c + 1, :]).astype(
            jnp.bfloat16
        )


def other_grad_body(
    passages, embed, powers1, powers2, totals1, totals2, sent1, sent2,
    first1, own1, third1, first2, second2, own2, to_query1, to_query2, grad_sim,
):
    rows = powers1.shape[1]
    turned = embed[...].T
    for column, powers, totals, sent, parts, own, out in (
        (rows, powers2, totals2, sent2, (first2, second2, own2), own2, to_query2),
        (0, powers1, totals1, sent1, (first1, own1, third1), own1, to_query1),
    ):
        log_total = score_softmax(*[part[...] for part in parts])
        dscore = loss_scale * jnp.exp(own[...] - log_total)
        coefficient = outer_scale * dscore * sent_keep(sent, rows) / totals[...]
        fill_grad_sim(passages, coefficient, powers, grad_sim, column)
        out[...] = dot32(turned, grad_sim[:, column : column + rows]).astype(jnp.bfloat16)


def own_grad_body(
    queries, passages, positives, hidden, embed, before, powers, totals, sent0, sent1, sent2,
    own, second, third, other_grad_sim,
    losses, to_query, pre_grad, partial, grad_sim,
):
    rows = powers.shape[1]
    scores = own[...]
    log_total = score_softmax(scores, second[...], third[...])
    wanted = spread(positives, queries, rows // queries)
    onehot = lax.broadcasted_iota(jnp.int32, scores.shape, 0) == wanted
    losses[...] = log_total - jnp.sum(jnp.where(onehot, scores, 0.0), axis=0, keepdims=True)
    dscore = loss_scale * (jnp.exp(scores - log_total) - onehot.astype(jnp.float32))
    coefficient = outer_scale * dscore * sent_keep(sent0, rows) / totals[...]
    fill_grad_sim(passages, coefficient, powers, grad_sim, 0)
    to_query[...] = dot32(embed[...].T, grad_sim[...])
    grad = dot32(grad_sim[...], sent0[:rows, :])
    grad += dot32(other_grad_sim[:, :rows], sent1[:rows, :])
    grad += dot32(other_grad_sim[:, rows:], sent2[:rows, :])
    pre = back_rows(grad, before[...])
    pre_grad[...] = pre
    partial[...] = dot32(pre.T, hidden[...])


def query_grad_body(hidden, before, own, back1, back2, passage_partial, pre_grad, partial):
    total = own[...] + back1[...].astype(jnp.float32) + back2[...].astype(jnp.float32)
    pre = back_rows(total.T, before[...])
    pre_grad[...] = pre
    both = passage_partial[...] + dot32(pre.T, hidden[...])
    partial[...] = both.T.astype(jnp.bfloat16)


def mean_over_devices(partial):
    axes = ("batch", "mp")
    devices = lax.axis_size("batch") * lax.axis_size("mp")
    rows, columns = partial.shape
    share = -(-rows // (devices * 8)) * 8
    padded = jnp.pad(partial, ((0, share * devices - rows), (0, 0)))
    pieces = padded.reshape(devices, share, columns)
    pieces = lax.all_to_all(pieces, axes, 0, 0)
    mean = (jnp.sum(pieces.astype(jnp.float32), axis=0) / devices).astype(jnp.bfloat16)
    whole = lax.all_to_all(jnp.broadcast_to(mean[None], (devices, share, columns)), axes, 0, 0)
    return whole.reshape(devices * share, columns)[:rows].astype(jnp.float32)


def per_device(query_hidden, passage_hidden, projection, query_lengths, passage_lengths, positives):
    queries = query_lengths.shape[0]
    passages = passage_lengths.shape[0]
    rows, width = query_hidden.shape
    slots = passage_hidden.shape[0]
    dim = projection.shape[1]
    f32, bf16 = jnp.float32, jnp.bfloat16
    of = jax.ShapeDtypeStruct
    pair = of((ROWS, rows), f32)
    pairs = pltpu.VMEM((ROWS, rows), f32)

    query_before, sent0 = call(
        functools.partial(query_embed_body, queries),
        (of((rows, dim), f32), of((rows + ROWS, dim), bf16)),
        (smem, vmem, vmem),
        (query_lengths, query_hidden, projection),
        flops=2 * rows * width * dim,
    )
    sent1 = shifted(sent0, "batch", 1)
    sent2 = shifted(sent0, "batch", 2)
    passage_before, embed, powers0, totals0, scores0 = call(
        functools.partial(own_score_body, queries),
        (of((slots, dim), f32), of((slots, dim), bf16), of((slots, rows), f32), pair, pair),
        (smem, vmem, vmem, vmem),
        (passage_lengths, passage_hidden, projection, sent0),
        scratch=(pairs,),
        flops=2 * slots * dim * (width + rows),
        trans=slots * rows,
    )
    first1 = shifted(scores0, "batch", 1)
    first2 = shifted(scores0, "batch", 2)
    powers1, powers2, totals1, totals2, scores1, scores2 = call(
        functools.partial(other_score_body, queries),
        (of((slots, rows), f32),) * 2 + (pair,) * 4,
        (smem, vmem, vmem, vmem),
        (passage_lengths, embed, sent1, sent2),
        scratch=(pairs,),
        flops=4 * slots * dim * rows,
        trans=2 * slots * rows,
    )
    second2 = shifted(scores1, "batch", 1)
    below = shifted(jnp.concatenate([scores1, scores2], axis=0), "batch", -1)
    second0, third1 = below[:ROWS], below[ROWS:]
    third0 = shifted(scores2, "batch", -2)
    to_query1, to_query2, grad_sim = call(
        functools.partial(other_grad_body, passages),
        (of((dim, rows), bf16),) * 2 + (of((slots, 2 * rows), bf16),),
        (vmem,) * 13,
        (embed, powers1, powers2, totals1, totals2, sent1, sent2,
         first1, scores1, third1, first2, second2, scores2),
        flops=4 * slots * dim * rows,
    )
    back1 = shifted(to_query1, "batch", -1)
    back2 = shifted(to_query2, "batch", -2)
    losses, to_query0, passage_pre_grad, passage_partial = call(
        functools.partial(own_grad_body, queries, passages),
        (of((1, rows), f32), of((dim, rows), f32), of((slots, dim), bf16), of((dim, width), f32)),
        (smem,) + (vmem,) * 12,
        (positives, passage_hidden, embed, passage_before, powers0, totals0, sent0, sent1, sent2,
         scores0, second0, third0, grad_sim),
        scratch=(pltpu.VMEM((slots, rows), bf16),),
        flops=8 * slots * dim * rows + 2 * slots * width * dim,
    )
    query_pre_grad, partial = call(
        query_grad_body,
        (of((rows, dim), bf16), of((width, dim), bf16)),
        (vmem,) * 6,
        (query_hidden, query_before, to_query0, back1, back2, passage_partial),
        flops=2 * rows * width * dim,
    )
    grad_projection = mean_over_devices(partial)
    grad_query_hidden = dot32(query_pre_grad, projection, NT).astype(bf16)
    grad_passage_hidden = dot32(passage_pre_grad, projection, NT).astype(bf16)
    losses = losses.reshape(queries, rows // queries)[:, 0]
    return (losses, grad_query_hidden, grad_passage_hidden, grad_projection)


def solution(mesh):
    in_specs = (
        P(("batch", "mp"), None),
        P(("batch", "mp"), None),
        P(),
        P(("batch", "mp")),
        P(("batch", "mp")),
        P(("batch", "mp")),
    )
    out_specs = (P(("batch", "mp")), P(("batch", "mp"), None), P(("batch", "mp"), None), P())
    return jax.shard_map(
        per_device, mesh=mesh, in_specs=in_specs, out_specs=out_specs, check_vma=False
    )
```

```python
import functools
import math

import jax
import jax.numpy as jnp
from jax import lax
from jax.experimental import pallas as pl
from jax.experimental.pallas import tpu as pltpu
from jax.sharding import PartitionSpec as P

inner_scale = 128.0
outer_scale = 8.0
loss_scale = 32.0
norm_eps = 1e-06

LANES = 128
ROWS = 16
LOG2E = 1.0 / math.log(2.0)
NT = (((1,), (1,)), ((), ()))

vmem = pl.BlockSpec(memory_space=pltpu.VMEM)
hbm = pl.BlockSpec(memory_space=pltpu.HBM)


def shifted(block, axis, distance):
    devices = range(lax.axis_size(axis))
    route = [((i - distance) % len(devices), i) for i in devices]
    return lax.ppermute(block, axis, route)


def dot32(left, right, dims=(((1,), (0,)), ((), ()))):
    return lax.dot_general(left, right, dims, preferred_element_type=jnp.float32)


def call(body, outs, in_specs, args, scratch=(), flops=0, trans=0):
    moved = sum(a.size * a.dtype.itemsize for a in args)
    moved += sum(math.prod(o.shape) * o.dtype.itemsize for o in outs)
    return pl.pallas_call(
        body,
        out_shape=tuple(outs),
        in_specs=list(in_specs),
        out_specs=tuple(vmem for _ in outs),
        scratch_shapes=list(scratch),
        compiler_params=pltpu.CompilerParams(vmem_limit_bytes=24 * 2**20),
        cost_estimate=pl.CostEstimate(flops=flops, bytes_accessed=moved, transcendentals=trans),
    )(*args)


def spread(values, count, group):
    lane = lax.broadcasted_iota(jnp.int32, (1, count * group), 1) // group
    row = jnp.zeros((1, count * group), jnp.int32)
    for item in range(count):
        row = jnp.where(lane == item, values[item], row)
    return row


def keep_row(lengths, queries, tokens):
    slot = lax.broadcasted_iota(jnp.int32, (1, queries * tokens), 1) % tokens
    return (slot < spread(lengths, queries, tokens)).astype(jnp.float32)


def unit_rows(before):
    inverse = lax.rsqrt(jnp.sum(before * before, axis=1, keepdims=True) + norm_eps)
    return before * inverse, inverse


def back_rows(grad, before):
    unit, inverse = unit_rows(before)
    inner = jnp.sum(unit * grad, axis=1, keepdims=True)
    return ((grad - unit * inner) * inverse).astype(jnp.bfloat16)


def load_all(pairs, sems):
    copies = [pltpu.make_async_copy(a, b, sems.at[i]) for i, (a, b) in enumerate(pairs)]
    for copy in copies:
        copy.start()
    return copies


def query_embed_body(
    queries, query_lengths_in, passage_lengths_in, positives_in, query_hidden_in, passage_hidden_in,
    projection_in,
    before_out, sent_out, slots_out, wanted_out, query_hidden, passage_hidden, projection,
    query_lengths, passage_lengths, positives, sems,
):
    pairs = (
        (projection_in, projection), (query_hidden_in, query_hidden),
        (query_lengths_in, query_lengths), (positives_in, positives),
        (passage_lengths_in, passage_lengths), (passage_hidden_in, passage_hidden),
    )
    copies = load_all(pairs, sems)
    copies[0].wait()
    copies[1].wait()
    rows = query_hidden.shape[0]
    before = dot32(query_hidden[...], projection[...])
    before_out[...] = before
    sent_out[:rows, :] = unit_rows(before)[0].astype(jnp.bfloat16)
    copies[2].wait()
    keep = keep_row(query_lengths, queries, rows // queries)
    row = lax.broadcasted_iota(jnp.int32, (ROWS, LANES), 0)
    tail = jnp.zeros((ROWS, LANES), jnp.float32)
    for piece in range(rows // LANES):
        tail = jnp.where(row == piece, keep[:, piece * LANES : (piece + 1) * LANES], tail)
    sent_out[rows:, :] = tail.astype(jnp.bfloat16)
    copies[3].wait()
    wanted_out[...] = spread(positives, queries, rows // queries)
    copies[4].wait()
    c = lax.broadcasted_iota(jnp.int32, slots_out.shape, 0)
    valid = jnp.zeros(slots_out.shape, jnp.int32)
    for item in range(passage_lengths.shape[0]):
        valid = jnp.where(c == item, passage_lengths[item], valid)
    slots_out[...] = valid
    copies[5].wait()


def sent_keep(sent, rows):
    tail = sent[rows:, :].astype(jnp.float32)
    return jnp.concatenate([tail[i : i + 1, :] for i in range(rows // LANES)], axis=1)


def score_block(queries, passages, valid, embed, sent, powers, totals, scores, tops):
    rows = sent.shape[0] - ROWS
    tokens = embed.shape[0] // passages
    query = sent[:rows, :]
    slot = lax.broadcasted_iota(jnp.int32, (tokens, rows), 0)
    totals[...] = jnp.ones(totals.shape, jnp.float32)
    tops[...] = jnp.zeros(tops.shape, jnp.float32)
    for c in range(passages):
        part = slice(c * tokens, (c + 1) * tokens)
        sims = dot32(embed[part, :], query, NT)
        sims = jnp.where(slot < valid[c : c + 1, :], sims, -jnp.inf)
        top = jnp.max(sims, axis=0, keepdims=True)
        power = jnp.exp2((sims - top) * (inner_scale * LOG2E))
        powers[part, :] = power
        tops[c : c + 1, :] = top
        totals[c : c + 1, :] = jnp.sum(power, axis=0, keepdims=True)
    best = tops[...] + jnp.log(totals[...]) / inner_scale
    best = best * sent_keep(sent, rows)
    group = rows // queries
    same = lax.broadcasted_iota(jnp.int32, (rows, rows), 0) // group
    same = (same == lax.broadcasted_iota(jnp.int32, (rows, rows), 1) // group).astype(jnp.bfloat16)
    high = best.astype(jnp.bfloat16)
    rest = best - high.astype(jnp.float32)
    middle = rest.astype(jnp.bfloat16)
    low = (rest - middle.astype(jnp.float32)).astype(jnp.bfloat16)
    total = dot32(high, same) + dot32(middle, same) + dot32(low, same)
    c = lax.broadcasted_iota(jnp.int32, total.shape, 0)
    scores[...] = jnp.where(c < passages, outer_scale * total, -jnp.inf)


def own_score_body(
    queries, passages, valid, hidden, projection, sent,
    before_out, embed_out, powers, totals, scores, tops,
):
    before = dot32(hidden[...], projection[...])
    before_out[...] = before
    embed_out[...] = unit_rows(before)[0].astype(jnp.bfloat16)
    score_block(queries, passages, valid, embed_out, sent, powers, totals, scores, tops)


def log_sum(scores):
    top = jnp.max(scores, axis=0, keepdims=True)
    return top + jnp.log(jnp.sum(jnp.exp(scores - top), axis=0, keepdims=True))


def other_score_body(
    queries, passages, valid, embed, sent1, sent2, scores0,
    powers1, powers2, totals1, totals2, scores1, scores2, logs, tops,
):
    score_block(queries, passages, valid, embed, sent1, powers1, totals1, scores1, tops)
    score_block(queries, passages, valid, embed, sent2, powers2, totals2, scores2, tops)
    row = lax.broadcasted_iota(jnp.int32, logs.shape[1:], 0)
    mine = jnp.zeros(logs.shape[1:], jnp.float32)
    for part, scores in enumerate((scores0, scores1, scores2)):
        mine = jnp.where(row == part, log_sum(scores[...]), mine)
    for target in range(logs.shape[0]):
        logs[target] = mine


def all_logs(logs, block):
    count = logs.shape[0]
    parts = [logs[lax.rem(block + t, count)][t : t + 1, :] for t in range(3)]
    top = functools.reduce(jnp.maximum, parts)
    return top + jnp.log(sum(jnp.exp(part - top) for part in parts))


def fill_grad_sim(passages, coefficient, powers, out, column):
    tokens = powers.shape[0] // passages
    rows = powers.shape[1]
    for c in range(passages):
        part = slice(c * tokens, (c + 1) * tokens)
        out[part, column : column + rows] = (powers[part, :] * coefficient[c : c + 1, :]).astype(
            jnp.bfloat16
        )


def other_grad_body(
    passages, embed, powers1, powers2, totals1, totals2, sent1, sent2,
    scores1, scores2, logs, to_query1, to_query2, grad_sim,
):
    rows = powers1.shape[1]
    turned = embed[...].T
    count = logs.shape[0]
    me = lax.axis_index("batch")
    for distance, powers, totals, sent, own, out in (
        (2, powers2, totals2, sent2, scores2, to_query2),
        (1, powers1, totals1, sent1, scores1, to_query1),
    ):
        column = (distance - 1) * rows
        log_total = all_logs(logs, lax.rem(me + (count - distance), count))
        dscore = loss_scale * jnp.exp(own[...] - log_total)
        coefficient = outer_scale * dscore * sent_keep(sent, rows) / totals[...]
        fill_grad_sim(passages, coefficient, powers, grad_sim, column)
        out[...] = dot32(turned, grad_sim[:, column : column + rows]).astype(jnp.bfloat16)


def own_grad_body(
    passages, wanted, hidden, embed, before, powers, totals, sent0, sent1, sent2,
    own, logs, other_grad_sim,
    losses, to_query, pre_grad, partial, grad_sim,
):
    rows = powers.shape[1]
    scores = own[...]
    log_total = all_logs(logs, lax.axis_index("batch"))
    onehot = lax.broadcasted_iota(jnp.int32, scores.shape, 0) == wanted[...]
    losses[...] = log_total - jnp.sum(jnp.where(onehot, scores, 0.0), axis=0, keepdims=True)
    dscore = loss_scale * (jnp.exp(scores - log_total) - onehot.astype(jnp.float32))
    coefficient = outer_scale * dscore * sent_keep(sent0, rows) / totals[...]
    fill_grad_sim(passages, coefficient, powers, grad_sim, 0)
    to_query[...] = dot32(embed[...].T, grad_sim[...])
    grad = dot32(grad_sim[...], sent0[:rows, :])
    grad += dot32(other_grad_sim[:, :rows], sent1[:rows, :])
    grad += dot32(other_grad_sim[:, rows:], sent2[:rows, :])
    pre = back_rows(grad, before[...])
    pre_grad[...] = pre
    partial[...] = dot32(pre.T, hidden[...])


def query_grad_body(hidden, before, own, back1, back2, passage_partial, pre_grad, partial):
    total = own[...] + back1[...].astype(jnp.float32) + back2[...].astype(jnp.float32)
    pre = back_rows(total.T, before[...])
    pre_grad[...] = pre
    both = passage_partial[...] + dot32(pre.T, hidden[...])
    partial[...] = both.T.astype(jnp.bfloat16)


def sum_body(scale, copies, pieces, out):
    total = jnp.sum(pieces[...].astype(jnp.float32), axis=0) * scale
    total = total.astype(jnp.bfloat16)
    for copy in range(copies):
        out[copy] = total


def copies_body(pieces, out):
    for copy in range(out.shape[0]):
        out[copy] = pieces[...]


def sum_call(pieces, scale, copies):
    return call(
        functools.partial(sum_body, scale, copies),
        (jax.ShapeDtypeStruct((copies,) + pieces.shape[1:], jnp.bfloat16),),
        (vmem,),
        (pieces,),
    )[0]


def mean_over_devices(partial):
    outer, inner = lax.axis_size("batch"), lax.axis_size("mp")
    devices = outer * inner
    rows, columns = partial.shape
    share = -(-rows // (devices * 8)) * 8
    padded = jnp.pad(partial, ((0, share * devices - rows), (0, 0)))
    pieces = padded.reshape(inner, outer * share, columns)
    pieces = lax.all_to_all(pieces, "mp", 0, 0)
    pieces = sum_call(pieces, 1.0, 1).reshape(outer, share, columns)
    pieces = lax.all_to_all(pieces, "batch", 0, 0)
    whole = lax.all_to_all(sum_call(pieces, 1.0 / devices, outer), "batch", 0, 0)
    whole = whole.reshape(outer * share, columns)
    whole = call(
        copies_body,
        (jax.ShapeDtypeStruct((inner,) + whole.shape, jnp.bfloat16),),
        (vmem,),
        (whole,),
    )[0]
    whole = lax.all_to_all(whole, "mp", 0, 0)
    return whole.reshape(devices * share, columns)[:rows].astype(jnp.float32)


def per_device(query_hidden, passage_hidden, projection, query_lengths, passage_lengths, positives):
    queries = query_lengths.shape[0]
    passages = passage_lengths.shape[0]
    rows, width = query_hidden.shape
    slots = passage_hidden.shape[0]
    dim = projection.shape[1]
    f32, bf16 = jnp.float32, jnp.bfloat16
    of = jax.ShapeDtypeStruct
    pair = of((ROWS, rows), f32)
    pairs = pltpu.VMEM((ROWS, rows), f32)
    count = lax.axis_size("batch")

    taken = (
        query_lengths, passage_lengths, positives, query_hidden, passage_hidden, projection
    )
    taken = tuple(pltpu.with_memory_space_constraint(x, pltpu.HBM) for x in taken)
    query_before, sent0, valid, wanted, query_rows, passage_rows, weight = call(
        functools.partial(query_embed_body, queries),
        (
            of((rows, dim), f32), of((rows + ROWS, dim), bf16), of((ROWS, rows), jnp.int32),
            of((1, rows), jnp.int32), of((rows, width), bf16), of((slots, width), bf16),
            of((width, dim), bf16),
        ),
        (hbm,) * 6,
        taken,
        scratch=(
            pltpu.SMEM((queries,), jnp.int32),
            pltpu.SMEM((passages,), jnp.int32),
            pltpu.SMEM((queries,), jnp.int32),
            pltpu.SemaphoreType.DMA((6,)),
        ),
        flops=2 * rows * width * dim,
    )
    sent1 = shifted(sent0, "batch", 1)
    sent2 = shifted(sent0, "batch", 2)
    passage_before, embed, powers0, totals0, scores0 = call(
        functools.partial(own_score_body, queries, passages),
        (of((slots, dim), f32), of((slots, dim), bf16), of((slots, rows), f32), pair, pair),
        (vmem,) * 4,
        (valid, passage_rows, weight, sent0),
        scratch=(pairs,),
        flops=2 * slots * dim * (width + rows),
        trans=slots * rows,
    )
    powers1, powers2, totals1, totals2, scores1, scores2, logs = call(
        functools.partial(other_score_body, queries, passages),
        (of((slots, rows), f32),) * 2 + (pair,) * 4 + (of((count, 8, rows), f32),),
        (vmem,) * 5,
        (valid, embed, sent1, sent2, scores0),
        scratch=(pairs,),
        flops=4 * slots * dim * rows,
        trans=2 * slots * rows,
    )
    logs = lax.all_to_all(logs, "batch", 0, 0)
    to_query1, to_query2, grad_sim = call(
        functools.partial(other_grad_body, passages),
        (of((dim, rows), bf16),) * 2 + (of((slots, 2 * rows), bf16),),
        (vmem,) * 10,
        (embed, powers1, powers2, totals1, totals2, sent1, sent2, scores1, scores2, logs),
        flops=4 * slots * dim * rows,
    )
    back1 = shifted(to_query1, "batch", -1)
    back2 = shifted(to_query2, "batch", -2)
    losses, to_query0, passage_pre_grad, passage_partial = call(
        functools.partial(own_grad_body, passages),
        (of((1, rows), f32), of((dim, rows), f32), of((slots, dim), bf16), of((dim, width), f32)),
        (vmem,) * 12,
        (wanted, passage_rows, embed, passage_before, powers0, totals0, sent0, sent1, sent2,
         scores0, logs, grad_sim),
        scratch=(pltpu.VMEM((slots, rows), bf16),),
        flops=8 * slots * dim * rows + 2 * slots * width * dim,
    )
    query_pre_grad, partial = call(
        query_grad_body,
        (of((rows, dim), bf16), of((width, dim), bf16)),
        (vmem,) * 6,
        (query_rows, query_before, to_query0, back1, back2, passage_partial),
        flops=2 * rows * width * dim,
    )
    grad_projection = mean_over_devices(partial)
    grad_query_hidden = dot32(query_pre_grad, weight, NT).astype(bf16)
    grad_passage_hidden = dot32(passage_pre_grad, weight, NT).astype(bf16)
    losses = losses.reshape(queries, rows // queries)[:, 0]
    return (losses, grad_query_hidden, grad_passage_hidden, grad_projection)


def solution(mesh):
    in_specs = (
        P(("batch", "mp"), None),
        P(("batch", "mp"), None),
        P(),
        P(("batch", "mp")),
        P(("batch", "mp")),
        P(("batch", "mp")),
    )
    out_specs = (P(("batch", "mp")), P(("batch", "mp"), None), P(("batch", "mp"), None), P())
    return jax.shard_map(
        per_device, mesh=mesh, in_specs=in_specs, out_specs=out_specs, check_vma=False
    )
```

```python
import functools
import math

import jax
import jax.numpy as jnp
from jax import lax
from jax.experimental import pallas as pl
from jax.experimental.pallas import tpu as pltpu
from jax.sharding import PartitionSpec as P

inner_scale = 128.0
outer_scale = 8.0
loss_scale = 32.0
norm_eps = 1e-06

LANES = 128
ROWS = 16
LOG2E = 1.0 / math.log(2.0)
NT = (((1,), (1,)), ((), ()))

vmem = pl.BlockSpec(memory_space=pltpu.VMEM)
hbm = pl.BlockSpec(memory_space=pltpu.HBM)


def shifted(block, axis, distance):
    devices = range(lax.axis_size(axis))
    route = [((i - distance) % len(devices), i) for i in devices]
    return lax.ppermute(block, axis, route)


def dot32(left, right, dims=(((1,), (0,)), ((), ()))):
    return lax.dot_general(left, right, dims, preferred_element_type=jnp.float32)


def call(body, outs, in_specs, args, scratch=(), flops=0, trans=0):
    moved = sum(a.size * a.dtype.itemsize for a in args)
    moved += sum(math.prod(o.shape) * o.dtype.itemsize for o in outs)
    return pl.pallas_call(
        body,
        out_shape=tuple(outs),
        in_specs=list(in_specs),
        out_specs=tuple(vmem for _ in outs),
        scratch_shapes=list(scratch),
        compiler_params=pltpu.CompilerParams(vmem_limit_bytes=24 * 2**20),
        cost_estimate=pl.CostEstimate(flops=flops, bytes_accessed=moved, transcendentals=trans),
    )(*args)


def spread(values, count, group):
    lane = lax.broadcasted_iota(jnp.int32, (1, count * group), 1) // group
    row = jnp.zeros((1, count * group), jnp.int32)
    for item in range(count):
        row = jnp.where(lane == item, values[item], row)
    return row


def keep_row(lengths, queries, tokens):
    slot = lax.broadcasted_iota(jnp.int32, (1, queries * tokens), 1) % tokens
    return (slot < spread(lengths, queries, tokens)).astype(jnp.float32)


def unit_rows(before):
    inverse = lax.rsqrt(jnp.sum(before * before, axis=1, keepdims=True) + norm_eps)
    return before * inverse, inverse


def back_rows(grad, before):
    unit, inverse = unit_rows(before)
    inner = jnp.sum(unit * grad, axis=1, keepdims=True)
    return ((grad - unit * inner) * inverse).astype(jnp.bfloat16)


def load_all(pairs, sems):
    copies = [pltpu.make_async_copy(a, b, sems.at[i]) for i, (a, b) in enumerate(pairs)]
    for copy in copies:
        copy.start()
    return copies


def query_embed_body(
    queries, query_lengths_in, passage_lengths_in, positives_in, query_hidden_in, passage_hidden_in,
    projection_in,
    before_out, sent_out, slots_out, wanted_out, query_hidden, passage_hidden, projection,
    query_lengths, passage_lengths, positives, sems,
):
    pairs = (
        (projection_in, projection), (query_hidden_in, query_hidden),
        (query_lengths_in, query_lengths), (positives_in, positives),
        (passage_lengths_in, passage_lengths), (passage_hidden_in, passage_hidden),
    )
    copies = load_all(pairs, sems)
    copies[0].wait()
    copies[1].wait()
    rows = query_hidden.shape[0]
    before = dot32(query_hidden[...], projection[...])
    before_out[...] = before
    sent_out[:rows, :] = unit_rows(before)[0].astype(jnp.bfloat16)
    copies[2].wait()
    keep = keep_row(query_lengths, queries, rows // queries)
    row = lax.broadcasted_iota(jnp.int32, (ROWS, LANES), 0)
    tail = jnp.zeros((ROWS, LANES), jnp.float32)
    for piece in range(rows // LANES):
        tail = jnp.where(row == piece, keep[:, piece * LANES : (piece + 1) * LANES], tail)
    sent_out[rows:, :] = tail.astype(jnp.bfloat16)
    copies[3].wait()
    wanted_out[...] = spread(positives, queries, rows // queries)
    copies[4].wait()
    c = lax.broadcasted_iota(jnp.int32, slots_out.shape, 0)
    valid = jnp.zeros(slots_out.shape, jnp.int32)
    for item in range(passage_lengths.shape[0]):
        valid = jnp.where(c == item, passage_lengths[item], valid)
    slots_out[...] = valid
    copies[5].wait()


def sent_keep(sent, rows):
    tail = sent[rows:, :].astype(jnp.float32)
    return jnp.concatenate([tail[i : i + 1, :] for i in range(rows // LANES)], axis=1)


def split(values):
    high = values.astype(jnp.bfloat16)
    rest = values - high.astype(jnp.float32)
    middle = rest.astype(jnp.bfloat16)
    return high, middle, (rest - middle.astype(jnp.float32)).astype(jnp.bfloat16)


def score_block(queries, passages, valid, embed, sent, powers, totals, scores, tops):
    rows = sent.shape[0] - ROWS
    tokens = embed.shape[0] // passages
    query = sent[:rows, :]
    slot = lax.broadcasted_iota(jnp.int32, (tokens, rows), 0)
    totals[...] = jnp.ones(totals.shape, jnp.float32)
    tops[...] = jnp.zeros(tops.shape, jnp.float32)
    for c in range(passages):
        part = slice(c * tokens, (c + 1) * tokens)
        sims = dot32(embed[part, :], query, NT)
        sims = jnp.where(slot < valid[c : c + 1, :], sims, -jnp.inf)
        top = jnp.max(sims, axis=0, keepdims=True)
        power = jnp.exp2((sims - top) * (inner_scale * LOG2E))
        powers[part, :] = power
        tops[c : c + 1, :] = top
        totals[c : c + 1, :] = jnp.sum(power, axis=0, keepdims=True)
    best = tops[...] + jnp.log(totals[...]) / inner_scale
    best = best * sent_keep(sent, rows)
    group = rows // queries
    same = lax.broadcasted_iota(jnp.int32, (rows, rows), 0) // group
    same = (same == lax.broadcasted_iota(jnp.int32, (rows, rows), 1) // group).astype(jnp.bfloat16)
    total = sum(dot32(part, same) for part in split(best))
    c = lax.broadcasted_iota(jnp.int32, total.shape, 0)
    scores[...] = jnp.where(c < passages, outer_scale * total, -jnp.inf)


def own_score_body(
    queries, passages, valid, hidden, projection, sent,
    before_out, embed_out, powers, totals, scores, tops,
):
    before = dot32(hidden[...], projection[...])
    before_out[...] = before
    embed_out[...] = unit_rows(before)[0].astype(jnp.bfloat16)
    score_block(queries, passages, valid, embed_out, sent, powers, totals, scores, tops)


def log_sum(scores):
    top = jnp.max(scores, axis=0, keepdims=True)
    return top + jnp.log(jnp.sum(jnp.exp(scores - top), axis=0, keepdims=True))


def log_add(parts):
    top = functools.reduce(jnp.maximum, parts)
    return top + jnp.log(sum(jnp.exp(part - top) for part in parts))


def stack_rows(shape, rows):
    index = lax.broadcasted_iota(jnp.int32, shape, 0)
    tile = jnp.zeros(shape, jnp.float32)
    for place, row in enumerate(rows):
        tile = jnp.where(index == place, row, tile)
    return tile


def fill_grad_sim(passages, coefficient, powers, out, column):
    tokens = powers.shape[0] // passages
    rows = powers.shape[1]
    for c in range(passages):
        part = slice(c * tokens, (c + 1) * tokens)
        out[part, column : column + rows] = (powers[part, :] * coefficient[c : c + 1, :]).astype(
            jnp.bfloat16
        )


def other_score_body(
    queries, passages, valid, embed, sent1, sent2, scores0,
    powers1, powers2, totals1, totals2, scores1, scores2, logs, back1, back2, tops, grad_sim,
):
    rows = powers1.shape[1]
    dim = embed.shape[1]
    score_block(queries, passages, valid, embed, sent2, powers2, totals2, scores2, tops)
    score_block(queries, passages, valid, embed, sent1, powers1, totals1, scores1, tops)
    log0, log1, log2 = [log_sum(scores[...]) for scores in (scores0, scores1, scores2)]
    logs[...] = stack_rows(logs.shape, (log0, log1, log2))
    turned = embed[...].T
    for log, sent, powers, totals, scores, back, tail in (
        (log2, sent2, powers2, totals2, scores2, back2, split(log2)),
        (log1, sent1, powers1, totals1, scores1, back1, split(log1) + split(log2)),
    ):
        dscore = loss_scale * jnp.exp(scores[...] - log)
        coefficient = outer_scale * dscore * sent_keep(sent, rows) / totals[...]
        fill_grad_sim(passages, coefficient, powers, grad_sim, 0)
        back[:dim, :] = dot32(turned, grad_sim[...]).astype(jnp.bfloat16)
        tail = stack_rows((ROWS, rows), [part.astype(jnp.float32) for part in tail])
        back[dim:, :] = tail.astype(jnp.bfloat16)


def joined(back, dim, place):
    tail = back[dim:, :].astype(jnp.float32)
    high, middle, low = [tail[i : i + 1, :] for i in range(place, place + 3)]
    return high + (middle + low)


def grad_body(
    queries, passages, wanted, query_hidden, passage_hidden, embed, query_before, passage_before,
    powers0, powers1, powers2, totals0, totals1, totals2, scores0, scores1, scores2,
    sent0, sent1, sent2, logs, logs1, logs2, back1, back2,
    losses, query_pre_grad, passage_pre_grad, partial, grad_sim,
):
    rows = powers0.shape[1]
    dim = embed.shape[1]
    second, third = joined(back1, dim, 0), joined(back2, dim, 0)
    total0 = log_add((logs[0:1, :], second, third))
    total1 = log_add((logs1[0:1, :], logs[1:2, :], joined(back1, dim, 3)))
    total2 = log_add((logs2[0:1, :], logs1[1:2, :], logs[2:3, :]))
    scores = scores0[...]
    onehot = lax.broadcasted_iota(jnp.int32, scores.shape, 0) == wanted[...]
    loss = total0 - jnp.sum(jnp.where(onehot, scores, 0.0), axis=0, keepdims=True)
    pick = lax.broadcasted_iota(jnp.int32, (rows, LANES), 1) * (rows // queries)
    pick = (pick == lax.broadcasted_iota(jnp.int32, (rows, LANES), 0)).astype(jnp.bfloat16)
    losses[...] = sum(dot32(part, pick) for part in split(loss))[:, :queries]

    for block, (total, sent, powers, totals, scores) in enumerate((
        (total0, sent0, powers0, totals0, scores0),
        (total1, sent1, powers1, totals1, scores1),
        (total2, sent2, powers2, totals2, scores2),
    )):
        dscore = jnp.exp(scores[...] - total)
        if block == 0:
            dscore = dscore - onehot.astype(jnp.float32)
        coefficient = (outer_scale * loss_scale) * dscore * sent_keep(sent, rows) / totals[...]
        fill_grad_sim(passages, coefficient, powers, grad_sim, block * rows)

    to_query = dot32(embed[...].T, grad_sim[:, :rows])
    to_query += back1[:dim, :].astype(jnp.float32) * jnp.exp(second - total0)
    to_query += back2[:dim, :].astype(jnp.float32) * jnp.exp(third - total0)
    pre = back_rows(to_query.T, query_before[...])
    query_pre_grad[...] = pre
    both = dot32(pre.T, query_hidden[...])
    grad = dot32(grad_sim[:, :rows], sent0[:rows, :])
    grad += dot32(grad_sim[:, rows : 2 * rows], sent1[:rows, :])
    grad += dot32(grad_sim[:, 2 * rows :], sent2[:rows, :])
    pre = back_rows(grad, passage_before[...])
    passage_pre_grad[...] = pre
    both += dot32(pre.T, passage_hidden[...])
    partial[...] = both.T.astype(jnp.bfloat16)


def sum_body(scale, copies, pieces, out):
    total = jnp.sum(pieces[...].astype(jnp.float32), axis=0) * scale
    total = total.astype(jnp.bfloat16)
    for copy in range(copies):
        out[copy] = total


def mean_over_devices(partial):
    axes = ("batch", "mp")
    devices = lax.axis_size("batch") * lax.axis_size("mp")
    rows, columns = partial.shape
    share = -(-rows // (devices * 8)) * 8
    padded = jnp.pad(partial, ((0, share * devices - rows), (0, 0)))
    pieces = lax.all_to_all(padded.reshape(devices, share, columns), axes, 0, 0)
    means = call(
        functools.partial(sum_body, 1.0 / devices, devices),
        (jax.ShapeDtypeStruct(pieces.shape, jnp.bfloat16),),
        (vmem,),
        (pieces,),
    )[0]
    whole = lax.all_to_all(means, axes, 0, 0)
    return whole.reshape(devices * share, columns)[:rows].astype(jnp.float32)


def per_device(query_hidden, passage_hidden, projection, query_lengths, passage_lengths, positives):
    queries = query_lengths.shape[0]
    passages = passage_lengths.shape[0]
    rows, width = query_hidden.shape
    slots = passage_hidden.shape[0]
    dim = projection.shape[1]
    f32, bf16 = jnp.float32, jnp.bfloat16
    of = jax.ShapeDtypeStruct
    pair = of((ROWS, rows), f32)
    pairs = pltpu.VMEM((ROWS, rows), f32)

    taken = (
        query_lengths, passage_lengths, positives, query_hidden, passage_hidden, projection
    )
    taken = tuple(pltpu.with_memory_space_constraint(x, pltpu.HBM) for x in taken)
    query_before, sent0, valid, wanted, query_rows, passage_rows, weight = call(
        functools.partial(query_embed_body, queries),
        (
            of((rows, dim), f32), of((rows + ROWS, dim), bf16), of((ROWS, rows), jnp.int32),
            of((1, rows), jnp.int32), of((rows, width), bf16), of((slots, width), bf16),
            of((width, dim), bf16),
        ),
        (hbm,) * 6,
        taken,
        scratch=(
            pltpu.SMEM((queries,), jnp.int32),
            pltpu.SMEM((passages,), jnp.int32),
            pltpu.SMEM((queries,), jnp.int32),
            pltpu.SemaphoreType.DMA((6,)),
        ),
        flops=2 * rows * width * dim,
    )
    sent1 = shifted(sent0, "batch", 1)
    sent2 = shifted(sent0, "batch", 2)
    passage_before, embed, powers0, totals0, scores0 = call(
        functools.partial(own_score_body, queries, passages),
        (of((slots, dim), f32), of((slots, dim), bf16), of((slots, rows), f32), pair, pair),
        (vmem,) * 4,
        (valid, passage_rows, weight, sent0),
        scratch=(pairs,),
        flops=2 * slots * dim * (width + rows),
        trans=slots * rows,
    )
    powers1, powers2, totals1, totals2, scores1, scores2, logs, back1, back2 = call(
        functools.partial(other_score_body, queries, passages),
        (of((slots, rows), f32),) * 2 + (pair,) * 4
        + (of((8, rows), f32),) + (of((dim + ROWS, rows), bf16),) * 2,
        (vmem,) * 5,
        (valid, embed, sent1, sent2, scores0),
        scratch=(pairs, pltpu.VMEM((slots, rows), bf16)),
        flops=8 * slots * dim * rows,
        trans=2 * slots * rows,
    )
    back2 = shifted(back2, "batch", -2)
    back1 = shifted(back1, "batch", -1)
    logs1 = shifted(logs, "batch", 1)
    logs2 = shifted(logs, "batch", 2)
    losses, query_pre_grad, passage_pre_grad, partial = call(
        functools.partial(grad_body, queries, passages),
        (
            of((1, queries), f32), of((rows, dim), bf16), of((slots, dim), bf16),
            of((width, dim), bf16),
        ),
        (vmem,) * 23,
        (wanted, query_rows, passage_rows, embed, query_before, passage_before,
         powers0, powers1, powers2, totals0, totals1, totals2, scores0, scores1, scores2,
         sent0, sent1, sent2, logs, logs1, logs2, back1, back2),
        scratch=(pltpu.VMEM((slots, 3 * rows), bf16),),
        flops=8 * slots * dim * rows + 2 * (slots + rows) * width * dim,
    )
    grad_projection = mean_over_devices(partial)
    grad_query_hidden = dot32(query_pre_grad, weight, NT).astype(bf16)
    grad_passage_hidden = dot32(passage_pre_grad, weight, NT).astype(bf16)
    losses = losses.reshape(queries)
    return (losses, grad_query_hidden, grad_passage_hidden, grad_projection)


def solution(mesh):
    in_specs = (
        P(("batch", "mp"), None),
        P(("batch", "mp"), None),
        P(),
        P(("batch", "mp")),
        P(("batch", "mp")),
        P(("batch", "mp")),
    )
    out_specs = (P(("batch", "mp")), P(("batch", "mp"), None), P(("batch", "mp"), None), P())
    return jax.shard_map(
        per_device, mesh=mesh, in_specs=in_specs, out_specs=out_specs, check_vma=False
    )
```

```python
import functools
import math

import jax
import jax.numpy as jnp
from jax import lax
from jax.experimental import pallas as pl
from jax.experimental.pallas import tpu as pltpu
from jax.sharding import PartitionSpec as P

inner_scale = 128.0
outer_scale = 8.0
loss_scale = 32.0
norm_eps = 1e-06

LANES = 128
ROWS = 16
LOG2E = 1.0 / math.log(2.0)
NT = (((1,), (1,)), ((), ()))

vmem = pl.BlockSpec(memory_space=pltpu.VMEM)
hbm = pl.BlockSpec(memory_space=pltpu.HBM)


def shifted(block, axis, distance):
    devices = range(lax.axis_size(axis))
    route = [((i - distance) % len(devices), i) for i in devices]
    return lax.ppermute(block, axis, route)


def dot32(left, right, dims=(((1,), (0,)), ((), ()))):
    return lax.dot_general(left, right, dims, preferred_element_type=jnp.float32)


def call(body, outs, in_specs, args, scratch=(), flops=0, trans=0):
    moved = sum(a.size * a.dtype.itemsize for a in args)
    moved += sum(math.prod(o.shape) * o.dtype.itemsize for o in outs)
    return pl.pallas_call(
        body,
        out_shape=tuple(outs),
        in_specs=list(in_specs),
        out_specs=tuple(vmem for _ in outs),
        scratch_shapes=list(scratch),
        compiler_params=pltpu.CompilerParams(vmem_limit_bytes=24 * 2**20),
        cost_estimate=pl.CostEstimate(flops=flops, bytes_accessed=moved, transcendentals=trans),
    )(*args)


def spread(values, count, group):
    lane = lax.broadcasted_iota(jnp.int32, (1, count * group), 1) // group
    row = jnp.zeros((1, count * group), jnp.int32)
    for item in range(count):
        row = jnp.where(lane == item, values[item], row)
    return row


def keep_row(lengths, queries, tokens):
    slot = lax.broadcasted_iota(jnp.int32, (1, queries * tokens), 1) % tokens
    return (slot < spread(lengths, queries, tokens)).astype(jnp.float32)


def unit_rows(before):
    inverse = lax.rsqrt(jnp.sum(before * before, axis=1, keepdims=True) + norm_eps)
    return before * inverse, inverse


def back_rows(grad, before):
    unit, inverse = unit_rows(before)
    inner = jnp.sum(unit * grad, axis=1, keepdims=True)
    return ((grad - unit * inner) * inverse).astype(jnp.bfloat16)


def load_all(pairs, sems):
    copies = [pltpu.make_async_copy(a, b, sems.at[i]) for i, (a, b) in enumerate(pairs)]
    for copy in copies:
        copy.start()
    return copies


def query_embed_body(
    queries, query_lengths_in, passage_lengths_in, positives_in, query_hidden_in, passage_hidden_in,
    projection_in,
    before_out, sent_out, slots_out, wanted_out, query_hidden, passage_hidden, projection,
    query_lengths, passage_lengths, positives, sems,
):
    pairs = (
        (projection_in, projection), (query_hidden_in, query_hidden),
        (query_lengths_in, query_lengths), (positives_in, positives),
        (passage_lengths_in, passage_lengths), (passage_hidden_in, passage_hidden),
    )
    copies = load_all(pairs, sems)
    copies[0].wait()
    copies[1].wait()
    rows = query_hidden.shape[0]
    before = dot32(query_hidden[...], projection[...])
    before_out[...] = before
    sent_out[:rows, :] = unit_rows(before)[0].astype(jnp.bfloat16)
    copies[2].wait()
    keep = keep_row(query_lengths, queries, rows // queries)
    row = lax.broadcasted_iota(jnp.int32, (ROWS, LANES), 0)
    tail = jnp.zeros((ROWS, LANES), jnp.float32)
    for piece in range(rows // LANES):
        tail = jnp.where(row == piece, keep[:, piece * LANES : (piece + 1) * LANES], tail)
    sent_out[rows:, :] = tail.astype(jnp.bfloat16)
    copies[3].wait()
    wanted_out[...] = spread(positives, queries, rows // queries)
    copies[4].wait()
    c = lax.broadcasted_iota(jnp.int32, slots_out.shape, 0)
    valid = jnp.zeros(slots_out.shape, jnp.int32)
    for item in range(passage_lengths.shape[0]):
        valid = jnp.where(c == item, passage_lengths[item], valid)
    slots_out[...] = valid
    copies[5].wait()


def sent_keep(sent, rows):
    tail = sent[rows:, :].astype(jnp.float32)
    return jnp.concatenate([tail[i : i + 1, :] for i in range(rows // LANES)], axis=1)


def split(values):
    high = values.astype(jnp.bfloat16)
    rest = values - high.astype(jnp.float32)
    middle = rest.astype(jnp.bfloat16)
    return high, middle, (rest - middle.astype(jnp.float32)).astype(jnp.bfloat16)


def score_block(queries, passages, valid, embed, sent, powers, totals, scores, tops):
    rows = sent.shape[0] - ROWS
    tokens = embed.shape[0] // passages
    query = sent[:rows, :]
    slot = lax.broadcasted_iota(jnp.int32, (tokens, rows), 0)
    totals[...] = jnp.ones(totals.shape, jnp.float32)
    tops[...] = jnp.zeros(tops.shape, jnp.float32)
    for c in range(passages):
        part = slice(c * tokens, (c + 1) * tokens)
        sims = dot32(embed[part, :], query, NT)
        sims = jnp.where(slot < valid[c : c + 1, :], sims, -jnp.inf)
        top = jnp.max(sims, axis=0, keepdims=True)
        power = jnp.exp2((sims - top) * (inner_scale * LOG2E))
        powers[part, :] = power
        tops[c : c + 1, :] = top
        totals[c : c + 1, :] = jnp.sum(power, axis=0, keepdims=True)
    best = tops[...] + jnp.log(totals[...]) / inner_scale
    best = best * sent_keep(sent, rows)
    group = rows // queries
    same = lax.broadcasted_iota(jnp.int32, (rows, rows), 0) // group
    same = (same == lax.broadcasted_iota(jnp.int32, (rows, rows), 1) // group).astype(jnp.bfloat16)
    total = sum(dot32(part, same) for part in split(best))
    c = lax.broadcasted_iota(jnp.int32, total.shape, 0)
    scores[...] = jnp.where(c < passages, outer_scale * total, -jnp.inf)


def own_score_body(
    queries, passages, valid, hidden, projection, sent,
    before_out, embed_out, powers, totals, scores, tops,
):
    before = dot32(hidden[...], projection[...])
    before_out[...] = before
    embed_out[...] = unit_rows(before)[0].astype(jnp.bfloat16)
    score_block(queries, passages, valid, embed_out, sent, powers, totals, scores, tops)


def log_sum(scores):
    top = jnp.max(scores, axis=0, keepdims=True)
    return top + jnp.log(jnp.sum(jnp.exp(scores - top), axis=0, keepdims=True))


def log_add(parts):
    top = functools.reduce(jnp.maximum, parts)
    return top + jnp.log(sum(jnp.exp(part - top) for part in parts))


def stack_rows(shape, rows):
    index = lax.broadcasted_iota(jnp.int32, shape, 0)
    tile = jnp.zeros(shape, jnp.float32)
    for place, row in enumerate(rows):
        tile = jnp.where(index == place, row, tile)
    return tile


def fill_grad_sim(passages, coefficient, powers, out, column):
    tokens = powers.shape[0] // passages
    rows = powers.shape[1]
    for c in range(passages):
        part = slice(c * tokens, (c + 1) * tokens)
        out[part, column : column + rows] = (powers[part, :] * coefficient[c : c + 1, :]).astype(
            jnp.bfloat16
        )


def other_score_body(
    queries, passages, valid, embed, sent1, sent2, scores0,
    powers1, powers2, totals1, totals2, scores1, scores2, logs, back1, back2, tops, grad_sim,
):
    rows = powers1.shape[1]
    dim = embed.shape[1]
    score_block(queries, passages, valid, embed, sent2, powers2, totals2, scores2, tops)
    score_block(queries, passages, valid, embed, sent1, powers1, totals1, scores1, tops)
    log0, log1, log2 = [log_sum(scores[...]) for scores in (scores0, scores1, scores2)]
    logs[...] = stack_rows(logs.shape, (log0, log1, log2))
    turned = embed[...].T
    for log, sent, powers, totals, scores, back, tail in (
        (log2, sent2, powers2, totals2, scores2, back2, split(log2)),
        (log1, sent1, powers1, totals1, scores1, back1, split(log1) + split(log2)),
    ):
        dscore = loss_scale * jnp.exp(scores[...] - log)
        coefficient = outer_scale * dscore * sent_keep(sent, rows) / totals[...]
        fill_grad_sim(passages, coefficient, powers, grad_sim, 0)
        back[:dim, :] = dot32(turned, grad_sim[...]).astype(jnp.bfloat16)
        tail = stack_rows((ROWS, rows), [part.astype(jnp.float32) for part in tail])
        back[dim:, :] = tail.astype(jnp.bfloat16)


def joined(back, dim, place):
    tail = back[dim:, :].astype(jnp.float32)
    high, middle, low = [tail[i : i + 1, :] for i in range(place, place + 3)]
    return high + (middle + low)


def half_at(bit, size, other):
    side = lax.rem(lax.axis_index("mp") // bit, 2)
    side = 1 - side if other else side
    return pl.ds(pl.multiple_of(side * size, size), size)


def share_halves(bit, whole, kept, sent):
    size = kept.shape[0]
    kept[...] = whole[half_at(bit, size, False), :]
    sent[...] = whole[half_at(bit, size, True), :].astype(sent.dtype)


def halve_body(bit, kept, taken, next_kept, next_sent, total):
    total[...] = kept[...] + taken[...].astype(jnp.float32)
    share_halves(bit, total, next_kept, next_sent)


def last_half_body(scale, kept, taken, out):
    out[...] = ((kept[...] + taken[...].astype(jnp.float32)) * scale).astype(out.dtype)


def join_body(bit, mine, taken, out):
    size = mine.shape[0]
    out[half_at(bit, size, False), :] = mine[...].astype(out.dtype)
    out[half_at(bit, size, True), :] = taken[...].astype(out.dtype)


def swapped(block, bit):
    return lax.ppermute(block, "mp", [(i, i ^ bit) for i in range(lax.axis_size("mp"))])


def mean_over_devices(kept, sent):
    of = jax.ShapeDtypeStruct
    inner = lax.axis_size("mp")
    scale = 1.0 / (lax.axis_size("batch") * inner)
    bit = 1
    while True:
        taken = swapped(sent, bit)
        size, columns = kept.shape
        if 2 * bit == inner:
            break
        bit *= 2
        kept, sent = call(
            functools.partial(halve_body, bit),
            (of((size // 2, columns), jnp.float32), of((size // 2, columns), jnp.bfloat16)),
            (vmem,) * 2,
            (kept, taken),
            scratch=(pltpu.VMEM((size, columns), jnp.float32),),
        )
    share = call(
        functools.partial(last_half_body, scale),
        (of((size, columns), jnp.bfloat16),),
        (vmem,) * 2,
        (kept, taken),
    )[0]
    share = lax.psum(share, "batch")
    while bit:
        dtype = jnp.float32 if bit == 1 else jnp.bfloat16
        share = call(
            functools.partial(join_body, bit),
            (of((2 * share.shape[0], columns), dtype),),
            (vmem,) * 2,
            (share, swapped(share, bit)),
        )[0]
        bit //= 2
    return share


def grad_body(
    queries, passages, wanted, query_hidden, passage_hidden, embed, query_before, passage_before,
    powers0, powers1, powers2, totals0, totals1, totals2, scores0, scores1, scores2,
    sent0, sent1, sent2, logs, logs1, logs2, back1, back2,
    losses, query_pre_grad, passage_pre_grad, kept, sent, grad_sim, partial,
):
    rows = powers0.shape[1]
    dim = embed.shape[1]
    second, third = joined(back1, dim, 0), joined(back2, dim, 0)
    total0 = log_add((logs[0:1, :], second, third))
    total1 = log_add((logs1[0:1, :], logs[1:2, :], joined(back1, dim, 3)))
    total2 = log_add((logs2[0:1, :], logs1[1:2, :], logs[2:3, :]))
    scores = scores0[...]
    onehot = lax.broadcasted_iota(jnp.int32, scores.shape, 0) == wanted[...]
    loss = total0 - jnp.sum(jnp.where(onehot, scores, 0.0), axis=0, keepdims=True)
    pick = lax.broadcasted_iota(jnp.int32, (rows, LANES), 1) * (rows // queries)
    pick = (pick == lax.broadcasted_iota(jnp.int32, (rows, LANES), 0)).astype(jnp.bfloat16)
    losses[...] = sum(dot32(part, pick) for part in split(loss))[:, :queries]

    for block, (total, query, powers, totals, scores) in enumerate((
        (total0, sent0, powers0, totals0, scores0),
        (total1, sent1, powers1, totals1, scores1),
        (total2, sent2, powers2, totals2, scores2),
    )):
        dscore = jnp.exp(scores[...] - total)
        if block == 0:
            dscore = dscore - onehot.astype(jnp.float32)
        coefficient = (outer_scale * loss_scale) * dscore * sent_keep(query, rows) / totals[...]
        fill_grad_sim(passages, coefficient, powers, grad_sim, block * rows)

    to_query = dot32(embed[...].T, grad_sim[:, :rows])
    to_query += back1[:dim, :].astype(jnp.float32) * jnp.exp(second - total0)
    to_query += back2[:dim, :].astype(jnp.float32) * jnp.exp(third - total0)
    pre = back_rows(to_query.T, query_before[...])
    query_pre_grad[...] = pre
    both = dot32(pre.T, query_hidden[...])
    grad = dot32(grad_sim[:, :rows], sent0[:rows, :])
    grad += dot32(grad_sim[:, rows : 2 * rows], sent1[:rows, :])
    grad += dot32(grad_sim[:, 2 * rows :], sent2[:rows, :])
    pre = back_rows(grad, passage_before[...])
    passage_pre_grad[...] = pre
    both += dot32(pre.T, passage_hidden[...])
    partial[...] = both.T
    share_halves(1, partial, kept, sent)


def per_device(query_hidden, passage_hidden, projection, query_lengths, passage_lengths, positives):
    queries = query_lengths.shape[0]
    passages = passage_lengths.shape[0]
    rows, width = query_hidden.shape
    slots = passage_hidden.shape[0]
    dim = projection.shape[1]
    f32, bf16 = jnp.float32, jnp.bfloat16
    of = jax.ShapeDtypeStruct
    pair = of((ROWS, rows), f32)
    pairs = pltpu.VMEM((ROWS, rows), f32)

    taken = (
        query_lengths, passage_lengths, positives, query_hidden, passage_hidden, projection
    )
    taken = tuple(pltpu.with_memory_space_constraint(x, pltpu.HBM) for x in taken)
    query_before, sent0, valid, wanted, query_rows, passage_rows, weight = call(
        functools.partial(query_embed_body, queries),
        (
            of((rows, dim), f32), of((rows + ROWS, dim), bf16), of((ROWS, rows), jnp.int32),
            of((1, rows), jnp.int32), of((rows, width), bf16), of((slots, width), bf16),
            of((width, dim), bf16),
        ),
        (hbm,) * 6,
        taken,
        scratch=(
            pltpu.SMEM((queries,), jnp.int32),
            pltpu.SMEM((passages,), jnp.int32),
            pltpu.SMEM((queries,), jnp.int32),
            pltpu.SemaphoreType.DMA((6,)),
        ),
        flops=2 * rows * width * dim,
    )
    sent1 = shifted(sent0, "batch", 1)
    sent2 = shifted(sent0, "batch", 2)
    passage_before, embed, powers0, totals0, scores0 = call(
        functools.partial(own_score_body, queries, passages),
        (of((slots, dim), f32), of((slots, dim), bf16), of((slots, rows), f32), pair, pair),
        (vmem,) * 4,
        (valid, passage_rows, weight, sent0),
        scratch=(pairs,),
        flops=2 * slots * dim * (width + rows),
        trans=slots * rows,
    )
    powers1, powers2, totals1, totals2, scores1, scores2, logs, back1, back2 = call(
        functools.partial(other_score_body, queries, passages),
        (of((slots, rows), f32),) * 2 + (pair,) * 4
        + (of((8, rows), f32),) + (of((dim + ROWS, rows), bf16),) * 2,
        (vmem,) * 5,
        (valid, embed, sent1, sent2, scores0),
        scratch=(pairs, pltpu.VMEM((slots, rows), bf16)),
        flops=8 * slots * dim * rows,
        trans=2 * slots * rows,
    )
    back2 = shifted(back2, "batch", -2)
    back1 = shifted(back1, "batch", -1)
    logs1 = shifted(logs, "batch", 1)
    logs2 = shifted(logs, "batch", 2)
    losses, query_pre_grad, passage_pre_grad, kept, sent = call(
        functools.partial(grad_body, queries, passages),
        (
            of((1, queries), f32), of((rows, dim), bf16), of((slots, dim), bf16),
            of((width // 2, dim), f32), of((width // 2, dim), bf16),
        ),
        (vmem,) * 23,
        (wanted, query_rows, passage_rows, embed, query_before, passage_before,
         powers0, powers1, powers2, totals0, totals1, totals2, scores0, scores1, scores2,
         sent0, sent1, sent2, logs, logs1, logs2, back1, back2),
        scratch=(pltpu.VMEM((slots, 3 * rows), bf16), pltpu.VMEM((width, dim), f32)),
        flops=8 * slots * dim * rows + 2 * (slots + rows) * width * dim,
    )
    grad_projection = mean_over_devices(kept, sent)
    grad_query_hidden = dot32(query_pre_grad, weight, NT).astype(bf16)
    grad_passage_hidden = dot32(passage_pre_grad, weight, NT).astype(bf16)
    losses = losses.reshape(queries)
    return (losses, grad_query_hidden, grad_passage_hidden, grad_projection)


def solution(mesh):
    in_specs = (
        P(("batch", "mp"), None),
        P(("batch", "mp"), None),
        P(),
        P(("batch", "mp")),
        P(("batch", "mp")),
        P(("batch", "mp")),
    )
    out_specs = (P(("batch", "mp")), P(("batch", "mp"), None), P(("batch", "mp"), None), P())
    return jax.shard_map(
        per_device, mesh=mesh, in_specs=in_specs, out_specs=out_specs, check_vma=False
    )
```

```python
import functools
import math

import jax
import jax.numpy as jnp
from jax import lax
from jax.experimental import pallas as pl
from jax.experimental.pallas import tpu as pltpu
from jax.sharding import PartitionSpec as P

inner_scale = 128.0
outer_scale = 8.0
loss_scale = 32.0
norm_eps = 1e-06

LANES = 128
ROWS = 16
LOG2E = 1.0 / math.log(2.0)
NT = (((1,), (1,)), ((), ()))

vmem = pl.BlockSpec(memory_space=pltpu.VMEM)
hbm = pl.BlockSpec(memory_space=pltpu.HBM)


def shifted(block, axis, distance):
    devices = range(lax.axis_size(axis))
    route = [((i - distance) % len(devices), i) for i in devices]
    return lax.ppermute(block, axis, route)


def dot32(left, right, dims=(((1,), (0,)), ((), ()))):
    return lax.dot_general(left, right, dims, preferred_element_type=jnp.float32)


def call(body, outs, in_specs, args, scratch=(), flops=0, trans=0):
    moved = sum(a.size * a.dtype.itemsize for a in args)
    moved += sum(math.prod(o.shape) * jnp.dtype(o.dtype).itemsize for o in outs)
    return pl.pallas_call(
        body,
        out_shape=tuple(outs),
        in_specs=list(in_specs),
        out_specs=tuple(vmem for _ in outs),
        scratch_shapes=list(scratch),
        compiler_params=pltpu.CompilerParams(vmem_limit_bytes=24 * 2**20),
        cost_estimate=pl.CostEstimate(flops=flops, bytes_accessed=moved, transcendentals=trans),
    )(*args)


def spread(values, count, group):
    lane = lax.broadcasted_iota(jnp.int32, (1, count * group), 1) // group
    row = jnp.zeros((1, count * group), jnp.int32)
    for item in range(count):
        row = jnp.where(lane == item, values[item], row)
    return row


def keep_row(lengths, queries, tokens):
    slot = lax.broadcasted_iota(jnp.int32, (1, queries * tokens), 1) % tokens
    return (slot < spread(lengths, queries, tokens)).astype(jnp.float32)


def unit_rows(before):
    inverse = lax.rsqrt(jnp.sum(before * before, axis=1, keepdims=True) + norm_eps)
    return before * inverse, inverse


def back_rows(grad, before):
    unit, inverse = unit_rows(before)
    inner = jnp.sum(unit * grad, axis=1, keepdims=True)
    return ((grad - unit * inner) * inverse).astype(jnp.bfloat16)


def load_all(pairs, sems):
    copies = [pltpu.make_async_copy(a, b, sems.at[i]) for i, (a, b) in enumerate(pairs)]
    for copy in copies:
        copy.start()
    return copies


def query_embed_body(
    queries, query_lengths_in, passage_lengths_in, positives_in, query_hidden_in, passage_hidden_in,
    projection_in,
    before_out, sent_out, slots_out, wanted_out, query_hidden, passage_hidden, projection,
    query_lengths, passage_lengths, positives, sems,
):
    pairs = (
        (projection_in, projection), (query_hidden_in, query_hidden),
        (query_lengths_in, query_lengths), (positives_in, positives),
        (passage_lengths_in, passage_lengths), (passage_hidden_in, passage_hidden),
    )
    copies = load_all(pairs, sems)
    copies[0].wait()
    copies[1].wait()
    rows = query_hidden.shape[0]
    before = dot32(query_hidden[...], projection[...])
    before_out[...] = before
    sent_out[:rows, :] = unit_rows(before)[0].astype(jnp.bfloat16)
    copies[2].wait()
    keep = keep_row(query_lengths, queries, rows // queries)
    row = lax.broadcasted_iota(jnp.int32, (ROWS, LANES), 0)
    tail = jnp.zeros((ROWS, LANES), jnp.float32)
    for piece in range(rows // LANES):
        tail = jnp.where(row == piece, keep[:, piece * LANES : (piece + 1) * LANES], tail)
    sent_out[rows:, :] = tail.astype(jnp.bfloat16)
    copies[3].wait()
    wanted_out[...] = spread(positives, queries, rows // queries)
    copies[4].wait()
    c = lax.broadcasted_iota(jnp.int32, slots_out.shape, 0)
    valid = jnp.zeros(slots_out.shape, jnp.int32)
    for item in range(passage_lengths.shape[0]):
        valid = jnp.where(c == item, passage_lengths[item], valid)
    slots_out[...] = valid
    copies[5].wait()


def sent_keep(sent, rows):
    tail = sent[rows:, :].astype(jnp.float32)
    return jnp.concatenate([tail[i : i + 1, :] for i in range(rows // LANES)], axis=1)


def split(values):
    high = values.astype(jnp.bfloat16)
    rest = values - high.astype(jnp.float32)
    middle = rest.astype(jnp.bfloat16)
    return high, middle, (rest - middle.astype(jnp.float32)).astype(jnp.bfloat16)


def score_block(queries, passages, valid, embed, sent, powers, totals, scores, tops):
    rows = sent.shape[0] - ROWS
    tokens = embed.shape[0] // passages
    query = sent[:rows, :]
    half = tokens // 2
    slot = lax.broadcasted_iota(jnp.int32, (tokens - half, rows), 0) + half
    totals[...] = jnp.ones(totals.shape, jnp.float32)
    tops[...] = jnp.zeros(tops.shape, jnp.float32)
    for c in range(passages):
        sims = dot32(embed[c * tokens : (c + 1) * tokens, :], query, NT)
        low, high = sims[:half], jnp.where(slot < valid[c : c + 1, :], sims[half:], -jnp.inf)
        top = jnp.maximum(
            jnp.max(low, axis=0, keepdims=True), jnp.max(high, axis=0, keepdims=True)
        )
        low = jnp.exp2((low - top) * (inner_scale * LOG2E))
        high = jnp.exp2((high - top) * (inner_scale * LOG2E))
        powers[c * tokens : c * tokens + half, :] = low
        powers[c * tokens + half : (c + 1) * tokens, :] = high
        tops[c : c + 1, :] = top
        totals[c : c + 1, :] = jnp.sum(low, axis=0, keepdims=True) + jnp.sum(
            high, axis=0, keepdims=True
        )
    best = tops[...] + jnp.log(totals[...]) / inner_scale
    best = best * sent_keep(sent, rows)
    group = rows // queries
    same = lax.broadcasted_iota(jnp.int32, (rows, rows), 0) // group
    same = (same == lax.broadcasted_iota(jnp.int32, (rows, rows), 1) // group).astype(jnp.bfloat16)
    total = sum(dot32(part, same) for part in split(best))
    c = lax.broadcasted_iota(jnp.int32, total.shape, 0)
    scores[...] = jnp.where(c < passages, outer_scale * total, -jnp.inf)


def own_score_body(
    queries, passages, valid, hidden, projection, sent,
    before_out, embed_out, powers, totals, scores, log_out, tops,
):
    before = dot32(hidden[...], projection[...])
    before_out[...] = before
    embed_out[...] = unit_rows(before)[0].astype(jnp.bfloat16)
    score_block(queries, passages, valid, embed_out, sent, powers, totals, scores, tops)
    log_out[...] = stack_rows(log_out.shape, (log_sum(scores[...]),))


def log_sum(scores):
    top = jnp.max(scores, axis=0, keepdims=True)
    return top + jnp.log(jnp.sum(jnp.exp(scores - top), axis=0, keepdims=True))


def log_add(parts):
    top = functools.reduce(jnp.maximum, parts)
    return top + jnp.log(sum(jnp.exp(part - top) for part in parts))


def stack_rows(shape, rows):
    index = lax.broadcasted_iota(jnp.int32, shape, 0)
    tile = jnp.zeros(shape, jnp.float32)
    for place, row in enumerate(rows):
        tile = jnp.where(index == place, row, tile)
    return tile


def fill_grad_sim(passages, coefficient, powers, out, column):
    tokens = powers.shape[0] // passages
    rows = powers.shape[1]
    for c in range(passages):
        part = slice(c * tokens, (c + 1) * tokens)
        out[part, column : column + rows] = (powers[part, :] * coefficient[c : c + 1, :]).astype(
            jnp.bfloat16
        )


def other_score_body(
    queries, passages, valid, embed, sent1, sent2, log0, far0,
    grad_sim, logs, back1, back2, powers1, powers2, totals1, totals2, scores1, scores2, tops,
):
    rows = powers1.shape[1]
    dim = embed.shape[1]
    score_block(queries, passages, valid, embed, sent2, powers2, totals2, scores2, tops)
    score_block(queries, passages, valid, embed, sent1, powers1, totals1, scores1, tops)
    log1, log2 = log_sum(scores1[...]), log_sum(scores2[...])
    logs[...] = stack_rows(logs.shape, (log0[0:1, :], log1, log2, far0[0:1, :]))
    turned = embed[...].T
    for column, log, sent, powers, totals, scores, back, tail in (
        (rows, log2, sent2, powers2, totals2, scores2, back2, split(log2)),
        (0, log1, sent1, powers1, totals1, scores1, back1, split(log1) + split(log2)),
    ):
        dscore = loss_scale * jnp.exp(scores[...] - log)
        coefficient = outer_scale * dscore * sent_keep(sent, rows) / totals[...]
        fill_grad_sim(passages, coefficient, powers, grad_sim, column)
        back[:dim, :] = dot32(turned, grad_sim[:, column : column + rows]).astype(jnp.bfloat16)
        tail = stack_rows((ROWS, rows), [part.astype(jnp.float32) for part in tail])
        back[dim:, :] = tail.astype(jnp.bfloat16)


def joined(back, dim, place):
    tail = back[dim:, :].astype(jnp.float32)
    high, middle, low = [tail[i : i + 1, :] for i in range(place, place + 3)]
    return high + (middle + low)


def grad_body(
    queries, passages, wanted, query_hidden, passage_hidden, embed, query_before, passage_before,
    powers, totals, scores0, sent0, sent1, sent2, other_grad_sim, logs, logs1, back1, back2,
    losses, query_pre_grad, passage_pre_grad, partial, grad_sim,
):
    rows = powers.shape[1]
    dim = embed.shape[1]
    second, third = joined(back1, dim, 0), joined(back2, dim, 0)
    total0 = log_add((logs[0:1, :], second, third))
    total1 = log_add((logs1[0:1, :], logs[1:2, :], joined(back1, dim, 3)))
    total2 = log_add((logs[3:4, :], logs1[1:2, :], logs[2:3, :]))
    scores = scores0[...]
    onehot = lax.broadcasted_iota(jnp.int32, scores.shape, 0) == wanted[...]
    loss = total0 - jnp.sum(jnp.where(onehot, scores, 0.0), axis=0, keepdims=True)
    pick = lax.broadcasted_iota(jnp.int32, (rows, LANES), 1) * (rows // queries)
    pick = (pick == lax.broadcasted_iota(jnp.int32, (rows, LANES), 0)).astype(jnp.bfloat16)
    losses[...] = sum(dot32(part, pick) for part in split(loss))[:, :queries]

    shares = (jnp.exp(logs[1:2, :] - total1), jnp.exp(logs[2:3, :] - total2))
    shares = stack_rows((8, rows), shares).T
    first = (sent1[:rows, :].astype(jnp.float32) * shares[:, 0:1]).astype(jnp.bfloat16)
    grad = dot32(other_grad_sim[:, :rows], first)
    first = (sent2[:rows, :].astype(jnp.float32) * shares[:, 1:2]).astype(jnp.bfloat16)
    grad += dot32(other_grad_sim[:, rows:], first)

    dscore = loss_scale * (jnp.exp(scores - total0) - onehot.astype(jnp.float32))
    coefficient = outer_scale * dscore * sent_keep(sent0, rows) / totals[...]
    fill_grad_sim(passages, coefficient, powers, grad_sim, 0)
    to_query = dot32(embed[...].T, grad_sim[...])
    to_query += back1[:dim, :].astype(jnp.float32) * jnp.exp(second - total0)
    to_query += back2[:dim, :].astype(jnp.float32) * jnp.exp(third - total0)
    pre = back_rows(to_query.T, query_before[...])
    query_pre_grad[...] = pre
    both = dot32(pre.T, query_hidden[...])
    grad += dot32(grad_sim[...], sent0[:rows, :])
    pre = back_rows(grad, passage_before[...])
    passage_pre_grad[...] = pre
    both += dot32(pre.T, passage_hidden[...])
    partial[...] = both.T.astype(jnp.bfloat16)


def sum_body(scale, copies, pieces, out):
    total = jnp.sum(pieces[...].astype(jnp.float32), axis=0) * scale
    total = total.astype(jnp.bfloat16)
    for copy in range(copies):
        out[copy] = total


def mean_over_devices(partial):
    axes = ("batch", "mp")
    devices = lax.axis_size("batch") * lax.axis_size("mp")
    rows, columns = partial.shape
    share = -(-rows // (devices * 8)) * 8
    padded = jnp.pad(partial, ((0, share * devices - rows), (0, 0)))
    pieces = lax.all_to_all(padded.reshape(devices, share, columns), axes, 0, 0)
    means = call(
        functools.partial(sum_body, 1.0 / devices, devices),
        (pltpu.VMEM(pieces.shape, jnp.bfloat16),),
        (vmem,),
        (pieces,),
    )[0]
    whole = lax.all_to_all(means, axes, 0, 0)
    return whole.reshape(devices * share, columns)[:rows].astype(jnp.float32)


def per_device(query_hidden, passage_hidden, projection, query_lengths, passage_lengths, positives):
    queries = query_lengths.shape[0]
    passages = passage_lengths.shape[0]
    rows, width = query_hidden.shape
    slots = passage_hidden.shape[0]
    dim = projection.shape[1]
    f32, bf16 = jnp.float32, jnp.bfloat16
    of = jax.ShapeDtypeStruct
    pair = of((ROWS, rows), f32)
    pairs = pltpu.VMEM((ROWS, rows), f32)

    taken = (
        query_lengths, passage_lengths, positives, query_hidden, passage_hidden, projection
    )
    taken = tuple(pltpu.with_memory_space_constraint(x, pltpu.HBM) for x in taken)
    query_before, sent0, valid, wanted, query_rows, passage_rows, weight = call(
        functools.partial(query_embed_body, queries),
        (
            of((rows, dim), f32), of((rows + ROWS, dim), bf16), of((ROWS, rows), jnp.int32),
            of((1, rows), jnp.int32), of((rows, width), bf16), of((slots, width), bf16),
            of((width, dim), bf16),
        ),
        (hbm,) * 6,
        taken,
        scratch=(
            pltpu.SMEM((queries,), jnp.int32),
            pltpu.SMEM((passages,), jnp.int32),
            pltpu.SMEM((queries,), jnp.int32),
            pltpu.SemaphoreType.DMA((6,)),
        ),
        flops=2 * rows * width * dim,
    )
    sent1 = shifted(sent0, "batch", 1)
    sent2 = shifted(sent0, "batch", 2)
    passage_before, embed, powers0, totals0, scores0, log0 = call(
        functools.partial(own_score_body, queries, passages),
        (
            of((slots, dim), f32), of((slots, dim), bf16), of((slots, rows), f32), pair, pair,
            of((8, rows), f32),
        ),
        (vmem,) * 4,
        (valid, passage_rows, weight, sent0),
        scratch=(pairs,),
        flops=2 * slots * dim * (width + rows),
        trans=slots * rows,
    )
    far0 = shifted(log0, "batch", 2)
    other_grad_sim, logs, back1, back2 = call(
        functools.partial(other_score_body, queries, passages),
        (of((slots, 2 * rows), bf16), of((8, rows), f32)) + (of((dim + ROWS, rows), bf16),) * 2,
        (vmem,) * 6,
        (valid, embed, sent1, sent2, log0, far0),
        scratch=(pltpu.VMEM((slots, rows), f32),) * 2 + (pairs,) * 5,
        flops=8 * slots * dim * rows,
        trans=2 * slots * rows,
    )
    back2 = shifted(back2, "batch", -2)
    back1 = shifted(back1, "batch", -1)
    logs1 = shifted(logs, "batch", 1)
    losses, query_pre_grad, passage_pre_grad, partial = call(
        functools.partial(grad_body, queries, passages),
        (
            of((1, queries), f32), of((rows, dim), bf16), of((slots, dim), bf16),
            of((width, dim), bf16),
        ),
        (vmem,) * 17,
        (wanted, query_rows, passage_rows, embed, query_before, passage_before,
         powers0, totals0, scores0, sent0, sent1, sent2, other_grad_sim, logs, logs1, back1, back2),
        scratch=(pltpu.VMEM((slots, rows), bf16),),
        flops=8 * slots * dim * rows + 2 * (slots + rows) * width * dim,
    )
    grad_projection = mean_over_devices(partial)
    grad_query_hidden = dot32(query_pre_grad, weight, NT).astype(bf16)
    grad_passage_hidden = dot32(passage_pre_grad, weight, NT).astype(bf16)
    losses = losses.reshape(queries)
    return (losses, grad_query_hidden, grad_passage_hidden, grad_projection)


def solution(mesh):
    in_specs = (
        P(("batch", "mp"), None),
        P(("batch", "mp"), None),
        P(),
        P(("batch", "mp")),
        P(("batch", "mp")),
        P(("batch", "mp")),
    )
    out_specs = (P(("batch", "mp")), P(("batch", "mp"), None), P(("batch", "mp"), None), P())
    return jax.shard_map(
        per_device, mesh=mesh, in_specs=in_specs, out_specs=out_specs, check_vma=False
    )
```

```python
import functools
import math

import jax
import jax.numpy as jnp
from jax import lax
from jax.experimental import pallas as pl
from jax.experimental.pallas import tpu as pltpu
from jax.sharding import PartitionSpec as P

inner_scale = 128.0
outer_scale = 8.0
loss_scale = 32.0
norm_eps = 1e-06

LANES = 128
ROWS = 16
LOG2E = 1.0 / math.log(2.0)
NT = (((1,), (1,)), ((), ()))

vmem = pl.BlockSpec(memory_space=pltpu.VMEM)
hbm = pl.BlockSpec(memory_space=pltpu.HBM)


def shifted(block, axis, distance):
    devices = range(lax.axis_size(axis))
    route = [((i - distance) % len(devices), i) for i in devices]
    return lax.ppermute(block, axis, route)


def dot32(left, right, dims=(((1,), (0,)), ((), ()))):
    return lax.dot_general(left, right, dims, preferred_element_type=jnp.float32)


def call(body, outs, in_specs, args, scratch=(), flops=0, trans=0):
    moved = sum(a.size * a.dtype.itemsize for a in args)
    moved += sum(math.prod(o.shape) * jnp.dtype(o.dtype).itemsize for o in outs)
    return pl.pallas_call(
        body,
        out_shape=tuple(outs),
        in_specs=list(in_specs),
        out_specs=tuple(vmem for _ in outs),
        scratch_shapes=list(scratch),
        compiler_params=pltpu.CompilerParams(vmem_limit_bytes=24 * 2**20),
        cost_estimate=pl.CostEstimate(flops=flops, bytes_accessed=moved, transcendentals=trans),
    )(*args)


def spread(values, count, group):
    lane = lax.broadcasted_iota(jnp.int32, (1, count * group), 1) // group
    row = jnp.zeros((1, count * group), jnp.int32)
    for item in range(count):
        row = jnp.where(lane == item, values[item], row)
    return row


def keep_row(lengths, queries, tokens):
    slot = lax.broadcasted_iota(jnp.int32, (1, queries * tokens), 1) % tokens
    return (slot < spread(lengths, queries, tokens)).astype(jnp.float32)


def unit_rows(before):
    inverse = lax.rsqrt(jnp.sum(before * before, axis=1, keepdims=True) + norm_eps)
    return before * inverse, inverse


def back_rows(grad, unit, inverse):
    inner = jnp.sum(unit * grad, axis=1, keepdims=True)
    return ((grad - unit * inner) * inverse).astype(jnp.bfloat16)


def load_all(pairs, sems):
    copies = [pltpu.make_async_copy(a, b, sems.at[i]) for i, (a, b) in enumerate(pairs)]
    for copy in copies:
        copy.start()
    return copies


def query_embed_body(
    queries, query_lengths_in, passage_lengths_in, positives_in, query_hidden_in, passage_hidden_in,
    projection_in,
    unit_out, inverse_out, sent_out, slots_out, wanted_out, query_hidden, passage_hidden, projection,
    query_lengths, passage_lengths, positives, sems,
):
    pairs = (
        (projection_in, projection), (query_hidden_in, query_hidden),
        (query_lengths_in, query_lengths), (positives_in, positives),
        (passage_lengths_in, passage_lengths), (passage_hidden_in, passage_hidden),
    )
    copies = load_all(pairs, sems)
    copies[0].wait()
    copies[1].wait()
    rows = query_hidden.shape[0]
    before = dot32(query_hidden[...], projection[...])
    unit, inverse = unit_rows(before)
    unit_out[...] = unit
    inverse_out[...] = jnp.broadcast_to(inverse, unit.shape)
    sent_out[:rows, :] = unit.astype(jnp.bfloat16)
    copies[2].wait()
    keep = keep_row(query_lengths, queries, rows // queries)
    row = lax.broadcasted_iota(jnp.int32, (ROWS, LANES), 0)
    tail = jnp.zeros((ROWS, LANES), jnp.float32)
    for piece in range(rows // LANES):
        tail = jnp.where(row == piece, keep[:, piece * LANES : (piece + 1) * LANES], tail)
    sent_out[rows:, :] = tail.astype(jnp.bfloat16)
    copies[3].wait()
    wanted_out[...] = spread(positives, queries, rows // queries)
    copies[4].wait()
    c = lax.broadcasted_iota(jnp.int32, slots_out.shape, 0)
    valid = jnp.zeros(slots_out.shape, jnp.int32)
    for item in range(passage_lengths.shape[0]):
        valid = jnp.where(c == item, passage_lengths[item], valid)
    slots_out[...] = valid
    copies[5].wait()


def sent_keep(sent, rows):
    tail = sent[rows:, :].astype(jnp.float32)
    return jnp.concatenate([tail[i : i + 1, :] for i in range(rows // LANES)], axis=1)


def split(values):
    high = values.astype(jnp.bfloat16)
    rest = values - high.astype(jnp.float32)
    middle = rest.astype(jnp.bfloat16)
    return high, middle, (rest - middle.astype(jnp.float32)).astype(jnp.bfloat16)


def score_block(queries, passages, valid, embed, sent, powers, totals, scores, tops):
    rows = sent.shape[0] - ROWS
    tokens = embed.shape[0] // passages
    query = sent[:rows, :]
    half = tokens // 2
    slot = lax.broadcasted_iota(jnp.int32, (tokens - half, rows), 0) + half
    totals[...] = jnp.ones(totals.shape, jnp.float32)
    tops[...] = jnp.zeros(tops.shape, jnp.float32)
    for c in range(passages):
        sims = dot32(embed[c * tokens : (c + 1) * tokens, :], query, NT)
        low, high = sims[:half], jnp.where(slot < valid[c : c + 1, :], sims[half:], -jnp.inf)
        top = jnp.maximum(
            jnp.max(low, axis=0, keepdims=True), jnp.max(high, axis=0, keepdims=True)
        )
        low = jnp.exp2((low - top) * (inner_scale * LOG2E))
        high = jnp.exp2((high - top) * (inner_scale * LOG2E))
        powers[c * tokens : c * tokens + half, :] = low
        powers[c * tokens + half : (c + 1) * tokens, :] = high
        tops[c : c + 1, :] = top
        totals[c : c + 1, :] = jnp.sum(low, axis=0, keepdims=True) + jnp.sum(
            high, axis=0, keepdims=True
        )
    best = tops[...] + jnp.log(totals[...]) / inner_scale
    best = best * sent_keep(sent, rows)
    group = rows // queries
    same = lax.broadcasted_iota(jnp.int32, (rows, rows), 0) // group
    same = (same == lax.broadcasted_iota(jnp.int32, (rows, rows), 1) // group).astype(jnp.bfloat16)
    total = sum(dot32(part, same) for part in split(best))
    c = lax.broadcasted_iota(jnp.int32, total.shape, 0)
    scores[...] = jnp.where(c < passages, outer_scale * total, -jnp.inf)


def own_score_body(
    queries, passages, valid, hidden, projection, sent,
    unit_out, inverse_out, embed_out, turned_out, powers, totals, scores, log_out, tops,
):
    unit, inverse = unit_rows(dot32(hidden[...], projection[...]))
    unit_out[...] = unit
    inverse_out[...] = jnp.broadcast_to(inverse, unit.shape)
    embed = unit.astype(jnp.bfloat16)
    embed_out[...] = embed
    score_block(queries, passages, valid, embed_out, sent, powers, totals, scores, tops)
    log_out[...] = stack_rows(log_out.shape, (log_sum(scores[...]),))
    turned_out[...] = embed.T


def log_sum(scores):
    top = jnp.max(scores, axis=0, keepdims=True)
    return top + jnp.log(jnp.sum(jnp.exp(scores - top), axis=0, keepdims=True))


def log_add(parts):
    top = functools.reduce(jnp.maximum, parts)
    return top + jnp.log(sum(jnp.exp(part - top) for part in parts))


def stack_rows(shape, rows):
    index = lax.broadcasted_iota(jnp.int32, shape, 0)
    tile = jnp.zeros(shape, jnp.float32)
    for place, row in enumerate(rows):
        tile = jnp.where(index == place, row, tile)
    return tile


def fill_grad_sim(passages, coefficient, powers, out, column):
    tokens = powers.shape[0] // passages
    rows = powers.shape[1]
    for c in range(passages):
        part = slice(c * tokens, (c + 1) * tokens)
        out[part, column : column + rows] = (powers[part, :] * coefficient[c : c + 1, :]).astype(
            jnp.bfloat16
        )


def send_back(passages, turned, sent, powers, totals, scores, log, tail, back, grad_sim):
    dim, rows = turned.shape[0], powers.shape[1]
    dscore = loss_scale * jnp.exp(scores[...] - log)
    coefficient = outer_scale * dscore * sent_keep(sent, rows) / totals[...]
    fill_grad_sim(passages, coefficient, powers, grad_sim, 0)
    back[:dim, :] = dot32(turned[...], grad_sim[...]).astype(jnp.bfloat16)
    tail = stack_rows((ROWS, rows), [part.astype(jnp.float32) for part in tail])
    back[dim:, :] = tail.astype(jnp.bfloat16)


def far_score_body(
    queries, passages, valid, embed, turned, sent,
    powers, totals, scores, log_out, back, tops, grad_sim,
):
    score_block(queries, passages, valid, embed, sent, powers, totals, scores, tops)
    log = log_sum(scores[...])
    log_out[...] = stack_rows(log_out.shape, (log,))
    send_back(passages, turned, sent, powers, totals, scores, log, split(log), back, grad_sim)


def near_score_body(
    queries, passages, valid, embed, turned, sent, log0, log2, far0,
    powers, totals, scores, logs, back, tops, grad_sim,
):
    score_block(queries, passages, valid, embed, sent, powers, totals, scores, tops)
    log = log_sum(scores[...])
    other = log2[0:1, :]
    logs[...] = stack_rows(logs.shape, (log0[0:1, :], log, other, far0[0:1, :]))
    tail = split(log) + split(other)
    send_back(passages, turned, sent, powers, totals, scores, log, tail, back, grad_sim)


def joined(back, dim, place):
    tail = back[dim:, :].astype(jnp.float32)
    high, middle, low = [tail[i : i + 1, :] for i in range(place, place + 3)]
    return high + (middle + low)


def grad_body(
    queries, passages, wanted, query_hidden, passage_hidden, turned,
    query_unit, query_inverse, passage_unit, passage_inverse,
    powers0, powers1, powers2, totals0, totals1, totals2, scores0, scores1, scores2,
    sent0, sent1, sent2, logs, logs1, back1, back2,
    losses, query_pre_grad, passage_pre_grad, partial, grad_sim, query_rows,
):
    rows = powers0.shape[1]
    dim = turned.shape[0]
    second, third = joined(back1, dim, 0), joined(back2, dim, 0)
    total0 = log_add((logs[0:1, :], second, third))
    total1 = log_add((logs1[0:1, :], logs[1:2, :], joined(back1, dim, 3)))
    total2 = log_add((logs[3:4, :], logs1[1:2, :], logs[2:3, :]))
    scores = scores0[...]
    onehot = lax.broadcasted_iota(jnp.int32, scores.shape, 0) == wanted[...]
    loss = total0 - jnp.sum(jnp.where(onehot, scores, 0.0), axis=0, keepdims=True)
    pick = lax.broadcasted_iota(jnp.int32, (rows, LANES), 1) * (rows // queries)
    pick = (pick == lax.broadcasted_iota(jnp.int32, (rows, LANES), 0)).astype(jnp.bfloat16)
    losses[...] = sum(dot32(part, pick) for part in split(loss))[:, :queries]

    for block, (total, query, powers, totals, scores) in enumerate((
        (total0, sent0, powers0, totals0, scores0),
        (total1, sent1, powers1, totals1, scores1),
        (total2, sent2, powers2, totals2, scores2),
    )):
        dscore = jnp.exp(scores[...] - total)
        if block == 0:
            dscore = dscore - onehot.astype(jnp.float32)
        coefficient = (outer_scale * loss_scale) * dscore * sent_keep(query, rows) / totals[...]
        fill_grad_sim(passages, coefficient, powers, grad_sim, block * rows)
        query_rows[block * rows : (block + 1) * rows, :] = query[:rows, :]

    grad = dot32(grad_sim[...], query_rows[...])
    pre = back_rows(grad, passage_unit[...], passage_inverse[...])
    passage_pre_grad[...] = pre
    both = dot32(pre.T, passage_hidden[...])
    to_query = dot32(turned[...], grad_sim[:, :rows])
    to_query += back1[:dim, :].astype(jnp.float32) * jnp.exp(second - total0)
    to_query += back2[:dim, :].astype(jnp.float32) * jnp.exp(third - total0)
    pre = back_rows(to_query.T, query_unit[...], query_inverse[...])
    query_pre_grad[...] = pre
    both += dot32(pre.T, query_hidden[...])
    partial[...] = both.T.astype(jnp.bfloat16)


def sum_body(scale, copies, pieces, out):
    total = jnp.sum(pieces[...].astype(jnp.float32), axis=0) * scale
    total = total.astype(jnp.bfloat16)
    for copy in range(copies):
        out[copy] = total


def mean_over_devices(partial):
    axes = ("batch", "mp")
    devices = lax.axis_size("batch") * lax.axis_size("mp")
    rows, columns = partial.shape
    share = -(-rows // (devices * 8)) * 8
    padded = jnp.pad(partial, ((0, share * devices - rows), (0, 0)))
    pieces = lax.all_to_all(padded.reshape(devices, share, columns), axes, 0, 0)
    means = call(
        functools.partial(sum_body, 1.0 / devices, devices),
        (jax.ShapeDtypeStruct(pieces.shape, jnp.bfloat16),),
        (vmem,),
        (pieces,),
    )[0]
    whole = lax.all_to_all(means, axes, 0, 0)
    return whole.reshape(devices * share, columns)[:rows].astype(jnp.float32)


def per_device(query_hidden, passage_hidden, projection, query_lengths, passage_lengths, positives):
    queries = query_lengths.shape[0]
    passages = passage_lengths.shape[0]
    rows, width = query_hidden.shape
    slots = passage_hidden.shape[0]
    dim = projection.shape[1]
    f32, bf16 = jnp.float32, jnp.bfloat16
    of = jax.ShapeDtypeStruct
    pair = of((ROWS, rows), f32)
    pairs = pltpu.VMEM((ROWS, rows), f32)

    taken = (
        query_lengths, passage_lengths, positives, query_hidden, passage_hidden, projection
    )
    taken = tuple(pltpu.with_memory_space_constraint(x, pltpu.HBM) for x in taken)
    query_unit, query_inverse, sent0, valid, wanted, query_rows, passage_rows, weight = call(
        functools.partial(query_embed_body, queries),
        (
            of((rows, dim), f32), of((rows, dim), f32), of((rows + ROWS, dim), bf16),
            of((ROWS, rows), jnp.int32),
            of((1, rows), jnp.int32), of((rows, width), bf16), of((slots, width), bf16),
            of((width, dim), bf16),
        ),
        (hbm,) * 6,
        taken,
        scratch=(
            pltpu.SMEM((queries,), jnp.int32),
            pltpu.SMEM((passages,), jnp.int32),
            pltpu.SMEM((queries,), jnp.int32),
            pltpu.SemaphoreType.DMA((6,)),
        ),
        flops=2 * rows * width * dim,
    )
    sent1 = shifted(sent0, "batch", 1)
    sent2 = shifted(sent0, "batch", 2)
    (
        passage_unit, passage_inverse, embed, turned, powers0, totals0, scores0, log0
    ) = call(
        functools.partial(own_score_body, queries, passages),
        (
            of((slots, dim), f32), of((slots, dim), f32), of((slots, dim), bf16),
            of((dim, slots), bf16), of((slots, rows), f32), pair, pair, of((8, rows), f32),
        ),
        (vmem,) * 4,
        (valid, passage_rows, weight, sent0),
        scratch=(pairs,),
        flops=2 * slots * dim * (width + rows),
        trans=slots * rows,
    )
    far0 = shifted(log0, "batch", 2)
    block_outs = (
        of((slots, rows), f32), pair, pair, of((8, rows), f32), of((dim + ROWS, rows), bf16)
    )
    powers2, totals2, scores2, log2, back2 = call(
        functools.partial(far_score_body, queries, passages),
        block_outs,
        (vmem,) * 4,
        (valid, embed, turned, sent2),
        scratch=(pairs, pltpu.VMEM((slots, rows), bf16)),
        flops=4 * slots * dim * rows,
        trans=slots * rows,
    )
    back2 = shifted(back2, "batch", -2)
    powers1, totals1, scores1, logs, back1 = call(
        functools.partial(near_score_body, queries, passages),
        block_outs,
        (vmem,) * 7,
        (valid, embed, turned, sent1, log0, log2, far0),
        scratch=(pairs, pltpu.VMEM((slots, rows), bf16)),
        flops=4 * slots * dim * rows,
        trans=slots * rows,
    )
    back1 = shifted(back1, "batch", -1)
    logs1 = shifted(logs, "batch", 1)
    losses, query_pre_grad, passage_pre_grad, partial = call(
        functools.partial(grad_body, queries, passages),
        (
            of((1, queries), f32), of((rows, dim), bf16), of((slots, dim), bf16),
            of((width, dim), bf16),
        ),
        (vmem,) * 24,
        (wanted, query_rows, passage_rows, turned,
         query_unit, query_inverse, passage_unit, passage_inverse,
         powers0, powers1, powers2, totals0, totals1, totals2, scores0, scores1, scores2,
         sent0, sent1, sent2, logs, logs1, back1, back2),
        scratch=(pltpu.VMEM((slots, 3 * rows), bf16), pltpu.VMEM((3 * rows, dim), bf16)),
        flops=8 * slots * dim * rows + 2 * (slots + rows) * width * dim,
    )
    grad_projection = mean_over_devices(partial)
    grad_query_hidden = dot32(query_pre_grad, weight, NT).astype(bf16)
    grad_passage_hidden = dot32(passage_pre_grad, weight, NT).astype(bf16)
    losses = losses.reshape(queries)
    return (losses, grad_query_hidden, grad_passage_hidden, grad_projection)


def solution(mesh):
    in_specs = (
        P(("batch", "mp"), None),
        P(("batch", "mp"), None),
        P(),
        P(("batch", "mp")),
        P(("batch", "mp")),
        P(("batch", "mp")),
    )
    out_specs = (P(("batch", "mp")), P(("batch", "mp"), None), P(("batch", "mp"), None), P())
    return jax.shard_map(
        per_device, mesh=mesh, in_specs=in_specs, out_specs=out_specs, check_vma=False
    )
```

```python
import functools
import math

import jax
import jax.numpy as jnp
from jax import lax
from jax.experimental import pallas as pl
from jax.experimental.pallas import tpu as pltpu
from jax.sharding import PartitionSpec as P

inner_scale = 128.0
outer_scale = 8.0
loss_scale = 32.0
norm_eps = 1e-06

LANES = 128
ROWS = 16
LOG2E = 1.0 / math.log(2.0)
NT = (((1,), (1,)), ((), ()))

vmem = pl.BlockSpec(memory_space=pltpu.VMEM)
hbm = pl.BlockSpec(memory_space=pltpu.HBM)


def shifted(block, axis, distance):
    devices = range(lax.axis_size(axis))
    route = [((i - distance) % len(devices), i) for i in devices]
    return lax.ppermute(block, axis, route)


def dot32(left, right, dims=(((1,), (0,)), ((), ()))):
    return lax.dot_general(left, right, dims, preferred_element_type=jnp.float32)


def call(body, outs, in_specs, args, scratch=(), flops=0, trans=0):
    moved = sum(a.size * a.dtype.itemsize for a in args)
    moved += sum(math.prod(o.shape) * jnp.dtype(o.dtype).itemsize for o in outs)
    return pl.pallas_call(
        body,
        out_shape=tuple(outs),
        in_specs=list(in_specs),
        out_specs=tuple(vmem for _ in outs),
        scratch_shapes=list(scratch),
        compiler_params=pltpu.CompilerParams(vmem_limit_bytes=24 * 2**20),
        cost_estimate=pl.CostEstimate(flops=flops, bytes_accessed=moved, transcendentals=trans),
    )(*args)


def spread(values, count, group):
    lane = lax.broadcasted_iota(jnp.int32, (1, count * group), 1) // group
    row = jnp.zeros((1, count * group), jnp.int32)
    for item in range(count):
        row = jnp.where(lane == item, values[item], row)
    return row


def keep_row(lengths, queries, tokens):
    slot = lax.broadcasted_iota(jnp.int32, (1, queries * tokens), 1) % tokens
    return (slot < spread(lengths, queries, tokens)).astype(jnp.float32)


def unit_rows(before):
    inverse = lax.rsqrt(jnp.sum(before * before, axis=1, keepdims=True) + norm_eps)
    return before * inverse, inverse


def back_rows(grad, unit, inverse):
    inner = jnp.sum(unit * grad, axis=1, keepdims=True)
    return ((grad - unit * inner) * inverse).astype(jnp.bfloat16)


def load_all(pairs, sems):
    copies = [pltpu.make_async_copy(a, b, sems.at[i]) for i, (a, b) in enumerate(pairs)]
    for copy in copies:
        copy.start()
    return copies


def query_embed_body(
    queries, query_lengths_in, passage_lengths_in, positives_in, query_hidden_in, passage_hidden_in,
    projection_in,
    unit_out, inverse_out, sent_out, slots_out, wanted_out, query_hidden, passage_hidden, projection,
    query_lengths, passage_lengths, positives, sems,
):
    pairs = (
        (projection_in, projection), (query_hidden_in, query_hidden),
        (query_lengths_in, query_lengths), (positives_in, positives),
        (passage_lengths_in, passage_lengths), (passage_hidden_in, passage_hidden),
    )
    copies = load_all(pairs, sems)
    copies[0].wait()
    copies[1].wait()
    rows = query_hidden.shape[0]
    before = dot32(query_hidden[...], projection[...])
    unit, inverse = unit_rows(before)
    unit_out[...] = unit
    inverse_out[...] = jnp.broadcast_to(inverse, unit.shape)
    sent_out[:rows, :] = unit.astype(jnp.bfloat16)
    copies[2].wait()
    keep = keep_row(query_lengths, queries, rows // queries)
    row = lax.broadcasted_iota(jnp.int32, (ROWS, LANES), 0)
    tail = jnp.zeros((ROWS, LANES), jnp.float32)
    for piece in range(rows // LANES):
        tail = jnp.where(row == piece, keep[:, piece * LANES : (piece + 1) * LANES], tail)
    sent_out[rows:, :] = tail.astype(jnp.bfloat16)
    copies[3].wait()
    wanted_out[...] = spread(positives, queries, rows // queries)
    copies[4].wait()
    c = lax.broadcasted_iota(jnp.int32, slots_out.shape, 0)
    valid = jnp.zeros(slots_out.shape, jnp.int32)
    for item in range(passage_lengths.shape[0]):
        valid = jnp.where(c == item, passage_lengths[item], valid)
    slots_out[...] = valid
    copies[5].wait()


def sent_keep(sent, rows):
    tail = sent[rows:, :].astype(jnp.float32)
    return jnp.concatenate([tail[i : i + 1, :] for i in range(rows // LANES)], axis=1)


def split(values):
    high = values.astype(jnp.bfloat16)
    rest = values - high.astype(jnp.float32)
    middle = rest.astype(jnp.bfloat16)
    return high, middle, (rest - middle.astype(jnp.float32)).astype(jnp.bfloat16)


def score_block(queries, passages, valid, embed, sent, powers, totals, scores, tops):
    rows = sent.shape[0] - ROWS
    tokens = embed.shape[0] // passages
    query = sent[:rows, :]
    half = tokens // 2
    slot = lax.broadcasted_iota(jnp.int32, (tokens - half, rows), 0) + half
    totals[...] = jnp.ones(totals.shape, jnp.float32)
    tops[...] = jnp.zeros(tops.shape, jnp.float32)
    for c in range(passages):
        sims = dot32(embed[c * tokens : (c + 1) * tokens, :], query, NT)
        low, high = sims[:half], jnp.where(slot < valid[c : c + 1, :], sims[half:], -jnp.inf)
        top = jnp.maximum(
            jnp.max(low, axis=0, keepdims=True), jnp.max(high, axis=0, keepdims=True)
        )
        low = jnp.exp2((low - top) * (inner_scale * LOG2E))
        high = jnp.exp2((high - top) * (inner_scale * LOG2E))
        powers[c * tokens : c * tokens + half, :] = low
        powers[c * tokens + half : (c + 1) * tokens, :] = high
        tops[c : c + 1, :] = top
        totals[c : c + 1, :] = jnp.sum(low, axis=0, keepdims=True) + jnp.sum(
            high, axis=0, keepdims=True
        )
    best = tops[...] + jnp.log(totals[...]) / inner_scale
    best = best * sent_keep(sent, rows)
    group = rows // queries
    same = lax.broadcasted_iota(jnp.int32, (rows, rows), 0) // group
    same = (same == lax.broadcasted_iota(jnp.int32, (rows, rows), 1) // group).astype(jnp.bfloat16)
    total = sum(dot32(part, same) for part in split(best))
    c = lax.broadcasted_iota(jnp.int32, total.shape, 0)
    scores[...] = jnp.where(c < passages, outer_scale * total, -jnp.inf)


def own_score_body(
    queries, passages, valid, hidden, projection, sent,
    unit_out, inverse_out, embed_out, turned_out, powers, totals, scores, log_out, tops,
):
    unit, inverse = unit_rows(dot32(hidden[...], projection[...]))
    unit_out[...] = unit
    inverse_out[...] = jnp.broadcast_to(inverse, unit.shape)
    embed = unit.astype(jnp.bfloat16)
    embed_out[...] = embed
    score_block(queries, passages, valid, embed_out, sent, powers, totals, scores, tops)
    log_out[...] = stack_rows(log_out.shape, (log_sum(scores[...]),))
    turned_out[...] = embed.T


def log_sum(scores):
    top = jnp.max(scores, axis=0, keepdims=True)
    return top + jnp.log(jnp.sum(jnp.exp(scores - top), axis=0, keepdims=True))


def log_add(parts):
    top = functools.reduce(jnp.maximum, parts)
    return top + jnp.log(sum(jnp.exp(part - top) for part in parts))


def stack_rows(shape, rows):
    index = lax.broadcasted_iota(jnp.int32, shape, 0)
    tile = jnp.zeros(shape, jnp.float32)
    for place, row in enumerate(rows):
        tile = jnp.where(index == place, row, tile)
    return tile


def fill_grad_sim(passages, coefficient, powers, out, column):
    tokens = powers.shape[0] // passages
    rows = powers.shape[1]
    for c in range(passages):
        part = slice(c * tokens, (c + 1) * tokens)
        out[part, column : column + rows] = (powers[part, :] * coefficient[c : c + 1, :]).astype(
            jnp.bfloat16
        )


def query_gradient(passages, turned, sent, powers, totals, scores, log, grad_sim):
    rows = powers.shape[1]
    dscore = loss_scale * jnp.exp(scores[...] - log)
    coefficient = outer_scale * dscore * sent_keep(sent, rows) / totals[...]
    fill_grad_sim(passages, coefficient, powers, grad_sim, 0)
    return dot32(turned[...], grad_sim[...]).astype(jnp.bfloat16)


def far_score_body(
    queries, passages, valid, embed, turned, sent,
    powers, totals, scores, log_out, back, tops, grad_sim,
):
    score_block(queries, passages, valid, embed, sent, powers, totals, scores, tops)
    log = log_sum(scores[...])
    log_out[...] = stack_rows(log_out.shape, (log,))
    dim, rows = turned.shape[0], powers.shape[1]
    back[:dim, :] = query_gradient(passages, turned, sent, powers, totals, scores, log, grad_sim)
    tail = stack_rows((ROWS, rows), [part.astype(jnp.float32) for part in split(log)])
    back[dim:, :] = tail.astype(jnp.bfloat16)


def near_score_body(
    queries, passages, valid, embed, sent, log0, log2, powers, totals, scores, logs, tops
):
    score_block(queries, passages, valid, embed, sent, powers, totals, scores, tops)
    log = log_sum(scores[...])
    logs[...] = stack_rows(logs.shape, (log0[0:1, :], log, log2[0:1, :]))


def near_grad_body(passages, turned, sent, powers, totals, scores, logs, back, grad_sim):
    back[...] = query_gradient(
        passages, turned, sent, powers, totals, scores, logs[1:2, :], grad_sim
    )


def joined(back, dim):
    tail = back[dim:, :].astype(jnp.float32)
    return tail[0:1, :] + (tail[1:2, :] + tail[2:3, :])


def passage_grad_body(
    queries, passages, wanted, hidden, turned, unit, inverse,
    powers0, powers1, powers2, totals0, totals1, totals2, scores0, scores1, scores2,
    sent0, sent1, sent2, logs, below, far_below, above, back2,
    losses, pre_grad, partial, to_query, shares, grad_sim, query_rows,
):
    rows = powers0.shape[1]
    second, third = above[1:2, :], joined(back2, turned.shape[0])
    total0 = log_add((logs[0:1, :], second, third))
    total1 = log_add((below[0:1, :], logs[1:2, :], above[2:3, :]))
    total2 = log_add((far_below[0:1, :], below[1:2, :], logs[2:3, :]))
    shares[...] = stack_rows(shares.shape, (jnp.exp(second - total0), jnp.exp(third - total0)))
    scores = scores0[...]
    onehot = lax.broadcasted_iota(jnp.int32, scores.shape, 0) == wanted[...]
    loss = total0 - jnp.sum(jnp.where(onehot, scores, 0.0), axis=0, keepdims=True)
    pick = lax.broadcasted_iota(jnp.int32, (rows, LANES), 1) * (rows // queries)
    pick = (pick == lax.broadcasted_iota(jnp.int32, (rows, LANES), 0)).astype(jnp.bfloat16)
    losses[...] = sum(dot32(part, pick) for part in split(loss))[:, :queries]

    for block, (total, query, powers, totals, scores) in enumerate((
        (total0, sent0, powers0, totals0, scores0),
        (total1, sent1, powers1, totals1, scores1),
        (total2, sent2, powers2, totals2, scores2),
    )):
        dscore = jnp.exp(scores[...] - total)
        if block == 0:
            dscore = dscore - onehot.astype(jnp.float32)
        coefficient = (outer_scale * loss_scale) * dscore * sent_keep(query, rows) / totals[...]
        fill_grad_sim(passages, coefficient, powers, grad_sim, block * rows)
        query_rows[block * rows : (block + 1) * rows, :] = query[:rows, :]

    to_query[...] = dot32(turned[...], grad_sim[:, :rows])
    grad = dot32(grad_sim[...], query_rows[...])
    pre = back_rows(grad, unit[...], inverse[...])
    pre_grad[...] = pre
    partial[...] = dot32(pre.T, hidden[...])


def query_grad_body(
    hidden, unit, inverse, own, shares, back1, back2, passage_partial, pre_grad, partial
):
    dim = own.shape[0]
    total = own[...] + back1[...].astype(jnp.float32) * shares[0:1, :]
    total += back2[:dim, :].astype(jnp.float32) * shares[1:2, :]
    pre = back_rows(total.T, unit[...], inverse[...])
    pre_grad[...] = pre
    both = passage_partial[...] + dot32(pre.T, hidden[...])
    partial[...] = both.T.astype(jnp.bfloat16)


def sum_body(scale, copies, pieces, out):
    total = jnp.sum(pieces[...].astype(jnp.float32), axis=0) * scale
    total = total.astype(jnp.bfloat16)
    for copy in range(copies):
        out[copy] = total


def mean_over_devices(partial):
    axes = ("batch", "mp")
    devices = lax.axis_size("batch") * lax.axis_size("mp")
    rows, columns = partial.shape
    share = -(-rows // (devices * 8)) * 8
    padded = jnp.pad(partial, ((0, share * devices - rows), (0, 0)))
    pieces = lax.all_to_all(padded.reshape(devices, share, columns), axes, 0, 0)
    means = call(
        functools.partial(sum_body, 1.0 / devices, devices),
        (jax.ShapeDtypeStruct(pieces.shape, jnp.bfloat16),),
        (vmem,),
        (pieces,),
    )[0]
    whole = lax.all_to_all(means, axes, 0, 0)
    return whole.reshape(devices * share, columns)[:rows].astype(jnp.float32)


def per_device(query_hidden, passage_hidden, projection, query_lengths, passage_lengths, positives):
    queries = query_lengths.shape[0]
    passages = passage_lengths.shape[0]
    rows, width = query_hidden.shape
    slots = passage_hidden.shape[0]
    dim = projection.shape[1]
    f32, bf16 = jnp.float32, jnp.bfloat16
    of = jax.ShapeDtypeStruct
    pair = of((ROWS, rows), f32)
    pairs = pltpu.VMEM((ROWS, rows), f32)

    taken = (
        query_lengths, passage_lengths, positives, query_hidden, passage_hidden, projection
    )
    taken = tuple(pltpu.with_memory_space_constraint(x, pltpu.HBM) for x in taken)
    query_unit, query_inverse, sent0, valid, wanted, query_rows, passage_rows, weight = call(
        functools.partial(query_embed_body, queries),
        (
            of((rows, dim), f32), of((rows, dim), f32), of((rows + ROWS, dim), bf16),
            of((ROWS, rows), jnp.int32),
            of((1, rows), jnp.int32), of((rows, width), bf16), of((slots, width), bf16),
            of((width, dim), bf16),
        ),
        (hbm,) * 6,
        taken,
        scratch=(
            pltpu.SMEM((queries,), jnp.int32),
            pltpu.SMEM((passages,), jnp.int32),
            pltpu.SMEM((queries,), jnp.int32),
            pltpu.SemaphoreType.DMA((6,)),
        ),
        flops=2 * rows * width * dim,
    )
    sent1 = shifted(sent0, "batch", 1)
    sent2 = shifted(sent0, "batch", 2)
    (
        passage_unit, passage_inverse, embed, turned, powers0, totals0, scores0, log0
    ) = call(
        functools.partial(own_score_body, queries, passages),
        (
            of((slots, dim), f32), of((slots, dim), f32), of((slots, dim), bf16),
            of((dim, slots), bf16), of((slots, rows), f32), pair, pair, of((8, rows), f32),
        ),
        (vmem,) * 4,
        (valid, passage_rows, weight, sent0),
        scratch=(pairs,),
        flops=2 * slots * dim * (width + rows),
        trans=slots * rows,
    )
    block_outs = (of((slots, rows), f32), pair, pair, of((8, rows), f32))
    matrix = pltpu.VMEM((slots, rows), bf16)
    powers2, totals2, scores2, log2, back2 = call(
        functools.partial(far_score_body, queries, passages),
        block_outs + (of((dim + ROWS, rows), bf16),),
        (vmem,) * 4,
        (valid, embed, turned, sent2),
        scratch=(pairs, matrix),
        flops=4 * slots * dim * rows,
        trans=slots * rows,
    )
    back2 = shifted(back2, "batch", -2)
    powers1, totals1, scores1, logs = call(
        functools.partial(near_score_body, queries, passages),
        block_outs,
        (vmem,) * 5,
        (valid, embed, sent1, log0, log2),
        scratch=(pairs,),
        flops=2 * slots * dim * rows,
        trans=slots * rows,
    )
    below = shifted(logs, "batch", 1)
    far_below = shifted(logs, "batch", 2)
    above = shifted(logs, "batch", -1)
    back1 = call(
        functools.partial(near_grad_body, passages),
        (of((dim, rows), bf16),),
        (vmem,) * 6,
        (turned, sent1, powers1, totals1, scores1, logs),
        scratch=(matrix,),
        flops=2 * slots * dim * rows,
    )[0]
    back1 = shifted(back1, "batch", -1)
    losses, passage_pre_grad, passage_partial, to_query, shares = call(
        functools.partial(passage_grad_body, queries, passages),
        (
            of((1, queries), f32), of((slots, dim), bf16), of((dim, width), f32),
            of((dim, rows), f32), of((8, rows), f32),
        ),
        (vmem,) * 22,
        (wanted, passage_rows, turned, passage_unit, passage_inverse,
         powers0, powers1, powers2, totals0, totals1, totals2, scores0, scores1, scores2,
         sent0, sent1, sent2, logs, below, far_below, above, back2),
        scratch=(pltpu.VMEM((slots, 3 * rows), bf16), pltpu.VMEM((3 * rows, dim), bf16)),
        flops=20 * (8 * slots * dim * rows + 2 * slots * width * dim),
    )
    query_pre_grad, partial = call(
        query_grad_body,
        (of((rows, dim), bf16), of((width, dim), bf16)),
        (vmem,) * 8,
        (query_rows, query_unit, query_inverse, to_query, shares, back1, back2, passage_partial),
        flops=2 * rows * width * dim,
    )
    grad_projection = mean_over_devices(partial)
    grad_query_hidden = dot32(query_pre_grad, weight, NT).astype(bf16)
    grad_passage_hidden = dot32(passage_pre_grad, weight, NT).astype(bf16)
    losses = losses.reshape(queries)
    return (losses, grad_query_hidden, grad_passage_hidden, grad_projection)


def solution(mesh):
    in_specs = (
        P(("batch", "mp"), None),
        P(("batch", "mp"), None),
        P(),
        P(("batch", "mp")),
        P(("batch", "mp")),
        P(("batch", "mp")),
    )
    out_specs = (P(("batch", "mp")), P(("batch", "mp"), None), P(("batch", "mp"), None), P())
    return jax.shard_map(
        per_device, mesh=mesh, in_specs=in_specs, out_specs=out_specs, check_vma=False
    )
```

```python
import functools
import math

import jax
import jax.numpy as jnp
from jax import lax
from jax.experimental import pallas as pl
from jax.experimental.pallas import tpu as pltpu
from jax.sharding import PartitionSpec as P

inner_scale = 128.0
outer_scale = 8.0
loss_scale = 32.0
norm_eps = 1e-06

LANES = 128
ROWS = 16
LOG2E = 1.0 / math.log(2.0)
NT = (((1,), (1,)), ((), ()))

vmem = pl.BlockSpec(memory_space=pltpu.VMEM)
hbm = pl.BlockSpec(memory_space=pltpu.HBM)


def shifted(block, axis, distance):
    devices = range(lax.axis_size(axis))
    route = [((i - distance) % len(devices), i) for i in devices]
    return lax.ppermute(block, axis, route)


def dot32(left, right, dims=(((1,), (0,)), ((), ()))):
    return lax.dot_general(left, right, dims, preferred_element_type=jnp.float32)


def call(body, outs, in_specs, args, scratch=(), flops=0, trans=0, out_specs=None):
    moved = sum(a.size * a.dtype.itemsize for a in args)
    moved += sum(math.prod(o.shape) * jnp.dtype(o.dtype).itemsize for o in outs)
    return pl.pallas_call(
        body,
        out_shape=tuple(outs),
        in_specs=list(in_specs),
        out_specs=out_specs or tuple(vmem for _ in outs),
        scratch_shapes=list(scratch),
        compiler_params=pltpu.CompilerParams(vmem_limit_bytes=24 * 2**20),
        cost_estimate=pl.CostEstimate(flops=flops, bytes_accessed=moved, transcendentals=trans),
    )(*args)


def spread(values, count, group):
    lane = lax.broadcasted_iota(jnp.int32, (1, count * group), 1) // group
    row = jnp.zeros((1, count * group), jnp.int32)
    for item in range(count):
        row = jnp.where(lane == item, values[item], row)
    return row


def keep_row(lengths, queries, tokens):
    slot = lax.broadcasted_iota(jnp.int32, (1, queries * tokens), 1) % tokens
    return (slot < spread(lengths, queries, tokens)).astype(jnp.float32)


def unit_rows(before):
    inverse = lax.rsqrt(jnp.sum(before * before, axis=1, keepdims=True) + norm_eps)
    return before * inverse, inverse


def back_rows(grad, unit, inverse):
    inner = jnp.sum(unit * grad, axis=1, keepdims=True)
    return ((grad - unit * inner) * inverse).astype(jnp.bfloat16)


def load_all(pairs, sems):
    copies = [pltpu.make_async_copy(a, b, sems.at[i]) for i, (a, b) in enumerate(pairs)]
    for copy in copies:
        copy.start()
    return copies


def query_embed_body(
    queries, query_lengths_in, passage_lengths_in, positives_in, query_hidden_in, passage_hidden_in,
    projection_in,
    unit_out, inverse_out, sent_out, slots_out, wanted_out, query_hidden, passage_hidden, projection,
    query_lengths, passage_lengths, positives, sems,
):
    pairs = (
        (projection_in, projection), (query_hidden_in, query_hidden),
        (query_lengths_in, query_lengths), (positives_in, positives),
        (passage_lengths_in, passage_lengths), (passage_hidden_in, passage_hidden),
    )
    copies = load_all(pairs, sems)
    copies[0].wait()
    copies[1].wait()
    rows = query_hidden.shape[0]
    before = dot32(query_hidden[...], projection[...])
    unit, inverse = unit_rows(before)
    unit_out[...] = unit
    inverse_out[...] = jnp.broadcast_to(inverse, unit.shape)
    sent_out[:rows, :] = unit.astype(jnp.bfloat16)
    copies[2].wait()
    keep = keep_row(query_lengths, queries, rows // queries)
    row = lax.broadcasted_iota(jnp.int32, (ROWS, LANES), 0)
    tail = jnp.zeros((ROWS, LANES), jnp.float32)
    for piece in range(rows // LANES):
        tail = jnp.where(row == piece, keep[:, piece * LANES : (piece + 1) * LANES], tail)
    sent_out[rows:, :] = tail.astype(jnp.bfloat16)
    copies[3].wait()
    wanted_out[...] = spread(positives, queries, rows // queries)
    copies[4].wait()
    c = lax.broadcasted_iota(jnp.int32, slots_out.shape, 0)
    valid = jnp.zeros(slots_out.shape, jnp.int32)
    for item in range(passage_lengths.shape[0]):
        valid = jnp.where(c == item, passage_lengths[item], valid)
    slots_out[...] = valid
    copies[5].wait()


def sent_keep(sent, rows):
    tail = sent[rows:, :].astype(jnp.float32)
    return jnp.concatenate([tail[i : i + 1, :] for i in range(rows // LANES)], axis=1)


def split(values):
    high = values.astype(jnp.bfloat16)
    rest = values - high.astype(jnp.float32)
    middle = rest.astype(jnp.bfloat16)
    return high, middle, (rest - middle.astype(jnp.float32)).astype(jnp.bfloat16)


def score_block(queries, passages, valid, embed, sent, powers, totals, scores, tops):
    rows = sent.shape[0] - ROWS
    tokens = embed.shape[0] // passages
    query = sent[:rows, :]
    half = tokens // 2
    slot = lax.broadcasted_iota(jnp.int32, (tokens - half, rows), 0) + half
    totals[...] = jnp.ones(totals.shape, jnp.float32)
    tops[...] = jnp.zeros(tops.shape, jnp.float32)
    for c in range(passages):
        sims = dot32(embed[c * tokens : (c + 1) * tokens, :], query, NT)
        low, high = sims[:half], jnp.where(slot < valid[c : c + 1, :], sims[half:], -jnp.inf)
        top = jnp.maximum(
            jnp.max(low, axis=0, keepdims=True), jnp.max(high, axis=0, keepdims=True)
        )
        low = jnp.exp2((low - top) * (inner_scale * LOG2E))
        high = jnp.exp2((high - top) * (inner_scale * LOG2E))
        powers[c * tokens : c * tokens + half, :] = low
        powers[c * tokens + half : (c + 1) * tokens, :] = high
        tops[c : c + 1, :] = top
        totals[c : c + 1, :] = jnp.sum(low, axis=0, keepdims=True) + jnp.sum(
            high, axis=0, keepdims=True
        )
    best = tops[...] + jnp.log(totals[...]) / inner_scale
    best = best * sent_keep(sent, rows)
    group = rows // queries
    same = lax.broadcasted_iota(jnp.int32, (rows, rows), 0) // group
    same = (same == lax.broadcasted_iota(jnp.int32, (rows, rows), 1) // group).astype(jnp.bfloat16)
    total = sum(dot32(part, same) for part in split(best))
    c = lax.broadcasted_iota(jnp.int32, total.shape, 0)
    scores[...] = jnp.where(c < passages, outer_scale * total, -jnp.inf)


def own_score_body(
    queries, passages, valid, hidden, projection, sent,
    unit_out, inverse_out, embed_out, turned_out, powers, totals, scores, log_out, tops,
):
    unit, inverse = unit_rows(dot32(hidden[...], projection[...]))
    unit_out[...] = unit
    inverse_out[...] = jnp.broadcast_to(inverse, unit.shape)
    embed = unit.astype(jnp.bfloat16)
    embed_out[...] = embed
    score_block(queries, passages, valid, embed_out, sent, powers, totals, scores, tops)
    log_out[...] = stack_rows(log_out.shape, (log_sum(scores[...]),))
    turned_out[...] = embed.T


def log_sum(scores):
    top = jnp.max(scores, axis=0, keepdims=True)
    return top + jnp.log(jnp.sum(jnp.exp(scores - top), axis=0, keepdims=True))


def log_add(parts):
    top = functools.reduce(jnp.maximum, parts)
    return top + jnp.log(sum(jnp.exp(part - top) for part in parts))


def stack_rows(shape, rows):
    index = lax.broadcasted_iota(jnp.int32, shape, 0)
    tile = jnp.zeros(shape, jnp.float32)
    for place, row in enumerate(rows):
        tile = jnp.where(index == place, row, tile)
    return tile


def fill_grad_sim(passages, coefficient, powers, out, column):
    tokens = powers.shape[0] // passages
    rows = powers.shape[1]
    for c in range(passages):
        part = slice(c * tokens, (c + 1) * tokens)
        out[part, column : column + rows] = (powers[part, :] * coefficient[c : c + 1, :]).astype(
            jnp.bfloat16
        )


def send_back(passages, turned, sent, powers, totals, scores, log, tail, back, grad_sim):
    dim, rows = turned.shape[0], powers.shape[1]
    dscore = loss_scale * jnp.exp(scores[...] - log)
    coefficient = outer_scale * dscore * sent_keep(sent, rows) / totals[...]
    fill_grad_sim(passages, coefficient, powers, grad_sim, 0)
    back[:dim, :] = dot32(turned[...], grad_sim[...]).astype(jnp.bfloat16)
    tail = stack_rows((ROWS, rows), [part.astype(jnp.float32) for part in tail])
    back[dim:, :] = tail.astype(jnp.bfloat16)


def far_score_body(
    queries, passages, valid, embed, turned, sent,
    powers, totals, scores, log_out, back, tops, grad_sim,
):
    score_block(queries, passages, valid, embed, sent, powers, totals, scores, tops)
    log = log_sum(scores[...])
    log_out[...] = stack_rows(log_out.shape, (log,))
    send_back(passages, turned, sent, powers, totals, scores, log, split(log), back, grad_sim)


def near_score_body(
    queries, passages, valid, embed, turned, sent, log0, log2, far0,
    powers, totals, scores, logs, back, tops, grad_sim,
):
    score_block(queries, passages, valid, embed, sent, powers, totals, scores, tops)
    log = log_sum(scores[...])
    other = log2[0:1, :]
    logs[...] = stack_rows(logs.shape, (log0[0:1, :], log, other, far0[0:1, :]))
    tail = split(log) + split(other)
    send_back(passages, turned, sent, powers, totals, scores, log, tail, back, grad_sim)


def joined(back, dim, place):
    tail = back[dim:, :].astype(jnp.float32)
    high, middle, low = [tail[i : i + 1, :] for i in range(place, place + 3)]
    return high + (middle + low)


def grad_body(
    queries, passages, pieces, wanted, query_hidden, passage_hidden, turned,
    query_unit, query_inverse, passage_unit, passage_inverse,
    powers0, powers1, powers2, totals0, totals1, totals2, scores0, scores1, scores2,
    sent0, sent1, sent2, logs, logs1, back1, back2, weight,
    losses, partial, query_out, passage_out,
    grad_sim, query_rows, pre_rows, query_grad, passage_grad, sems,
):
    rows = powers0.shape[1]
    dim = turned.shape[0]
    second, third = joined(back1, dim, 0), joined(back2, dim, 0)
    total0 = log_add((logs[0:1, :], second, third))
    total1 = log_add((logs1[0:1, :], logs[1:2, :], joined(back1, dim, 3)))
    total2 = log_add((logs[3:4, :], logs1[1:2, :], logs[2:3, :]))
    scores = scores0[...]
    onehot = lax.broadcasted_iota(jnp.int32, scores.shape, 0) == wanted[...]
    loss = total0 - jnp.sum(jnp.where(onehot, scores, 0.0), axis=0, keepdims=True)
    pick = lax.broadcasted_iota(jnp.int32, (rows, LANES), 1) * (rows // queries)
    pick = (pick == lax.broadcasted_iota(jnp.int32, (rows, LANES), 0)).astype(jnp.bfloat16)
    losses[...] = sum(dot32(part, pick) for part in split(loss))[:, :queries]

    for block, (total, query, powers, totals, scores) in enumerate((
        (total0, sent0, powers0, totals0, scores0),
        (total1, sent1, powers1, totals1, scores1),
        (total2, sent2, powers2, totals2, scores2),
    )):
        dscore = jnp.exp(scores[...] - total)
        if block == 0:
            dscore = dscore - onehot.astype(jnp.float32)
        coefficient = (outer_scale * loss_scale) * dscore * sent_keep(query, rows) / totals[...]
        fill_grad_sim(passages, coefficient, powers, grad_sim, block * rows)
        query_rows[block * rows : (block + 1) * rows, :] = query[:rows, :]

    size = passage_hidden.shape[0] // pieces
    copies = []
    for piece in range(pieces):
        part = pl.ds(piece * size, size)
        grad = dot32(grad_sim[part, :], query_rows[...])
        pre = back_rows(grad, passage_unit[part, :], passage_inverse[part, :])
        pre_rows[part, :] = pre
        passage_grad[part, :] = dot32(pre, weight[...], NT).astype(jnp.bfloat16)
        copies.append(
            pltpu.make_async_copy(passage_grad.at[part], passage_out.at[part], sems.at[piece])
        )
        copies[-1].start()
    to_query = dot32(turned[...], grad_sim[:, :rows])
    to_query += back1[:dim, :].astype(jnp.float32) * jnp.exp(second - total0)
    to_query += back2[:dim, :].astype(jnp.float32) * jnp.exp(third - total0)
    pre = back_rows(to_query.T, query_unit[...], query_inverse[...])
    query_grad[...] = dot32(pre, weight[...], NT).astype(jnp.bfloat16)
    copies.append(pltpu.make_async_copy(query_grad, query_out, sems.at[pieces]))
    copies[-1].start()
    both = dot32(pre.T, query_hidden[...])
    both += dot32(pre_rows[...].T, passage_hidden[...])
    partial[...] = both.T.astype(jnp.bfloat16)
    for copy in copies:
        copy.wait()


def sum_body(scale, copies, pieces, out):
    total = jnp.sum(pieces[...].astype(jnp.float32), axis=0) * scale
    total = total.astype(jnp.bfloat16)
    for copy in range(copies):
        out[copy] = total


def mean_over_devices(partial):
    axes = ("batch", "mp")
    devices = lax.axis_size("batch") * lax.axis_size("mp")
    rows, columns = partial.shape
    share = -(-rows // (devices * 8)) * 8
    padded = jnp.pad(partial, ((0, share * devices - rows), (0, 0)))
    pieces = lax.all_to_all(padded.reshape(devices, share, columns), axes, 0, 0)
    means = call(
        functools.partial(sum_body, 1.0 / devices, devices),
        (jax.ShapeDtypeStruct(pieces.shape, jnp.bfloat16),),
        (vmem,),
        (pieces,),
    )[0]
    whole = lax.all_to_all(means, axes, 0, 0)
    return whole.reshape(devices * share, columns)[:rows].astype(jnp.float32)


def per_device(query_hidden, passage_hidden, projection, query_lengths, passage_lengths, positives):
    queries = query_lengths.shape[0]
    passages = passage_lengths.shape[0]
    rows, width = query_hidden.shape
    slots = passage_hidden.shape[0]
    dim = projection.shape[1]
    f32, bf16 = jnp.float32, jnp.bfloat16
    of = jax.ShapeDtypeStruct
    pair = of((ROWS, rows), f32)
    pairs = pltpu.VMEM((ROWS, rows), f32)

    taken = (
        query_lengths, passage_lengths, positives, query_hidden, passage_hidden, projection
    )
    taken = tuple(pltpu.with_memory_space_constraint(x, pltpu.HBM) for x in taken)
    query_unit, query_inverse, sent0, valid, wanted, query_rows, passage_rows, weight = call(
        functools.partial(query_embed_body, queries),
        (
            of((rows, dim), f32), of((rows, dim), f32), of((rows + ROWS, dim), bf16),
            of((ROWS, rows), jnp.int32),
            of((1, rows), jnp.int32), of((rows, width), bf16), of((slots, width), bf16),
            of((width, dim), bf16),
        ),
        (hbm,) * 6,
        taken,
        scratch=(
            pltpu.SMEM((queries,), jnp.int32),
            pltpu.SMEM((passages,), jnp.int32),
            pltpu.SMEM((queries,), jnp.int32),
            pltpu.SemaphoreType.DMA((6,)),
        ),
        flops=2 * rows * width * dim,
    )
    sent1 = shifted(sent0, "batch", 1)
    sent2 = shifted(sent0, "batch", 2)
    (
        passage_unit, passage_inverse, embed, turned, powers0, totals0, scores0, log0
    ) = call(
        functools.partial(own_score_body, queries, passages),
        (
            of((slots, dim), f32), of((slots, dim), f32), of((slots, dim), bf16),
            of((dim, slots), bf16), of((slots, rows), f32), pair, pair, of((8, rows), f32),
        ),
        (vmem,) * 4,
        (valid, passage_rows, weight, sent0),
        scratch=(pairs,),
        flops=2 * slots * dim * (width + rows),
        trans=slots * rows,
    )
    far0 = shifted(log0, "batch", 2)
    block_outs = (
        of((slots, rows), f32), pair, pair, of((8, rows), f32), of((dim + ROWS, rows), bf16)
    )
    powers2, totals2, scores2, log2, back2 = call(
        functools.partial(far_score_body, queries, passages),
        block_outs,
        (vmem,) * 4,
        (valid, embed, turned, sent2),
        scratch=(pairs, pltpu.VMEM((slots, rows), bf16)),
        flops=4 * slots * dim * rows,
        trans=slots * rows,
    )
    back2 = shifted(back2, "batch", -2)
    powers1, totals1, scores1, logs, back1 = call(
        functools.partial(near_score_body, queries, passages),
        block_outs,
        (vmem,) * 7,
        (valid, embed, turned, sent1, log0, log2, far0),
        scratch=(pairs, pltpu.VMEM((slots, rows), bf16)),
        flops=4 * slots * dim * rows,
        trans=slots * rows,
    )
    back1 = shifted(back1, "batch", -1)
    logs1 = shifted(logs, "batch", 1)
    pieces = passages // 2 if passages % 2 == 0 else passages
    losses, partial, grad_query_hidden, grad_passage_hidden = call(
        functools.partial(grad_body, queries, passages, pieces),
        (
            of((1, queries), f32), of((width, dim), bf16),
            of((rows, width), bf16), of((slots, width), bf16),
        ),
        (vmem,) * 25,
        (wanted, query_rows, passage_rows, turned,
         query_unit, query_inverse, passage_unit, passage_inverse,
         powers0, powers1, powers2, totals0, totals1, totals2, scores0, scores1, scores2,
         sent0, sent1, sent2, logs, logs1, back1, back2, weight),
        scratch=(
            pltpu.VMEM((slots, 3 * rows), bf16),
            pltpu.VMEM((3 * rows, dim), bf16),
            pltpu.VMEM((slots, dim), bf16),
            pltpu.VMEM((rows, width), bf16),
            pltpu.VMEM((slots, width), bf16),
            pltpu.SemaphoreType.DMA((pieces + 1,)),
        ),
        flops=8 * slots * dim * rows + 4 * (slots + rows) * width * dim,
        out_specs=(vmem, vmem, hbm, hbm),
    )
    grad_projection = mean_over_devices(partial)
    losses = losses.reshape(queries)
    return (losses, grad_query_hidden, grad_passage_hidden, grad_projection)


def solution(mesh):
    in_specs = (
        P(("batch", "mp"), None),
        P(("batch", "mp"), None),
        P(),
        P(("batch", "mp")),
        P(("batch", "mp")),
        P(("batch", "mp")),
    )
    out_specs = (P(("batch", "mp")), P(("batch", "mp"), None), P(("batch", "mp"), None), P())
    return jax.shard_map(
        per_device, mesh=mesh, in_specs=in_specs, out_specs=out_specs, check_vma=False
    )
```

```python
import functools
import math

import jax
import jax.numpy as jnp
from jax import lax
from jax.experimental import pallas as pl
from jax.experimental.pallas import tpu as pltpu
from jax.sharding import PartitionSpec as P

inner_scale = 128.0
outer_scale = 8.0
loss_scale = 32.0
norm_eps = 1e-06

LANES = 128
ROWS = 16
LOG2E = 1.0 / math.log(2.0)
NT = (((1,), (1,)), ((), ()))

vmem = pl.BlockSpec(memory_space=pltpu.VMEM)
hbm = pl.BlockSpec(memory_space=pltpu.HBM)


def shifted(block, axis, distance):
    devices = range(lax.axis_size(axis))
    route = [((i - distance) % len(devices), i) for i in devices]
    return lax.ppermute(block, axis, route)


def dot32(left, right, dims=(((1,), (0,)), ((), ()))):
    return lax.dot_general(left, right, dims, preferred_element_type=jnp.float32)


def call(body, outs, in_specs, args, scratch=(), flops=0, trans=0):
    moved = sum(a.size * a.dtype.itemsize for a in args)
    moved += sum(math.prod(o.shape) * jnp.dtype(o.dtype).itemsize for o in outs)
    return pl.pallas_call(
        body,
        out_shape=tuple(outs),
        in_specs=list(in_specs),
        out_specs=tuple(vmem for _ in outs),
        scratch_shapes=list(scratch),
        compiler_params=pltpu.CompilerParams(vmem_limit_bytes=24 * 2**20),
        cost_estimate=pl.CostEstimate(flops=flops, bytes_accessed=moved, transcendentals=trans),
    )(*args)


def spread(values, count, group):
    lane = lax.broadcasted_iota(jnp.int32, (1, count * group), 1) // group
    row = jnp.zeros((1, count * group), jnp.int32)
    for item in range(count):
        row = jnp.where(lane == item, values[item], row)
    return row


def keep_row(lengths, queries, tokens):
    slot = lax.broadcasted_iota(jnp.int32, (1, queries * tokens), 1) % tokens
    return (slot < spread(lengths, queries, tokens)).astype(jnp.float32)


def unit_rows(before):
    inverse = lax.rsqrt(jnp.sum(before * before, axis=1, keepdims=True) + norm_eps)
    return before * inverse, inverse


def back_rows(grad, unit, inverse):
    inner = jnp.sum(unit * grad, axis=1, keepdims=True)
    return ((grad - unit * inner) * inverse).astype(jnp.bfloat16)


def load_all(pairs, sems):
    copies = [pltpu.make_async_copy(a, b, sems.at[i]) for i, (a, b) in enumerate(pairs)]
    for copy in copies:
        copy.start()
    return copies


def own_body(
    queries, query_lengths_in, passage_lengths_in, positives_in, query_hidden_in, passage_hidden_in,
    projection_in,
    query_unit_out, query_inverse_out, passage_unit_out, passage_inverse_out, sent_out, embed_out,
    turned_out, slots_out, wanted_out, powers, totals, scores, log_out,
    query_hidden, passage_hidden, projection,
    tops, query_lengths, passage_lengths, positives, sems,
):
    pairs = (
        (projection_in, projection), (query_hidden_in, query_hidden),
        (query_lengths_in, query_lengths), (positives_in, positives),
        (passage_lengths_in, passage_lengths), (passage_hidden_in, passage_hidden),
    )
    copies = load_all(pairs, sems)
    copies[0].wait()
    copies[1].wait()
    rows = query_hidden.shape[0]
    unit, inverse = unit_rows(dot32(query_hidden[...], projection[...]))
    query_unit_out[...] = unit
    query_inverse_out[...] = jnp.broadcast_to(inverse, unit.shape)
    sent_out[:rows, :] = unit.astype(jnp.bfloat16)
    copies[2].wait()
    keep = keep_row(query_lengths, queries, rows // queries)
    copies[3].wait()
    wanted_out[...] = spread(positives, queries, rows // queries)
    copies[4].wait()
    passages = passage_lengths.shape[0]
    c = lax.broadcasted_iota(jnp.int32, slots_out.shape, 0)
    valid = jnp.zeros(slots_out.shape, jnp.int32)
    for item in range(passages):
        valid = jnp.where(c == item, passage_lengths[item], valid)
    slots_out[...] = valid
    copies[5].wait()
    unit, inverse = unit_rows(dot32(passage_hidden[...], projection[...]))
    passage_unit_out[...] = unit
    passage_inverse_out[...] = jnp.broadcast_to(inverse, unit.shape)
    embed = unit.astype(jnp.bfloat16)
    embed_out[...] = embed
    score_block(
        queries, passages, slots_out, embed_out, sent_out, powers, totals, scores, tops, keep
    )
    log = log_sum(scores[...])
    log_out[...] = stack_rows(log_out.shape, (log,))
    lines = [keep] + [part.astype(jnp.float32) for part in split(log)]
    lines = [
        line[:, i * LANES : (i + 1) * LANES] for line in lines for i in range(rows // LANES)
    ]
    sent_out[rows:, :] = stack_rows((ROWS, LANES), lines).astype(jnp.bfloat16)
    turned_out[...] = embed.T


def sent_row(sent, rows, place):
    tail = sent[rows:, :].astype(jnp.float32)
    count = rows // LANES
    return jnp.concatenate(
        [tail[i : i + 1, :] for i in range(place * count, (place + 1) * count)], axis=1
    )


def sent_keep(sent, rows):
    return sent_row(sent, rows, 0)


def sent_log(sent, rows):
    return sent_row(sent, rows, 1) + (sent_row(sent, rows, 2) + sent_row(sent, rows, 3))


def split(values):
    high = values.astype(jnp.bfloat16)
    rest = values - high.astype(jnp.float32)
    middle = rest.astype(jnp.bfloat16)
    return high, middle, (rest - middle.astype(jnp.float32)).astype(jnp.bfloat16)


def score_block(queries, passages, valid, embed, sent, powers, totals, scores, tops, keep=None):
    rows = sent.shape[0] - ROWS
    tokens = embed.shape[0] // passages
    query = sent[:rows, :]
    half = tokens // 2
    slot = lax.broadcasted_iota(jnp.int32, (tokens - half, rows), 0) + half
    totals[...] = jnp.ones(totals.shape, jnp.float32)
    tops[...] = jnp.zeros(tops.shape, jnp.float32)
    powers[...] = dot32(embed[...], query, NT)
    for c in range(passages):
        sims = powers[c * tokens : (c + 1) * tokens, :]
        low, high = sims[:half], jnp.where(slot < valid[c : c + 1, :], sims[half:], -jnp.inf)
        top = jnp.maximum(
            jnp.max(low, axis=0, keepdims=True), jnp.max(high, axis=0, keepdims=True)
        )
        low = jnp.exp2((low - top) * (inner_scale * LOG2E))
        high = jnp.exp2((high - top) * (inner_scale * LOG2E))
        powers[c * tokens : c * tokens + half, :] = low
        powers[c * tokens + half : (c + 1) * tokens, :] = high
        tops[c : c + 1, :] = top
        totals[c : c + 1, :] = jnp.sum(low, axis=0, keepdims=True) + jnp.sum(
            high, axis=0, keepdims=True
        )
    best = tops[...] + jnp.log(totals[...]) / inner_scale
    best = best * (sent_keep(sent, rows) if keep is None else keep)
    group = rows // queries
    same = lax.broadcasted_iota(jnp.int32, (rows, rows), 0) // group
    same = (same == lax.broadcasted_iota(jnp.int32, (rows, rows), 1) // group).astype(jnp.bfloat16)
    total = sum(dot32(part, same) for part in split(best))
    c = lax.broadcasted_iota(jnp.int32, total.shape, 0)
    scores[...] = jnp.where(c < passages, outer_scale * total, -jnp.inf)


def log_sum(scores):
    top = jnp.max(scores, axis=0, keepdims=True)
    return top + jnp.log(jnp.sum(jnp.exp(scores - top), axis=0, keepdims=True))


def log_add(parts):
    top = functools.reduce(jnp.maximum, parts)
    return top + jnp.log(sum(jnp.exp(part - top) for part in parts))


def stack_rows(shape, rows):
    index = lax.broadcasted_iota(jnp.int32, shape, 0)
    tile = jnp.zeros(shape, jnp.float32)
    for place, row in enumerate(rows):
        tile = jnp.where(index == place, row, tile)
    return tile


def fill_grad_sim(passages, coefficient, powers, out, column):
    tokens = powers.shape[0] // passages
    rows = powers.shape[1]
    for c in range(passages):
        part = slice(c * tokens, (c + 1) * tokens)
        out[part, column : column + rows] = (powers[part, :] * coefficient[c : c + 1, :]).astype(
            jnp.bfloat16
        )


def send_back(passages, turned, sent, powers, totals, scores, log, tail, back, grad_sim):
    dim, rows = turned.shape[0], powers.shape[1]
    dscore = loss_scale * jnp.exp(scores[...] - log)
    coefficient = outer_scale * dscore * sent_keep(sent, rows) / totals[...]
    fill_grad_sim(passages, coefficient, powers, grad_sim, 0)
    back[:dim, :] = dot32(turned[...], grad_sim[...]).astype(jnp.bfloat16)
    tail = stack_rows((ROWS, rows), [part.astype(jnp.float32) for part in tail])
    back[dim:, :] = tail.astype(jnp.bfloat16)


def far_score_body(
    queries, passages, valid, embed, turned, sent,
    powers, totals, scores, log_out, back, tops, grad_sim,
):
    score_block(queries, passages, valid, embed, sent, powers, totals, scores, tops)
    log = log_sum(scores[...])
    log_out[...] = stack_rows(log_out.shape, (log,))
    send_back(passages, turned, sent, powers, totals, scores, log, split(log), back, grad_sim)


def near_score_body(
    queries, passages, valid, embed, turned, sent, log0, log2,
    powers, totals, scores, logs, back, tops, grad_sim,
):
    score_block(queries, passages, valid, embed, sent, powers, totals, scores, tops)
    log = log_sum(scores[...])
    other = log2[0:1, :]
    logs[...] = stack_rows(logs.shape, (log0[0:1, :], log, other))
    tail = split(log) + split(other)
    send_back(passages, turned, sent, powers, totals, scores, log, tail, back, grad_sim)


def joined(back, dim, place):
    tail = back[dim:, :].astype(jnp.float32)
    high, middle, low = [tail[i : i + 1, :] for i in range(place, place + 3)]
    return high + (middle + low)


def grad_body(
    queries, passages, wanted, query_hidden, passage_hidden, turned,
    query_unit, query_inverse, passage_unit, passage_inverse,
    powers0, powers1, powers2, totals0, totals1, totals2, scores0, scores1, scores2,
    sent0, sent1, sent2, logs, logs1, back1, back2,
    losses, query_pre_grad, passage_pre_grad, partial, grad_sim, query_rows,
):
    rows = powers0.shape[1]
    dim = turned.shape[0]
    second, third = joined(back1, dim, 0), joined(back2, dim, 0)
    total0 = log_add((logs[0:1, :], second, third))
    total1 = log_add((sent_log(sent1, rows), logs[1:2, :], joined(back1, dim, 3)))
    total2 = log_add((sent_log(sent2, rows), logs1[1:2, :], logs[2:3, :]))
    scores = scores0[...]
    onehot = lax.broadcasted_iota(jnp.int32, scores.shape, 0) == wanted[...]
    loss = total0 - jnp.sum(jnp.where(onehot, scores, 0.0), axis=0, keepdims=True)
    pick = lax.broadcasted_iota(jnp.int32, (rows, LANES), 1) * (rows // queries)
    pick = (pick == lax.broadcasted_iota(jnp.int32, (rows, LANES), 0)).astype(jnp.bfloat16)
    losses[...] = sum(dot32(part, pick) for part in split(loss))[:, :queries]

    for block, (total, query, powers, totals, scores) in enumerate((
        (total0, sent0, powers0, totals0, scores0),
        (total1, sent1, powers1, totals1, scores1),
        (total2, sent2, powers2, totals2, scores2),
    )):
        dscore = jnp.exp(scores[...] - total)
        if block == 0:
            dscore = dscore - onehot.astype(jnp.float32)
        coefficient = (outer_scale * loss_scale) * dscore * sent_keep(query, rows) / totals[...]
        fill_grad_sim(passages, coefficient, powers, grad_sim, block * rows)
        query_rows[block * rows : (block + 1) * rows, :] = query[:rows, :]

    grad = dot32(grad_sim[...], query_rows[...])
    pre = back_rows(grad, passage_unit[...], passage_inverse[...])
    passage_pre_grad[...] = pre
    both = dot32(pre.T, passage_hidden[...])
    to_query = dot32(turned[...], grad_sim[:, :rows])
    to_query += back1[:dim, :].astype(jnp.float32) * jnp.exp(second - total0)
    to_query += back2[:dim, :].astype(jnp.float32) * jnp.exp(third - total0)
    pre = back_rows(to_query.T, query_unit[...], query_inverse[...])
    query_pre_grad[...] = pre
    both += dot32(pre.T, query_hidden[...])
    partial[...] = both.T.astype(jnp.bfloat16)


def sum_body(scale, copies, pieces, out):
    total = jnp.sum(pieces[...].astype(jnp.float32), axis=0) * scale
    total = total.astype(jnp.bfloat16)
    for copy in range(copies):
        out[copy] = total


def mean_over_devices(partial):
    axes = ("batch", "mp")
    devices = lax.axis_size("batch") * lax.axis_size("mp")
    rows, columns = partial.shape
    share = -(-rows // (devices * 8)) * 8
    padded = jnp.pad(partial, ((0, share * devices - rows), (0, 0)))
    pieces = lax.all_to_all(padded.reshape(devices, share, columns), axes, 0, 0)
    means = call(
        functools.partial(sum_body, 1.0 / devices, devices),
        (jax.ShapeDtypeStruct(pieces.shape, jnp.bfloat16),),
        (vmem,),
        (pieces,),
    )[0]
    whole = lax.all_to_all(means, axes, 0, 0)
    return whole.reshape(devices * share, columns)[:rows].astype(jnp.float32)


def per_device(query_hidden, passage_hidden, projection, query_lengths, passage_lengths, positives):
    queries = query_lengths.shape[0]
    passages = passage_lengths.shape[0]
    rows, width = query_hidden.shape
    slots = passage_hidden.shape[0]
    dim = projection.shape[1]
    f32, bf16 = jnp.float32, jnp.bfloat16
    of = jax.ShapeDtypeStruct
    pair = of((ROWS, rows), f32)
    pairs = pltpu.VMEM((ROWS, rows), f32)

    taken = (
        query_lengths, passage_lengths, positives, query_hidden, passage_hidden, projection
    )
    taken = tuple(pltpu.with_memory_space_constraint(x, pltpu.HBM) for x in taken)
    (
        query_unit, query_inverse, passage_unit, passage_inverse, sent0, embed, turned,
        valid, wanted, powers0, totals0, scores0, log0, query_rows, passage_rows, weight,
    ) = call(
        functools.partial(own_body, queries),
        (
            of((rows, dim), f32), of((rows, dim), f32), of((slots, dim), f32),
            of((slots, dim), f32), of((rows + ROWS, dim), bf16), of((slots, dim), bf16),
            of((dim, slots), bf16), of((ROWS, rows), jnp.int32), of((1, rows), jnp.int32),
            of((slots, rows), f32), pair, pair, of((8, rows), f32),
            of((rows, width), bf16), of((slots, width), bf16), of((width, dim), bf16),
        ),
        (hbm,) * 6,
        taken,
        scratch=(
            pairs,
            pltpu.SMEM((queries,), jnp.int32),
            pltpu.SMEM((passages,), jnp.int32),
            pltpu.SMEM((queries,), jnp.int32),
            pltpu.SemaphoreType.DMA((6,)),
        ),
        flops=2 * (slots + rows) * width * dim + 2 * slots * rows * dim,
        trans=slots * rows,
    )
    sent1 = shifted(sent0, "batch", 1)
    sent2 = shifted(sent0, "batch", 2)
    block_outs = (
        of((slots, rows), f32), pair, pair, of((8, rows), f32), of((dim + ROWS, rows), bf16)
    )
    powers2, totals2, scores2, log2, back2 = call(
        functools.partial(far_score_body, queries, passages),
        block_outs,
        (vmem,) * 4,
        (valid, embed, turned, sent2),
        scratch=(pairs, pltpu.VMEM((slots, rows), bf16)),
        flops=4 * slots * dim * rows,
        trans=slots * rows,
    )
    back2 = shifted(back2, "batch", -2)
    powers1, totals1, scores1, logs, back1 = call(
        functools.partial(near_score_body, queries, passages),
        block_outs,
        (vmem,) * 6,
        (valid, embed, turned, sent1, log0, log2),
        scratch=(pairs, pltpu.VMEM((slots, rows), bf16)),
        flops=4 * slots * dim * rows,
        trans=slots * rows,
    )
    back1 = shifted(back1, "batch", -1)
    logs1 = shifted(logs, "batch", 1)
    losses, query_pre_grad, passage_pre_grad, partial = call(
        functools.partial(grad_body, queries, passages),
        (
            of((1, queries), f32), of((rows, dim), bf16), of((slots, dim), bf16),
            of((width, dim), bf16),
        ),
        (vmem,) * 24,
        (wanted, query_rows, passage_rows, turned,
         query_unit, query_inverse, passage_unit, passage_inverse,
         powers0, powers1, powers2, totals0, totals1, totals2, scores0, scores1, scores2,
         sent0, sent1, sent2, logs, logs1, back1, back2),
        scratch=(pltpu.VMEM((slots, 3 * rows), bf16), pltpu.VMEM((3 * rows, dim), bf16)),
        flops=8 * slots * dim * rows + 2 * (slots + rows) * width * dim,
    )
    grad_projection = mean_over_devices(partial)
    grad_query_hidden = dot32(query_pre_grad, weight, NT).astype(bf16)
    grad_passage_hidden = dot32(passage_pre_grad, weight, NT).astype(bf16)
    losses = losses.reshape(queries)
    return (losses, grad_query_hidden, grad_passage_hidden, grad_projection)


def solution(mesh):
    in_specs = (
        P(("batch", "mp"), None),
        P(("batch", "mp"), None),
        P(),
        P(("batch", "mp")),
        P(("batch", "mp")),
        P(("batch", "mp")),
    )
    out_specs = (P(("batch", "mp")), P(("batch", "mp"), None), P(("batch", "mp"), None), P())
    return jax.shard_map(
        per_device, mesh=mesh, in_specs=in_specs, out_specs=out_specs, check_vma=False
    )
```

```python
import functools
import math

import jax
import jax.numpy as jnp
from jax import lax
from jax.experimental import pallas as pl
from jax.experimental.pallas import tpu as pltpu
from jax.sharding import PartitionSpec as P

inner_scale = 128.0
outer_scale = 8.0
loss_scale = 32.0
norm_eps = 1e-06

LANES = 128
ROWS = 16
LOG2E = 1.0 / math.log(2.0)
NT = (((1,), (1,)), ((), ()))

vmem = pl.BlockSpec(memory_space=pltpu.VMEM)
hbm = pl.BlockSpec(memory_space=pltpu.HBM)


def shifted(block, axis, distance):
    devices = range(lax.axis_size(axis))
    route = [((i - distance) % len(devices), i) for i in devices]
    return lax.ppermute(block, axis, route)


def dot32(left, right, dims=(((1,), (0,)), ((), ()))):
    return lax.dot_general(left, right, dims, preferred_element_type=jnp.float32)


def call(body, outs, in_specs, args, scratch=(), flops=0, trans=0):
    moved = sum(a.size * a.dtype.itemsize for a in args)
    moved += sum(math.prod(o.shape) * jnp.dtype(o.dtype).itemsize for o in outs)
    return pl.pallas_call(
        body,
        out_shape=tuple(outs),
        in_specs=list(in_specs),
        out_specs=tuple(vmem for _ in outs),
        scratch_shapes=list(scratch),
        compiler_params=pltpu.CompilerParams(vmem_limit_bytes=24 * 2**20),
        cost_estimate=pl.CostEstimate(flops=flops, bytes_accessed=moved, transcendentals=trans),
    )(*args)


def spread(values, count, group):
    lane = lax.broadcasted_iota(jnp.int32, (1, count * group), 1) // group
    row = jnp.zeros((1, count * group), jnp.int32)
    for item in range(count):
        row = jnp.where(lane == item, values[item], row)
    return row


def keep_row(lengths, queries, tokens):
    slot = lax.broadcasted_iota(jnp.int32, (1, queries * tokens), 1) % tokens
    return (slot < spread(lengths, queries, tokens)).astype(jnp.float32)


def unit_rows(before):
    inverse = lax.rsqrt(jnp.sum(before * before, axis=1, keepdims=True) + norm_eps)
    return before * inverse, inverse


def back_rows(grad, unit, inverse):
    inner = jnp.sum(unit * grad, axis=1, keepdims=True)
    return ((grad - unit * inner) * inverse).astype(jnp.bfloat16)


def load_all(pairs, sems):
    copies = [pltpu.make_async_copy(a, b, sems.at[i]) for i, (a, b) in enumerate(pairs)]
    for copy in copies:
        copy.start()
    return copies


def query_embed_body(
    queries, query_lengths_in, passage_lengths_in, positives_in, query_hidden_in, passage_hidden_in,
    projection_in,
    unit_out, inverse_out, sent_out, slots_out, wanted_out, query_hidden, passage_hidden, projection,
    query_lengths, passage_lengths, positives, sems,
):
    pairs = (
        (projection_in, projection), (query_hidden_in, query_hidden),
        (query_lengths_in, query_lengths), (positives_in, positives),
        (passage_lengths_in, passage_lengths), (passage_hidden_in, passage_hidden),
    )
    copies = load_all(pairs, sems)
    copies[0].wait()
    copies[1].wait()
    rows = query_hidden.shape[0]
    before = dot32(query_hidden[...], projection[...])
    unit, inverse = unit_rows(before)
    unit_out[...] = unit
    inverse_out[...] = jnp.broadcast_to(inverse, unit.shape)
    sent_out[:rows, :] = unit.astype(jnp.bfloat16)
    copies[2].wait()
    keep = keep_row(query_lengths, queries, rows // queries)
    row = lax.broadcasted_iota(jnp.int32, (ROWS, LANES), 0)
    tail = jnp.zeros((ROWS, LANES), jnp.float32)
    for piece in range(rows // LANES):
        tail = jnp.where(row == piece, keep[:, piece * LANES : (piece + 1) * LANES], tail)
    sent_out[rows:, :] = tail.astype(jnp.bfloat16)
    copies[3].wait()
    wanted_out[...] = spread(positives, queries, rows // queries)
    copies[4].wait()
    c = lax.broadcasted_iota(jnp.int32, slots_out.shape, 0)
    valid = jnp.zeros(slots_out.shape, jnp.int32)
    for item in range(passage_lengths.shape[0]):
        valid = jnp.where(c == item, passage_lengths[item], valid)
    slots_out[...] = valid
    copies[5].wait()


def sent_keep(sent, rows):
    tail = sent[rows:, :].astype(jnp.float32)
    return jnp.concatenate([tail[i : i + 1, :] for i in range(rows // LANES)], axis=1)


def split(values):
    high = values.astype(jnp.bfloat16)
    rest = values - high.astype(jnp.float32)
    middle = rest.astype(jnp.bfloat16)
    return high, middle, (rest - middle.astype(jnp.float32)).astype(jnp.bfloat16)


def score_block(queries, passages, valid, embed, sent, powers, totals, scores, tops):
    rows = sent.shape[0] - ROWS
    tokens = embed.shape[0] // passages
    query = sent[:rows, :]
    half = tokens // 2
    slot = lax.broadcasted_iota(jnp.int32, (tokens - half, rows), 0) + half
    totals[...] = jnp.ones(totals.shape, jnp.float32)
    tops[...] = jnp.zeros(tops.shape, jnp.float32)
    for c in range(passages):
        sims = dot32(embed[c * tokens : (c + 1) * tokens, :], query, NT)
        low, high = sims[:half], jnp.where(slot < valid[c : c + 1, :], sims[half:], -jnp.inf)
        top = jnp.maximum(
            jnp.max(low, axis=0, keepdims=True), jnp.max(high, axis=0, keepdims=True)
        )
        low = jnp.exp2((low - top) * (inner_scale * LOG2E))
        high = jnp.exp2((high - top) * (inner_scale * LOG2E))
        powers[c * tokens : c * tokens + half, :] = low
        powers[c * tokens + half : (c + 1) * tokens, :] = high
        tops[c : c + 1, :] = top
        totals[c : c + 1, :] = jnp.sum(low, axis=0, keepdims=True) + jnp.sum(
            high, axis=0, keepdims=True
        )
    best = tops[...] + jnp.log(totals[...]) / inner_scale
    best = best * sent_keep(sent, rows)
    group = rows // queries
    same = lax.broadcasted_iota(jnp.int32, (rows, rows), 0) // group
    same = (same == lax.broadcasted_iota(jnp.int32, (rows, rows), 1) // group).astype(jnp.bfloat16)
    total = sum(dot32(part, same) for part in split(best))
    c = lax.broadcasted_iota(jnp.int32, total.shape, 0)
    scores[...] = jnp.where(c < passages, outer_scale * total, -jnp.inf)


def own_score_body(
    queries, passages, valid, hidden, projection, sent,
    unit_out, inverse_out, embed_out, turned_out, powers, totals, scores, log_out, tops,
):
    unit, inverse = unit_rows(dot32(hidden[...], projection[...]))
    unit_out[...] = unit
    inverse_out[...] = jnp.broadcast_to(inverse, unit.shape)
    embed = unit.astype(jnp.bfloat16)
    embed_out[...] = embed
    score_block(queries, passages, valid, embed_out, sent, powers, totals, scores, tops)
    log_out[...] = stack_rows(log_out.shape, (log_sum(scores[...]),))
    turned_out[...] = embed.T


def log_sum(scores):
    top = jnp.max(scores, axis=0, keepdims=True)
    return top + jnp.log(jnp.sum(jnp.exp(scores - top), axis=0, keepdims=True))


def log_add(parts):
    top = functools.reduce(jnp.maximum, parts)
    return top + jnp.log(sum(jnp.exp(part - top) for part in parts))


def stack_rows(shape, rows):
    index = lax.broadcasted_iota(jnp.int32, shape, 0)
    tile = jnp.zeros(shape, jnp.float32)
    for place, row in enumerate(rows):
        tile = jnp.where(index == place, row, tile)
    return tile


def fill_grad_sim(passages, coefficient, powers, out, column):
    tokens = powers.shape[0] // passages
    rows = powers.shape[1]
    for c in range(passages):
        part = slice(c * tokens, (c + 1) * tokens)
        out[part, column : column + rows] = (powers[part, :] * coefficient[c : c + 1, :]).astype(
            jnp.bfloat16
        )


def send_back(passages, turned, sent, powers, totals, scores, log, tail, back, grad_sim):
    dim, rows = turned.shape[0], powers.shape[1]
    dscore = loss_scale * jnp.exp(scores[...] - log)
    coefficient = outer_scale * dscore * sent_keep(sent, rows) / totals[...]
    fill_grad_sim(passages, coefficient, powers, grad_sim, 0)
    back[:dim, :] = dot32(turned[...], grad_sim[...]).astype(jnp.bfloat16)
    tail = stack_rows((ROWS, rows), [part.astype(jnp.float32) for part in tail])
    back[dim:, :] = tail.astype(jnp.bfloat16)


def far_score_body(
    queries, passages, valid, embed, turned, sent,
    powers, totals, scores, log_out, back, tops, grad_sim,
):
    score_block(queries, passages, valid, embed, sent, powers, totals, scores, tops)
    log = log_sum(scores[...])
    log_out[...] = stack_rows(log_out.shape, (log,))
    send_back(passages, turned, sent, powers, totals, scores, log, split(log), back, grad_sim)


def near_score_body(
    queries, passages, valid, embed, sent, log0, log2, powers, totals, scores, logs, tops
):
    score_block(queries, passages, valid, embed, sent, powers, totals, scores, tops)
    log = log_sum(scores[...])
    logs[...] = stack_rows(logs.shape, (log0[0:1, :], log, log2[0:1, :]))


def near_grad_body(passages, turned, sent, powers, totals, scores, logs, back, grad_sim):
    log = logs[1:2, :]
    tail = split(log) + split(logs[2:3, :])
    send_back(passages, turned, sent, powers, totals, scores, log, tail, back, grad_sim)


def joined(back, dim, place):
    tail = back[dim:, :].astype(jnp.float32)
    high, middle, low = [tail[i : i + 1, :] for i in range(place, place + 3)]
    return high + (middle + low)


def far_passage_body(
    passages, powers, totals, scores, sent, logs, logs1, far0, back2, grad, partial, grad_sim
):
    rows = powers.shape[1]
    third = joined(back2, grad.shape[1], 0)
    partial[...] = stack_rows(partial.shape, (log_add((logs[0:1, :], third)), third))
    total = log_add((far0[0:1, :], logs1[1:2, :], logs[2:3, :]))
    dscore = loss_scale * jnp.exp(scores[...] - total)
    coefficient = outer_scale * dscore * sent_keep(sent, rows) / totals[...]
    fill_grad_sim(passages, coefficient, powers, grad_sim, 0)
    grad[...] = dot32(grad_sim[...], sent[:rows, :])


def grad_body(
    queries, passages, wanted, query_hidden, passage_hidden, turned,
    query_unit, query_inverse, passage_unit, passage_inverse,
    powers0, powers1, totals0, totals1, scores0, scores1, sent0, sent1, far_grad,
    two_logs, logs, logs1, back1, back2,
    losses, query_pre_grad, passage_pre_grad, partial, grad_sim, query_rows,
):
    rows = powers0.shape[1]
    dim = turned.shape[0]
    second, third = joined(back1, dim, 0), two_logs[1:2, :]
    total0 = log_add((two_logs[0:1, :], second))
    total1 = log_add((logs1[0:1, :], logs[1:2, :], joined(back1, dim, 3)))
    scores = scores0[...]
    onehot = lax.broadcasted_iota(jnp.int32, scores.shape, 0) == wanted[...]
    loss = total0 - jnp.sum(jnp.where(onehot, scores, 0.0), axis=0, keepdims=True)
    pick = lax.broadcasted_iota(jnp.int32, (rows, LANES), 1) * (rows // queries)
    pick = (pick == lax.broadcasted_iota(jnp.int32, (rows, LANES), 0)).astype(jnp.bfloat16)
    losses[...] = sum(dot32(part, pick) for part in split(loss))[:, :queries]

    for block, (total, query, powers, totals, scores) in enumerate((
        (total0, sent0, powers0, totals0, scores0),
        (total1, sent1, powers1, totals1, scores1),
    )):
        dscore = jnp.exp(scores[...] - total)
        if block == 0:
            dscore = dscore - onehot.astype(jnp.float32)
        coefficient = (outer_scale * loss_scale) * dscore * sent_keep(query, rows) / totals[...]
        fill_grad_sim(passages, coefficient, powers, grad_sim, block * rows)
        query_rows[block * rows : (block + 1) * rows, :] = query[:rows, :]

    grad = far_grad[...] + dot32(grad_sim[...], query_rows[...])
    pre = back_rows(grad, passage_unit[...], passage_inverse[...])
    passage_pre_grad[...] = pre
    both = dot32(pre.T, passage_hidden[...])
    to_query = dot32(turned[...], grad_sim[:, :rows])
    to_query += back1[:dim, :].astype(jnp.float32) * jnp.exp(second - total0)
    to_query += back2[:dim, :].astype(jnp.float32) * jnp.exp(third - total0)
    pre = back_rows(to_query.T, query_unit[...], query_inverse[...])
    query_pre_grad[...] = pre
    both += dot32(pre.T, query_hidden[...])
    partial[...] = both.T.astype(jnp.bfloat16)


def sum_body(scale, copies, pieces, out):
    total = jnp.sum(pieces[...].astype(jnp.float32), axis=0) * scale
    total = total.astype(jnp.bfloat16)
    for copy in range(copies):
        out[copy] = total


def mean_over_devices(partial):
    axes = ("batch", "mp")
    devices = lax.axis_size("batch") * lax.axis_size("mp")
    rows, columns = partial.shape
    share = -(-rows // (devices * 8)) * 8
    padded = jnp.pad(partial, ((0, share * devices - rows), (0, 0)))
    pieces = lax.all_to_all(padded.reshape(devices, share, columns), axes, 0, 0)
    means = call(
        functools.partial(sum_body, 1.0 / devices, devices),
        (jax.ShapeDtypeStruct(pieces.shape, jnp.bfloat16),),
        (vmem,),
        (pieces,),
    )[0]
    whole = lax.all_to_all(means, axes, 0, 0)
    return whole.reshape(devices * share, columns)[:rows].astype(jnp.float32)


def per_device(query_hidden, passage_hidden, projection, query_lengths, passage_lengths, positives):
    queries = query_lengths.shape[0]
    passages = passage_lengths.shape[0]
    rows, width = query_hidden.shape
    slots = passage_hidden.shape[0]
    dim = projection.shape[1]
    f32, bf16 = jnp.float32, jnp.bfloat16
    of = jax.ShapeDtypeStruct
    pair = of((ROWS, rows), f32)
    pairs = pltpu.VMEM((ROWS, rows), f32)

    taken = (
        query_lengths, passage_lengths, positives, query_hidden, passage_hidden, projection
    )
    taken = tuple(pltpu.with_memory_space_constraint(x, pltpu.HBM) for x in taken)
    query_unit, query_inverse, sent0, valid, wanted, query_rows, passage_rows, weight = call(
        functools.partial(query_embed_body, queries),
        (
            of((rows, dim), f32), of((rows, dim), f32), of((rows + ROWS, dim), bf16),
            of((ROWS, rows), jnp.int32),
            of((1, rows), jnp.int32), of((rows, width), bf16), of((slots, width), bf16),
            of((width, dim), bf16),
        ),
        (hbm,) * 6,
        taken,
        scratch=(
            pltpu.SMEM((queries,), jnp.int32),
            pltpu.SMEM((passages,), jnp.int32),
            pltpu.SMEM((queries,), jnp.int32),
            pltpu.SemaphoreType.DMA((6,)),
        ),
        flops=2 * rows * width * dim,
    )
    sent1 = shifted(sent0, "batch", 1)
    sent2 = shifted(sent0, "batch", 2)
    (
        passage_unit, passage_inverse, embed, turned, powers0, totals0, scores0, log0
    ) = call(
        functools.partial(own_score_body, queries, passages),
        (
            of((slots, dim), f32), of((slots, dim), f32), of((slots, dim), bf16),
            of((dim, slots), bf16), of((slots, rows), f32), pair, pair, of((8, rows), f32),
        ),
        (vmem,) * 4,
        (valid, passage_rows, weight, sent0),
        scratch=(pairs,),
        flops=2 * slots * dim * (width + rows),
        trans=slots * rows,
    )
    far0 = shifted(log0, "batch", 2)
    block_outs = (
        of((slots, rows), f32), pair, pair, of((8, rows), f32), of((dim + ROWS, rows), bf16)
    )
    powers2, totals2, scores2, log2, back2 = call(
        functools.partial(far_score_body, queries, passages),
        block_outs,
        (vmem,) * 4,
        (valid, embed, turned, sent2),
        scratch=(pairs, pltpu.VMEM((slots, rows), bf16)),
        flops=4 * slots * dim * rows,
        trans=slots * rows,
    )
    back2 = shifted(back2, "batch", -2)
    powers1, totals1, scores1, logs = call(
        functools.partial(near_score_body, queries, passages),
        block_outs[:4],
        (vmem,) * 5,
        (valid, embed, sent1, log0, log2),
        scratch=(pairs,),
        flops=2 * slots * dim * rows,
        trans=slots * rows,
    )
    logs1 = shifted(logs, "batch", 1)
    back1 = call(
        functools.partial(near_grad_body, passages),
        block_outs[4:],
        (vmem,) * 6,
        (turned, sent1, powers1, totals1, scores1, logs),
        scratch=(pltpu.VMEM((slots, rows), bf16),),
        flops=2 * slots * dim * rows,
    )[0]
    back1 = shifted(back1, "batch", -1)
    far_grad, two_logs = call(
        functools.partial(far_passage_body, passages),
        (of((slots, dim), f32), of((8, rows), f32)),
        (vmem,) * 8,
        (powers2, totals2, scores2, sent2, logs, logs1, far0, back2),
        scratch=(pltpu.VMEM((slots, rows), bf16),),
        flops=20 * slots * dim * rows,
    )
    losses, query_pre_grad, passage_pre_grad, partial = call(
        functools.partial(grad_body, queries, passages),
        (
            of((1, queries), f32), of((rows, dim), bf16), of((slots, dim), bf16),
            of((width, dim), bf16),
        ),
        (vmem,) * 22,
        (wanted, query_rows, passage_rows, turned,
         query_unit, query_inverse, passage_unit, passage_inverse,
         powers0, powers1, totals0, totals1, scores0, scores1, sent0, sent1, far_grad,
         two_logs, logs, logs1, back1, back2),
        scratch=(pltpu.VMEM((slots, 2 * rows), bf16), pltpu.VMEM((2 * rows, dim), bf16)),
        flops=6 * slots * dim * rows + 2 * (slots + rows) * width * dim,
    )
    grad_projection = mean_over_devices(partial)
    grad_query_hidden = dot32(query_pre_grad, weight, NT).astype(bf16)
    grad_passage_hidden = dot32(passage_pre_grad, weight, NT).astype(bf16)
    losses = losses.reshape(queries)
    return (losses, grad_query_hidden, grad_passage_hidden, grad_projection)


def solution(mesh):
    in_specs = (
        P(("batch", "mp"), None),
        P(("batch", "mp"), None),
        P(),
        P(("batch", "mp")),
        P(("batch", "mp")),
        P(("batch", "mp")),
    )
    out_specs = (P(("batch", "mp")), P(("batch", "mp"), None), P(("batch", "mp"), None), P())
    return jax.shard_map(
        per_device, mesh=mesh, in_specs=in_specs, out_specs=out_specs, check_vma=False
    )
```

```python
import functools
import math

import jax
import jax.numpy as jnp
from jax import lax
from jax.experimental import pallas as pl
from jax.experimental.pallas import tpu as pltpu
from jax.sharding import PartitionSpec as P

inner_scale = 128.0
outer_scale = 8.0
loss_scale = 32.0
norm_eps = 1e-06

LANES = 128
ROWS = 16
LOG2E = 1.0 / math.log(2.0)
NT = (((1,), (1,)), ((), ()))

vmem = pl.BlockSpec(memory_space=pltpu.VMEM)
hbm = pl.BlockSpec(memory_space=pltpu.HBM)


def shifted(block, axis, distance):
    devices = range(lax.axis_size(axis))
    route = [((i - distance) % len(devices), i) for i in devices]
    return lax.ppermute(block, axis, route)


def dot32(left, right, dims=(((1,), (0,)), ((), ()))):
    return lax.dot_general(left, right, dims, preferred_element_type=jnp.float32)


def call(body, outs, in_specs, args, scratch=(), flops=0, trans=0):
    moved = sum(a.size * a.dtype.itemsize for a in args)
    moved += sum(math.prod(o.shape) * jnp.dtype(o.dtype).itemsize for o in outs)
    return pl.pallas_call(
        body,
        out_shape=tuple(outs),
        in_specs=list(in_specs),
        out_specs=tuple(vmem for _ in outs),
        scratch_shapes=list(scratch),
        compiler_params=pltpu.CompilerParams(vmem_limit_bytes=24 * 2**20),
        cost_estimate=pl.CostEstimate(flops=flops, bytes_accessed=moved, transcendentals=trans),
    )(*args)


def spread(values, count, group):
    lane = lax.broadcasted_iota(jnp.int32, (1, count * group), 1) // group
    row = jnp.zeros((1, count * group), jnp.int32)
    for item in range(count):
        row = jnp.where(lane == item, values[item], row)
    return row


def keep_row(lengths, queries, tokens):
    slot = lax.broadcasted_iota(jnp.int32, (1, queries * tokens), 1) % tokens
    return (slot < spread(lengths, queries, tokens)).astype(jnp.float32)


def unit_rows(before):
    inverse = lax.rsqrt(jnp.sum(before * before, axis=1, keepdims=True) + norm_eps)
    return before * inverse, inverse


def back_rows(grad, unit, inverse):
    inner = jnp.sum(unit * grad, axis=1, keepdims=True)
    return ((grad - unit * inner) * inverse).astype(jnp.bfloat16)


def load_all(pairs, sems):
    copies = [pltpu.make_async_copy(a, b, sems.at[i]) for i, (a, b) in enumerate(pairs)]
    for copy in copies:
        copy.start()
    return copies


def query_embed_body(
    queries, query_lengths_in, passage_lengths_in, positives_in, query_hidden_in, passage_hidden_in,
    projection_in,
    unit_out, inverse_out, sent_out, slots_out, wanted_out, query_hidden, passage_hidden, projection,
    query_lengths, passage_lengths, positives, sems,
):
    pairs = (
        (projection_in, projection), (query_hidden_in, query_hidden),
        (query_lengths_in, query_lengths), (positives_in, positives),
        (passage_lengths_in, passage_lengths), (passage_hidden_in, passage_hidden),
    )
    copies = load_all(pairs, sems)
    copies[0].wait()
    copies[1].wait()
    rows = query_hidden.shape[0]
    before = dot32(query_hidden[...], projection[...])
    unit, inverse = unit_rows(before)
    unit_out[...] = unit
    inverse_out[...] = jnp.broadcast_to(inverse, unit.shape)
    sent_out[:rows, :] = unit.astype(jnp.bfloat16)
    copies[2].wait()
    keep = keep_row(query_lengths, queries, rows // queries)
    row = lax.broadcasted_iota(jnp.int32, (ROWS, LANES), 0)
    tail = jnp.zeros((ROWS, LANES), jnp.float32)
    for piece in range(rows // LANES):
        tail = jnp.where(row == piece, keep[:, piece * LANES : (piece + 1) * LANES], tail)
    sent_out[rows:, :] = tail.astype(jnp.bfloat16)
    copies[3].wait()
    wanted_out[...] = spread(positives, queries, rows // queries)
    copies[4].wait()
    c = lax.broadcasted_iota(jnp.int32, slots_out.shape, 0)
    valid = jnp.zeros(slots_out.shape, jnp.int32)
    for item in range(passage_lengths.shape[0]):
        valid = jnp.where(c == item, passage_lengths[item], valid)
    slots_out[...] = valid
    copies[5].wait()


def sent_keep(sent, rows):
    tail = sent[rows:, :].astype(jnp.float32)
    return jnp.concatenate([tail[i : i + 1, :] for i in range(rows // LANES)], axis=1)


def split(values):
    high = values.astype(jnp.bfloat16)
    rest = values - high.astype(jnp.float32)
    middle = rest.astype(jnp.bfloat16)
    return high, middle, (rest - middle.astype(jnp.float32)).astype(jnp.bfloat16)


def score_block(queries, passages, valid, embed, sent, powers, totals, scores, tops):
    rows = sent.shape[0] - ROWS
    tokens = embed.shape[0] // passages
    query = sent[:rows, :]
    half = tokens // 2
    slot = lax.broadcasted_iota(jnp.int32, (tokens - half, rows), 0) + half
    totals[...] = jnp.ones(totals.shape, jnp.float32)
    tops[...] = jnp.zeros(tops.shape, jnp.float32)
    for c in range(passages):
        sims = dot32(embed[c * tokens : (c + 1) * tokens, :], query, NT)
        low, high = sims[:half], jnp.where(slot < valid[c : c + 1, :], sims[half:], -jnp.inf)
        top = jnp.maximum(
            jnp.max(low, axis=0, keepdims=True), jnp.max(high, axis=0, keepdims=True)
        )
        low = jnp.exp2((low - top) * (inner_scale * LOG2E))
        high = jnp.exp2((high - top) * (inner_scale * LOG2E))
        powers[c * tokens : c * tokens + half, :] = low
        powers[c * tokens + half : (c + 1) * tokens, :] = high
        tops[c : c + 1, :] = top
        totals[c : c + 1, :] = jnp.sum(low, axis=0, keepdims=True) + jnp.sum(
            high, axis=0, keepdims=True
        )
    best = tops[...] + jnp.log(totals[...]) / inner_scale
    best = best * sent_keep(sent, rows)
    group = rows // queries
    same = lax.broadcasted_iota(jnp.int32, (rows, rows), 0) // group
    same = (same == lax.broadcasted_iota(jnp.int32, (rows, rows), 1) // group).astype(jnp.bfloat16)
    total = sum(dot32(part, same) for part in split(best))
    c = lax.broadcasted_iota(jnp.int32, total.shape, 0)
    scores[...] = jnp.where(c < passages, outer_scale * total, -jnp.inf)


def own_score_body(
    queries, passages, valid, hidden, projection, sent,
    unit_out, inverse_out, embed_out, turned_out, powers, totals, scores, log_out, tops,
):
    unit, inverse = unit_rows(dot32(hidden[...], projection[...]))
    unit_out[...] = unit
    inverse_out[...] = jnp.broadcast_to(inverse, unit.shape)
    embed = unit.astype(jnp.bfloat16)
    embed_out[...] = embed
    score_block(queries, passages, valid, embed_out, sent, powers, totals, scores, tops)
    log_out[...] = stack_rows(log_out.shape, (log_sum(scores[...]),))
    turned_out[...] = embed.T


def log_sum(scores):
    top = jnp.max(scores, axis=0, keepdims=True)
    return top + jnp.log(jnp.sum(jnp.exp(scores - top), axis=0, keepdims=True))


def log_add(parts):
    top = functools.reduce(jnp.maximum, parts)
    return top + jnp.log(sum(jnp.exp(part - top) for part in parts))


def stack_rows(shape, rows):
    index = lax.broadcasted_iota(jnp.int32, shape, 0)
    tile = jnp.zeros(shape, jnp.float32)
    for place, row in enumerate(rows):
        tile = jnp.where(index == place, row, tile)
    return tile


def fill_grad_sim(passages, coefficient, powers, out, column):
    tokens = powers.shape[0] // passages
    rows = powers.shape[1]
    for c in range(passages):
        part = slice(c * tokens, (c + 1) * tokens)
        out[part, column : column + rows] = (powers[part, :] * coefficient[c : c + 1, :]).astype(
            jnp.bfloat16
        )


def send_back(passages, turned, sent, powers, totals, scores, log, tail, back, grad_sim):
    dim, rows = turned.shape[0], powers.shape[1]
    dscore = loss_scale * jnp.exp(scores[...] - log)
    coefficient = outer_scale * dscore * sent_keep(sent, rows) / totals[...]
    fill_grad_sim(passages, coefficient, powers, grad_sim, 0)
    back[:dim, :] = dot32(turned[...], grad_sim[...]).astype(jnp.bfloat16)
    tail = stack_rows((ROWS, rows), [part.astype(jnp.float32) for part in tail])
    back[dim:, :] = tail.astype(jnp.bfloat16)


def far_score_body(
    queries, passages, valid, embed, turned, sent,
    powers, totals, scores, log_out, back, tops, grad_sim,
):
    score_block(queries, passages, valid, embed, sent, powers, totals, scores, tops)
    log = log_sum(scores[...])
    log_out[...] = stack_rows(log_out.shape, (log,))
    send_back(passages, turned, sent, powers, totals, scores, log, split(log), back, grad_sim)


def near_score_body(
    queries, passages, valid, embed, turned, sent, log0, log2, far0,
    powers, totals, scores, logs, back, tops, grad_sim,
):
    score_block(queries, passages, valid, embed, sent, powers, totals, scores, tops)
    log = log_sum(scores[...])
    other = log2[0:1, :]
    logs[...] = stack_rows(logs.shape, (log0[0:1, :], log, other, far0[0:1, :]))
    tail = split(log) + split(other)
    send_back(passages, turned, sent, powers, totals, scores, log, tail, back, grad_sim)


def joined(back, dim, place):
    tail = back[dim:, :].astype(jnp.float32)
    high, middle, low = [tail[i : i + 1, :] for i in range(place, place + 3)]
    return high + (middle + low)


def turn_body(query_hidden, passage_hidden, out):
    rows = query_hidden.shape[0]
    out[:, :rows] = query_hidden[...].T
    out[:, rows:] = passage_hidden[...].T


def grad_body(
    queries, passages, wanted, hidden_turned, turned,
    query_unit, query_inverse, passage_unit, passage_inverse,
    powers0, powers1, powers2, totals0, totals1, totals2, scores0, scores1, scores2,
    sent0, sent1, sent2, logs, logs1, back1, back2,
    all_logs, wanted_logs, query_pre_grad, passage_pre_grad, partial,
    grad_sim, query_rows, pre_rows,
):
    rows = powers0.shape[1]
    dim = turned.shape[0]
    second, third = joined(back1, dim, 0), joined(back2, dim, 0)
    total0 = log_add((logs[0:1, :], second, third))
    total1 = log_add((logs1[0:1, :], logs[1:2, :], joined(back1, dim, 3)))
    total2 = log_add((logs[3:4, :], logs1[1:2, :], logs[2:3, :]))
    scores = scores0[...]
    onehot = lax.broadcasted_iota(jnp.int32, scores.shape, 0) == wanted[...]
    wanted_score = jnp.sum(jnp.where(onehot, scores, 0.0), axis=0, keepdims=True)
    pick = lax.broadcasted_iota(jnp.int32, (rows, LANES), 1) * (rows // queries)
    pick = (pick == lax.broadcasted_iota(jnp.int32, (rows, LANES), 0)).astype(jnp.bfloat16)
    lines = [part.astype(jnp.float32) for part in split(total0) + split(wanted_score)]
    lines = dot32(stack_rows((ROWS, rows), lines).astype(jnp.bfloat16), pick)[:, :queries]
    all_logs[...] = lines[0:1] + (lines[1:2] + lines[2:3])
    wanted_logs[...] = lines[3:4] + (lines[4:5] + lines[5:6])

    for block, (total, query, powers, totals, scores) in enumerate((
        (total0, sent0, powers0, totals0, scores0),
        (total1, sent1, powers1, totals1, scores1),
        (total2, sent2, powers2, totals2, scores2),
    )):
        dscore = jnp.exp(scores[...] - total)
        if block == 0:
            dscore = dscore - onehot.astype(jnp.float32)
        coefficient = (outer_scale * loss_scale) * dscore * sent_keep(query, rows) / totals[...]
        fill_grad_sim(passages, coefficient, powers, grad_sim, block * rows)
        query_rows[block * rows : (block + 1) * rows, :] = query[:rows, :]

    grad = dot32(grad_sim[...], query_rows[...])
    pre = back_rows(grad, passage_unit[...], passage_inverse[...])
    passage_pre_grad[...] = pre
    pre_rows[rows:, :] = pre
    to_query = dot32(turned[...], grad_sim[:, :rows])
    to_query += back1[:dim, :].astype(jnp.float32) * jnp.exp(second - total0)
    to_query += back2[:dim, :].astype(jnp.float32) * jnp.exp(third - total0)
    pre = back_rows(to_query.T, query_unit[...], query_inverse[...])
    query_pre_grad[...] = pre
    pre_rows[:rows, :] = pre
    partial[...] = dot32(hidden_turned[...], pre_rows[...]).astype(jnp.bfloat16)


def sum_body(scale, copies, pieces, out):
    total = jnp.sum(pieces[...].astype(jnp.float32), axis=0) * scale
    total = total.astype(jnp.bfloat16)
    for copy in range(copies):
        out[copy] = total


def mean_over_devices(partial):
    axes = ("batch", "mp")
    devices = lax.axis_size("batch") * lax.axis_size("mp")
    rows, columns = partial.shape
    share = -(-rows // (devices * 8)) * 8
    padded = jnp.pad(partial, ((0, share * devices - rows), (0, 0)))
    pieces = lax.all_to_all(padded.reshape(devices, share, columns), axes, 0, 0)
    means = call(
        functools.partial(sum_body, 1.0 / devices, devices),
        (jax.ShapeDtypeStruct(pieces.shape, jnp.bfloat16),),
        (vmem,),
        (pieces,),
    )[0]
    whole = lax.all_to_all(means, axes, 0, 0)
    return whole.reshape(devices * share, columns)[:rows].astype(jnp.float32)


def per_device(query_hidden, passage_hidden, projection, query_lengths, passage_lengths, positives):
    queries = query_lengths.shape[0]
    passages = passage_lengths.shape[0]
    rows, width = query_hidden.shape
    slots = passage_hidden.shape[0]
    dim = projection.shape[1]
    f32, bf16 = jnp.float32, jnp.bfloat16
    of = jax.ShapeDtypeStruct
    pair = of((ROWS, rows), f32)
    pairs = pltpu.VMEM((ROWS, rows), f32)

    taken = (
        query_lengths, passage_lengths, positives, query_hidden, passage_hidden, projection
    )
    taken = tuple(pltpu.with_memory_space_constraint(x, pltpu.HBM) for x in taken)
    query_unit, query_inverse, sent0, valid, wanted, query_rows, passage_rows, weight = call(
        functools.partial(query_embed_body, queries),
        (
            of((rows, dim), f32), of((rows, dim), f32), of((rows + ROWS, dim), bf16),
            of((ROWS, rows), jnp.int32),
            of((1, rows), jnp.int32), of((rows, width), bf16), of((slots, width), bf16),
            of((width, dim), bf16),
        ),
        (hbm,) * 6,
        taken,
        scratch=(
            pltpu.SMEM((queries,), jnp.int32),
            pltpu.SMEM((passages,), jnp.int32),
            pltpu.SMEM((queries,), jnp.int32),
            pltpu.SemaphoreType.DMA((6,)),
        ),
        flops=2 * rows * width * dim,
    )
    sent1 = shifted(sent0, "batch", 1)
    sent2 = shifted(sent0, "batch", 2)
    (
        passage_unit, passage_inverse, embed, turned, powers0, totals0, scores0, log0
    ) = call(
        functools.partial(own_score_body, queries, passages),
        (
            of((slots, dim), f32), of((slots, dim), f32), of((slots, dim), bf16),
            of((dim, slots), bf16), of((slots, rows), f32), pair, pair, of((8, rows), f32),
        ),
        (vmem,) * 4,
        (valid, passage_rows, weight, sent0),
        scratch=(pairs,),
        flops=2 * slots * dim * (width + rows),
        trans=slots * rows,
    )
    far0 = shifted(log0, "batch", 2)
    block_outs = (
        of((slots, rows), f32), pair, pair, of((8, rows), f32), of((dim + ROWS, rows), bf16)
    )
    powers2, totals2, scores2, log2, back2 = call(
        functools.partial(far_score_body, queries, passages),
        block_outs,
        (vmem,) * 4,
        (valid, embed, turned, sent2),
        scratch=(pairs, pltpu.VMEM((slots, rows), bf16)),
        flops=4 * slots * dim * rows,
        trans=slots * rows,
    )
    back2 = shifted(back2, "batch", -2)
    powers1, totals1, scores1, logs, back1 = call(
        functools.partial(near_score_body, queries, passages),
        block_outs,
        (vmem,) * 7,
        (valid, embed, turned, sent1, log0, log2, far0),
        scratch=(pairs, pltpu.VMEM((slots, rows), bf16)),
        flops=4 * slots * dim * rows,
        trans=slots * rows,
    )
    back1 = shifted(back1, "batch", -1)
    logs1 = shifted(logs, "batch", 1)
    hidden_turned = call(
        turn_body,
        (of((width, rows + slots), bf16),),
        (vmem,) * 2,
        (query_rows, passage_rows),
        flops=500 * slots * width,
    )[0]
    all_logs, wanted_logs, query_pre_grad, passage_pre_grad, partial = call(
        functools.partial(grad_body, queries, passages),
        (
            of((1, queries), f32), of((1, queries), f32), of((rows, dim), bf16),
            of((slots, dim), bf16),
            of((width, dim), bf16),
        ),
        (vmem,) * 23,
        (wanted, hidden_turned, turned,
         query_unit, query_inverse, passage_unit, passage_inverse,
         powers0, powers1, powers2, totals0, totals1, totals2, scores0, scores1, scores2,
         sent0, sent1, sent2, logs, logs1, back1, back2),
        scratch=(
            pltpu.VMEM((slots, 3 * rows), bf16),
            pltpu.VMEM((3 * rows, dim), bf16),
            pltpu.VMEM((rows + slots, dim), bf16),
        ),
        flops=8 * slots * dim * rows + 2 * (slots + rows) * width * dim,
    )
    grad_projection = mean_over_devices(partial)
    grad_query_hidden = dot32(query_pre_grad, weight, NT).astype(bf16)
    grad_passage_hidden = dot32(passage_pre_grad, weight, NT).astype(bf16)
    losses = (all_logs - wanted_logs).reshape(queries)
    return (losses, grad_query_hidden, grad_passage_hidden, grad_projection)


def solution(mesh):
    in_specs = (
        P(("batch", "mp"), None),
        P(("batch", "mp"), None),
        P(),
        P(("batch", "mp")),
        P(("batch", "mp")),
        P(("batch", "mp")),
    )
    out_specs = (P(("batch", "mp")), P(("batch", "mp"), None), P(("batch", "mp"), None), P())
    return jax.shard_map(
        per_device, mesh=mesh, in_specs=in_specs, out_specs=out_specs, check_vma=False
    )
```

```python
import functools
import math

import jax
import jax.numpy as jnp
from jax import lax
from jax.experimental import pallas as pl
from jax.experimental.pallas import tpu as pltpu
from jax.sharding import PartitionSpec as P

inner_scale = 128.0
outer_scale = 8.0
loss_scale = 32.0
norm_eps = 1e-06

LANES = 128
ROWS = 16
LOG2E = 1.0 / math.log(2.0)
NT = (((1,), (1,)), ((), ()))

vmem = pl.BlockSpec(memory_space=pltpu.VMEM)
hbm = pl.BlockSpec(memory_space=pltpu.HBM)


def shifted(block, axis, distance):
    devices = range(lax.axis_size(axis))
    route = [((i - distance) % len(devices), i) for i in devices]
    return lax.ppermute(block, axis, route)


def dot32(left, right, dims=(((1,), (0,)), ((), ()))):
    return lax.dot_general(left, right, dims, preferred_element_type=jnp.float32)


def call(body, outs, in_specs, args, scratch=(), flops=0, trans=0, out_specs=None):
    moved = sum(a.size * a.dtype.itemsize for a in args)
    moved += sum(math.prod(o.shape) * jnp.dtype(o.dtype).itemsize for o in outs)
    return pl.pallas_call(
        body,
        out_shape=tuple(outs),
        in_specs=list(in_specs),
        out_specs=out_specs or tuple(vmem for _ in outs),
        scratch_shapes=list(scratch),
        compiler_params=pltpu.CompilerParams(vmem_limit_bytes=24 * 2**20),
        cost_estimate=pl.CostEstimate(flops=flops, bytes_accessed=moved, transcendentals=trans),
    )(*args)


def spread(values, count, group):
    lane = lax.broadcasted_iota(jnp.int32, (1, count * group), 1) // group
    row = jnp.zeros((1, count * group), jnp.int32)
    for item in range(count):
        row = jnp.where(lane == item, values[item], row)
    return row


def keep_row(lengths, queries, tokens):
    slot = lax.broadcasted_iota(jnp.int32, (1, queries * tokens), 1) % tokens
    return (slot < spread(lengths, queries, tokens)).astype(jnp.float32)


def unit_rows(before):
    inverse = lax.rsqrt(jnp.sum(before * before, axis=1, keepdims=True) + norm_eps)
    return before * inverse, inverse


def back_rows(grad, unit, inverse):
    inner = jnp.sum(unit * grad, axis=1, keepdims=True)
    return ((grad - unit * inner) * inverse).astype(jnp.bfloat16)


def load_all(pairs, sems):
    copies = [pltpu.make_async_copy(a, b, sems.at[i]) for i, (a, b) in enumerate(pairs)]
    for copy in copies:
        copy.start()
    return copies


def query_embed_body(
    queries, query_lengths_in, passage_lengths_in, positives_in, query_hidden_in, passage_hidden_in,
    projection_in,
    unit_out, inverse_out, sent_out, slots_out, wanted_out, query_hidden, passage_hidden, projection,
    query_lengths, passage_lengths, positives, sems,
):
    pairs = (
        (projection_in, projection), (query_hidden_in, query_hidden),
        (query_lengths_in, query_lengths), (positives_in, positives),
        (passage_lengths_in, passage_lengths), (passage_hidden_in, passage_hidden),
    )
    copies = load_all(pairs, sems)
    copies[0].wait()
    copies[1].wait()
    rows = query_hidden.shape[0]
    before = dot32(query_hidden[...], projection[...])
    unit, inverse = unit_rows(before)
    unit_out[...] = unit
    inverse_out[...] = jnp.broadcast_to(inverse, unit.shape)
    sent_out[:rows, :] = unit.astype(jnp.bfloat16)
    copies[2].wait()
    keep = keep_row(query_lengths, queries, rows // queries)
    row = lax.broadcasted_iota(jnp.int32, (ROWS, LANES), 0)
    tail = jnp.zeros((ROWS, LANES), jnp.float32)
    for piece in range(rows // LANES):
        tail = jnp.where(row == piece, keep[:, piece * LANES : (piece + 1) * LANES], tail)
    sent_out[rows:, :] = tail.astype(jnp.bfloat16)
    copies[3].wait()
    wanted_out[...] = spread(positives, queries, rows // queries)
    copies[4].wait()
    c = lax.broadcasted_iota(jnp.int32, slots_out.shape, 0)
    valid = jnp.zeros(slots_out.shape, jnp.int32)
    for item in range(passage_lengths.shape[0]):
        valid = jnp.where(c == item, passage_lengths[item], valid)
    slots_out[...] = valid
    copies[5].wait()


def sent_keep(sent, rows):
    tail = sent[rows:, :].astype(jnp.float32)
    return jnp.concatenate([tail[i : i + 1, :] for i in range(rows // LANES)], axis=1)


def split(values):
    high = values.astype(jnp.bfloat16)
    rest = values - high.astype(jnp.float32)
    middle = rest.astype(jnp.bfloat16)
    return high, middle, (rest - middle.astype(jnp.float32)).astype(jnp.bfloat16)


def score_block(queries, passages, valid, embed, sent, powers, totals, scores, tops):
    rows = sent.shape[0] - ROWS
    tokens = embed.shape[0] // passages
    query = sent[:rows, :]
    half = tokens // 2
    slot = lax.broadcasted_iota(jnp.int32, (tokens - half, rows), 0) + half
    totals[...] = jnp.ones(totals.shape, jnp.float32)
    tops[...] = jnp.zeros(tops.shape, jnp.float32)
    for c in range(passages):
        sims = dot32(embed[c * tokens : (c + 1) * tokens, :], query, NT)
        low, high = sims[:half], jnp.where(slot < valid[c : c + 1, :], sims[half:], -jnp.inf)
        top = jnp.maximum(
            jnp.max(low, axis=0, keepdims=True), jnp.max(high, axis=0, keepdims=True)
        )
        low = jnp.exp2((low - top) * (inner_scale * LOG2E))
        high = jnp.exp2((high - top) * (inner_scale * LOG2E))
        powers[c * tokens : c * tokens + half, :] = low
        powers[c * tokens + half : (c + 1) * tokens, :] = high
        tops[c : c + 1, :] = top
        totals[c : c + 1, :] = jnp.sum(low, axis=0, keepdims=True) + jnp.sum(
            high, axis=0, keepdims=True
        )
    best = tops[...] + jnp.log(totals[...]) / inner_scale
    best = best * sent_keep(sent, rows)
    group = rows // queries
    same = lax.broadcasted_iota(jnp.int32, (rows, rows), 0) // group
    same = (same == lax.broadcasted_iota(jnp.int32, (rows, rows), 1) // group).astype(jnp.bfloat16)
    total = sum(dot32(part, same) for part in split(best))
    c = lax.broadcasted_iota(jnp.int32, total.shape, 0)
    scores[...] = jnp.where(c < passages, outer_scale * total, -jnp.inf)


def own_score_body(
    queries, passages, valid, hidden, projection, sent,
    unit_out, inverse_out, embed_out, turned_out, powers, totals, scores, log_out, tops,
):
    unit, inverse = unit_rows(dot32(hidden[...], projection[...]))
    unit_out[...] = unit
    inverse_out[...] = jnp.broadcast_to(inverse, unit.shape)
    embed = unit.astype(jnp.bfloat16)
    embed_out[...] = embed
    score_block(queries, passages, valid, embed_out, sent, powers, totals, scores, tops)
    log_out[...] = stack_rows(log_out.shape, (log_sum(scores[...]),))
    turned_out[...] = embed.T


def log_sum(scores):
    top = jnp.max(scores, axis=0, keepdims=True)
    return top + jnp.log(jnp.sum(jnp.exp(scores - top), axis=0, keepdims=True))


def log_add(parts):
    top = functools.reduce(jnp.maximum, parts)
    return top + jnp.log(sum(jnp.exp(part - top) for part in parts))


def stack_rows(shape, rows):
    index = lax.broadcasted_iota(jnp.int32, shape, 0)
    tile = jnp.zeros(shape, jnp.float32)
    for place, row in enumerate(rows):
        tile = jnp.where(index == place, row, tile)
    return tile


def fill_grad_sim(passages, coefficient, powers, out, column):
    tokens = powers.shape[0] // passages
    rows = powers.shape[1]
    for c in range(passages):
        part = slice(c * tokens, (c + 1) * tokens)
        out[part, column : column + rows] = (powers[part, :] * coefficient[c : c + 1, :]).astype(
            jnp.bfloat16
        )


def send_back(passages, turned, sent, powers, totals, scores, log, tail, back, grad_sim):
    dim, rows = turned.shape[0], powers.shape[1]
    dscore = loss_scale * jnp.exp(scores[...] - log)
    coefficient = outer_scale * dscore * sent_keep(sent, rows) / totals[...]
    fill_grad_sim(passages, coefficient, powers, grad_sim, 0)
    back[:dim, :] = dot32(turned[...], grad_sim[...]).astype(jnp.bfloat16)
    tail = stack_rows((ROWS, rows), [part.astype(jnp.float32) for part in tail])
    back[dim:, :] = tail.astype(jnp.bfloat16)


def far_score_body(
    queries, passages, valid, embed, turned, sent,
    powers, totals, scores, log_out, back, tops, grad_sim,
):
    score_block(queries, passages, valid, embed, sent, powers, totals, scores, tops)
    log = log_sum(scores[...])
    log_out[...] = stack_rows(log_out.shape, (log,))
    send_back(passages, turned, sent, powers, totals, scores, log, split(log), back, grad_sim)


def near_score_body(
    queries, passages, valid, embed, turned, sent, log0, log2, far0,
    powers, totals, scores, logs, back, tops, grad_sim,
):
    score_block(queries, passages, valid, embed, sent, powers, totals, scores, tops)
    log = log_sum(scores[...])
    other = log2[0:1, :]
    logs[...] = stack_rows(logs.shape, (log0[0:1, :], log, other, far0[0:1, :]))
    tail = split(log) + split(other)
    send_back(passages, turned, sent, powers, totals, scores, log, tail, back, grad_sim)


def joined(back, dim, place):
    tail = back[dim:, :].astype(jnp.float32)
    high, middle, low = [tail[i : i + 1, :] for i in range(place, place + 3)]
    return high + (middle + low)


def grad_body(
    queries, passages, wanted, query_hidden, passage_hidden, turned,
    query_unit, query_inverse, passage_unit, passage_inverse,
    powers0, powers1, powers2, totals0, totals1, totals2, scores0, scores1, scores2,
    sent0, sent1, sent2, logs, logs1, back1, back2,
    all_logs, wanted_logs, query_pre_grad, passage_pre_grad, partial, grad_sim, query_rows,
):
    rows = powers0.shape[1]
    dim = turned.shape[0]
    second, third = joined(back1, dim, 0), joined(back2, dim, 0)
    total0 = log_add((logs[0:1, :], second, third))
    total1 = log_add((logs1[0:1, :], logs[1:2, :], joined(back1, dim, 3)))
    total2 = log_add((logs[3:4, :], logs1[1:2, :], logs[2:3, :]))
    scores = scores0[...]
    onehot = lax.broadcasted_iota(jnp.int32, scores.shape, 0) == wanted[...]
    wanted_score = jnp.sum(jnp.where(onehot, scores, 0.0), axis=0, keepdims=True)
    pick = lax.broadcasted_iota(jnp.int32, (rows, LANES), 1) * (rows // queries)
    pick = (pick == lax.broadcasted_iota(jnp.int32, (rows, LANES), 0)).astype(jnp.bfloat16)
    lines = [part.astype(jnp.float32) for part in split(total0) + split(wanted_score)]
    lines = dot32(stack_rows((ROWS, rows), lines).astype(jnp.bfloat16), pick)[:, :queries]
    all_logs[...] = lines[0:1] + (lines[1:2] + lines[2:3])
    wanted_logs[...] = lines[3:4] + (lines[4:5] + lines[5:6])

    for block, (total, query, powers, totals, scores) in enumerate((
        (total0, sent0, powers0, totals0, scores0),
        (total1, sent1, powers1, totals1, scores1),
        (total2, sent2, powers2, totals2, scores2),
    )):
        dscore = jnp.exp(scores[...] - total)
        if block == 0:
            dscore = dscore - onehot.astype(jnp.float32)
        coefficient = (outer_scale * loss_scale) * dscore * sent_keep(query, rows) / totals[...]
        fill_grad_sim(passages, coefficient, powers, grad_sim, block * rows)
        query_rows[block * rows : (block + 1) * rows, :] = query[:rows, :]

    grad = dot32(grad_sim[...], query_rows[...])
    pre = back_rows(grad, passage_unit[...], passage_inverse[...])
    passage_pre_grad[...] = pre
    both = dot32(pre.T, passage_hidden[...])
    to_query = dot32(turned[...], grad_sim[:, :rows])
    to_query += back1[:dim, :].astype(jnp.float32) * jnp.exp(second - total0)
    to_query += back2[:dim, :].astype(jnp.float32) * jnp.exp(third - total0)
    pre = back_rows(to_query.T, query_unit[...], query_inverse[...])
    query_pre_grad[...] = pre
    both += dot32(pre.T, query_hidden[...])
    partial[...] = both.T.astype(jnp.bfloat16)


def sum_body(scale, copies, pieces, out):
    total = jnp.sum(pieces[...].astype(jnp.float32), axis=0) * scale
    total = total.astype(jnp.bfloat16)
    for copy in range(copies):
        out[copy] = total


def cast_body(count, source, out, wide, sems):
    size = source.shape[0] // count
    copies = []
    for piece in range(count):
        part = pl.ds(piece * size, size)
        wide[part, :] = source[part, :].astype(jnp.float32)
        copies.append(pltpu.make_async_copy(wide.at[part], out.at[part], sems.at[piece]))
        copies[-1].start()
    for copy in copies:
        copy.wait()


def mean_over_devices(partial, later):
    axes = ("batch", "mp")
    devices = lax.axis_size("batch") * lax.axis_size("mp")
    rows, columns = partial.shape
    share = -(-rows // (devices * 8)) * 8
    padded = jnp.pad(partial, ((0, share * devices - rows), (0, 0)))
    pieces = lax.all_to_all(padded.reshape(devices, share, columns), axes, 0, 0)
    pieces, later = lax.optimization_barrier((pieces, later))
    means = call(
        functools.partial(sum_body, 1.0 / devices, devices),
        (jax.ShapeDtypeStruct(pieces.shape, jnp.bfloat16),),
        (vmem,),
        (pieces,),
    )[0]
    whole = lax.all_to_all(means, axes, 0, 0)
    whole = whole.reshape(devices * share, columns)[:rows]
    count = 4 if rows % 64 == 0 else 1
    whole = call(
        functools.partial(cast_body, count),
        (jax.ShapeDtypeStruct((rows, columns), jnp.float32),),
        (vmem,),
        (whole,),
        scratch=(pltpu.VMEM((rows, columns), jnp.float32), pltpu.SemaphoreType.DMA((count,))),
        out_specs=(hbm,),
    )[0]
    return whole, later


def per_device(query_hidden, passage_hidden, projection, query_lengths, passage_lengths, positives):
    queries = query_lengths.shape[0]
    passages = passage_lengths.shape[0]
    rows, width = query_hidden.shape
    slots = passage_hidden.shape[0]
    dim = projection.shape[1]
    f32, bf16 = jnp.float32, jnp.bfloat16
    of = jax.ShapeDtypeStruct
    pair = of((ROWS, rows), f32)
    pairs = pltpu.VMEM((ROWS, rows), f32)

    taken = (
        query_lengths, passage_lengths, positives, query_hidden, passage_hidden, projection
    )
    taken = tuple(pltpu.with_memory_space_constraint(x, pltpu.HBM) for x in taken)
    query_unit, query_inverse, sent0, valid, wanted, query_rows, passage_rows, weight = call(
        functools.partial(query_embed_body, queries),
        (
            of((rows, dim), f32), of((rows, dim), f32), of((rows + ROWS, dim), bf16),
            of((ROWS, rows), jnp.int32),
            of((1, rows), jnp.int32), of((rows, width), bf16), of((slots, width), bf16),
            of((width, dim), bf16),
        ),
        (hbm,) * 6,
        taken,
        scratch=(
            pltpu.SMEM((queries,), jnp.int32),
            pltpu.SMEM((passages,), jnp.int32),
            pltpu.SMEM((queries,), jnp.int32),
            pltpu.SemaphoreType.DMA((6,)),
        ),
        flops=2 * rows * width * dim,
    )
    sent1 = shifted(sent0, "batch", 1)
    sent2 = shifted(sent0, "batch", 2)
    (
        passage_unit, passage_inverse, embed, turned, powers0, totals0, scores0, log0
    ) = call(
        functools.partial(own_score_body, queries, passages),
        (
            of((slots, dim), f32), of((slots, dim), f32), of((slots, dim), bf16),
            of((dim, slots), bf16), of((slots, rows), f32), pair, pair, of((8, rows), f32),
        ),
        (vmem,) * 4,
        (valid, passage_rows, weight, sent0),
        scratch=(pairs,),
        flops=2 * slots * dim * (width + rows),
        trans=slots * rows,
    )
    far0 = shifted(log0, "batch", 2)
    block_outs = (
        of((slots, rows), f32), pair, pair, of((8, rows), f32), of((dim + ROWS, rows), bf16)
    )
    powers2, totals2, scores2, log2, back2 = call(
        functools.partial(far_score_body, queries, passages),
        block_outs,
        (vmem,) * 4,
        (valid, embed, turned, sent2),
        scratch=(pairs, pltpu.VMEM((slots, rows), bf16)),
        flops=4 * slots * dim * rows,
        trans=slots * rows,
    )
    back2 = shifted(back2, "batch", -2)
    powers1, totals1, scores1, logs, back1 = call(
        functools.partial(near_score_body, queries, passages),
        block_outs,
        (vmem,) * 7,
        (valid, embed, turned, sent1, log0, log2, far0),
        scratch=(pairs, pltpu.VMEM((slots, rows), bf16)),
        flops=4 * slots * dim * rows,
        trans=slots * rows,
    )
    back1 = shifted(back1, "batch", -1)
    logs1 = shifted(logs, "batch", 1)
    all_logs, wanted_logs, query_pre_grad, passage_pre_grad, partial = call(
        functools.partial(grad_body, queries, passages),
        (
            of((1, queries), f32), of((1, queries), f32), of((rows, dim), bf16),
            of((slots, dim), bf16),
            of((width, dim), bf16),
        ),
        (vmem,) * 24,
        (wanted, query_rows, passage_rows, turned,
         query_unit, query_inverse, passage_unit, passage_inverse,
         powers0, powers1, powers2, totals0, totals1, totals2, scores0, scores1, scores2,
         sent0, sent1, sent2, logs, logs1, back1, back2),
        scratch=(pltpu.VMEM((slots, 3 * rows), bf16), pltpu.VMEM((3 * rows, dim), bf16)),
        flops=8 * slots * dim * rows + 2 * (slots + rows) * width * dim,
    )
    later = (query_pre_grad, passage_pre_grad, all_logs, wanted_logs)
    grad_projection, later = mean_over_devices(partial, later)
    query_pre_grad, passage_pre_grad, all_logs, wanted_logs = later
    grad_query_hidden = dot32(query_pre_grad, weight, NT).astype(bf16)
    grad_passage_hidden = dot32(passage_pre_grad, weight, NT).astype(bf16)
    losses = (all_logs - wanted_logs).reshape(queries)
    return (losses, grad_query_hidden, grad_passage_hidden, grad_projection)


def solution(mesh):
    in_specs = (
        P(("batch", "mp"), None),
        P(("batch", "mp"), None),
        P(),
        P(("batch", "mp")),
        P(("batch", "mp")),
        P(("batch", "mp")),
    )
    out_specs = (P(("batch", "mp")), P(("batch", "mp"), None), P(("batch", "mp"), None), P())
    return jax.shard_map(
        per_device, mesh=mesh, in_specs=in_specs, out_specs=out_specs, check_vma=False
    )
```

```python
import functools
import math

import jax
import jax.numpy as jnp
from jax import lax
from jax.experimental import pallas as pl
from jax.experimental.pallas import tpu as pltpu
from jax.sharding import PartitionSpec as P

inner_scale = 128.0
outer_scale = 8.0
loss_scale = 32.0
norm_eps = 1e-06

LANES = 128
ROWS = 16
LOG2E = 1.0 / math.log(2.0)
NT = (((1,), (1,)), ((), ()))

vmem = pl.BlockSpec(memory_space=pltpu.VMEM)
hbm = pl.BlockSpec(memory_space=pltpu.HBM)


def shifted(block, axis, distance):
    devices = range(lax.axis_size(axis))
    route = [((i - distance) % len(devices), i) for i in devices]
    return lax.ppermute(block, axis, route)


def dot32(left, right, dims=(((1,), (0,)), ((), ()))):
    return lax.dot_general(left, right, dims, preferred_element_type=jnp.float32)


def call(body, outs, in_specs, args, scratch=(), flops=0, trans=0):
    moved = sum(a.size * a.dtype.itemsize for a in args)
    moved += sum(math.prod(o.shape) * jnp.dtype(o.dtype).itemsize for o in outs)
    return pl.pallas_call(
        body,
        out_shape=tuple(outs),
        in_specs=list(in_specs),
        out_specs=tuple(vmem for _ in outs),
        scratch_shapes=list(scratch),
        compiler_params=pltpu.CompilerParams(vmem_limit_bytes=24 * 2**20),
        cost_estimate=pl.CostEstimate(flops=flops, bytes_accessed=moved, transcendentals=trans),
    )(*args)


def spread(values, count, group):
    lane = lax.broadcasted_iota(jnp.int32, (1, count * group), 1) // group
    row = jnp.zeros((1, count * group), jnp.int32)
    for item in range(count):
        row = jnp.where(lane == item, values[item], row)
    return row


def keep_row(lengths, queries, tokens):
    slot = lax.broadcasted_iota(jnp.int32, (1, queries * tokens), 1) % tokens
    return (slot < spread(lengths, queries, tokens)).astype(jnp.float32)


def unit_rows(before):
    inverse = lax.rsqrt(jnp.sum(before * before, axis=1, keepdims=True) + norm_eps)
    return before * inverse, inverse


def back_rows(grad, unit, inverse):
    inner = jnp.sum(unit * grad, axis=1, keepdims=True)
    return ((grad - unit * inner) * inverse).astype(jnp.bfloat16)


def load_all(pairs, sems):
    copies = [pltpu.make_async_copy(a, b, sems.at[i]) for i, (a, b) in enumerate(pairs)]
    for copy in copies:
        copy.start()
    return copies


def query_embed_body(
    queries, query_lengths_in, passage_lengths_in, positives_in, query_hidden_in, passage_hidden_in,
    projection_in,
    unit_out, inverse_out, sent_out, slots_out, wanted_out, query_hidden, passage_hidden, projection,
    query_lengths, passage_lengths, positives, sems,
):
    pairs = (
        (projection_in, projection), (query_hidden_in, query_hidden),
        (query_lengths_in, query_lengths), (positives_in, positives),
        (passage_lengths_in, passage_lengths), (passage_hidden_in, passage_hidden),
    )
    copies = load_all(pairs, sems)
    copies[0].wait()
    copies[1].wait()
    rows = query_hidden.shape[0]
    before = dot32(query_hidden[...], projection[...])
    unit, inverse = unit_rows(before)
    unit_out[...] = unit
    inverse_out[...] = jnp.broadcast_to(inverse, unit.shape)
    sent_out[:rows, :] = unit.astype(jnp.bfloat16)
    copies[2].wait()
    keep = keep_row(query_lengths, queries, rows // queries)
    row = lax.broadcasted_iota(jnp.int32, (ROWS, LANES), 0)
    tail = jnp.zeros((ROWS, LANES), jnp.float32)
    for piece in range(rows // LANES):
        tail = jnp.where(row == piece, keep[:, piece * LANES : (piece + 1) * LANES], tail)
    sent_out[rows:, :] = tail.astype(jnp.bfloat16)
    copies[3].wait()
    wanted_out[...] = spread(positives, queries, rows // queries)
    copies[4].wait()
    c = lax.broadcasted_iota(jnp.int32, slots_out.shape, 0)
    valid = jnp.zeros(slots_out.shape, jnp.int32)
    for item in range(passage_lengths.shape[0]):
        valid = jnp.where(c == item, passage_lengths[item], valid)
    slots_out[...] = valid
    copies[5].wait()


def sent_row(sent, rows, place):
    tail = sent[rows:, :].astype(jnp.float32)
    count = rows // LANES
    return jnp.concatenate(
        [tail[i : i + 1, :] for i in range(place * count, (place + 1) * count)], axis=1
    )


def sent_keep(sent, rows):
    return sent_row(sent, rows, 0)


def sent_log(sent, rows):
    return sent_row(sent, rows, 1) + (sent_row(sent, rows, 2) + sent_row(sent, rows, 3))


def split(values):
    high = values.astype(jnp.bfloat16)
    rest = values - high.astype(jnp.float32)
    middle = rest.astype(jnp.bfloat16)
    return high, middle, (rest - middle.astype(jnp.float32)).astype(jnp.bfloat16)


def score_block(queries, passages, valid, embed, sent, powers, totals, scores, tops):
    rows = sent.shape[0] - ROWS
    tokens = embed.shape[0] // passages
    query = sent[:rows, :]
    half = tokens // 2
    slot = lax.broadcasted_iota(jnp.int32, (tokens - half, rows), 0) + half
    totals[...] = jnp.ones(totals.shape, jnp.float32)
    tops[...] = jnp.zeros(tops.shape, jnp.float32)
    for c in range(passages):
        sims = dot32(embed[c * tokens : (c + 1) * tokens, :], query, NT)
        low, high = sims[:half], jnp.where(slot < valid[c : c + 1, :], sims[half:], -jnp.inf)
        top = jnp.maximum(
            jnp.max(low, axis=0, keepdims=True), jnp.max(high, axis=0, keepdims=True)
        )
        low = jnp.exp2((low - top) * (inner_scale * LOG2E))
        high = jnp.exp2((high - top) * (inner_scale * LOG2E))
        powers[c * tokens : c * tokens + half, :] = low
        powers[c * tokens + half : (c + 1) * tokens, :] = high
        tops[c : c + 1, :] = top
        totals[c : c + 1, :] = jnp.sum(low, axis=0, keepdims=True) + jnp.sum(
            high, axis=0, keepdims=True
        )
    best = tops[...] + jnp.log(totals[...]) / inner_scale
    best = best * sent_keep(sent, rows)
    group = rows // queries
    same = lax.broadcasted_iota(jnp.int32, (rows, rows), 0) // group
    same = (same == lax.broadcasted_iota(jnp.int32, (rows, rows), 1) // group).astype(jnp.bfloat16)
    total = sum(dot32(part, same) for part in split(best))
    c = lax.broadcasted_iota(jnp.int32, total.shape, 0)
    scores[...] = jnp.where(c < passages, outer_scale * total, -jnp.inf)


def own_score_body(
    queries, passages, valid, hidden, projection, sent,
    unit_out, inverse_out, embed_out, turned_out, powers, totals, scores, log_out, far_out, tops,
):
    unit, inverse = unit_rows(dot32(hidden[...], projection[...]))
    unit_out[...] = unit
    inverse_out[...] = jnp.broadcast_to(inverse, unit.shape)
    embed = unit.astype(jnp.bfloat16)
    embed_out[...] = embed
    score_block(queries, passages, valid, embed_out, sent, powers, totals, scores, tops)
    log = log_sum(scores[...])
    log_out[...] = stack_rows(log_out.shape, (log,))
    rows = powers.shape[1]
    far_out[:rows, :] = sent[:rows, :]
    lines = [sent_keep(sent, rows)] + [part.astype(jnp.float32) for part in split(log)]
    lines = [
        line[:, i * LANES : (i + 1) * LANES] for line in lines for i in range(rows // LANES)
    ]
    far_out[rows:, :] = stack_rows((ROWS, LANES), lines).astype(jnp.bfloat16)
    turned_out[...] = embed.T


def log_sum(scores):
    top = jnp.max(scores, axis=0, keepdims=True)
    return top + jnp.log(jnp.sum(jnp.exp(scores - top), axis=0, keepdims=True))


def log_add(parts):
    top = functools.reduce(jnp.maximum, parts)
    return top + jnp.log(sum(jnp.exp(part - top) for part in parts))


def stack_rows(shape, rows):
    index = lax.broadcasted_iota(jnp.int32, shape, 0)
    tile = jnp.zeros(shape, jnp.float32)
    for place, row in enumerate(rows):
        tile = jnp.where(index == place, row, tile)
    return tile


def fill_grad_sim(passages, coefficient, powers, out, column):
    tokens = powers.shape[0] // passages
    rows = powers.shape[1]
    for c in range(passages):
        part = slice(c * tokens, (c + 1) * tokens)
        out[part, column : column + rows] = (powers[part, :] * coefficient[c : c + 1, :]).astype(
            jnp.bfloat16
        )


def query_gradient(passages, turned, sent, powers, totals, scores, log, grad_sim):
    rows = powers.shape[1]
    dscore = loss_scale * jnp.exp(scores[...] - log)
    coefficient = outer_scale * dscore * sent_keep(sent, rows) / totals[...]
    fill_grad_sim(passages, coefficient, powers, grad_sim, 0)
    return dot32(turned[...], grad_sim[...]).astype(jnp.bfloat16)


def near_score_body(
    queries, passages, valid, embed, turned, sent, log0,
    powers, totals, scores, logs, near, tops, grad_sim,
):
    score_block(queries, passages, valid, embed, sent, powers, totals, scores, tops)
    log = log_sum(scores[...])
    logs[...] = stack_rows(logs.shape, (log0[0:1, :], log))
    near[...] = query_gradient(passages, turned, sent, powers, totals, scores, log, grad_sim)


def far_score_body(
    queries, passages, valid, embed, turned, sent, near, logs,
    powers, totals, scores, log_out, back2, back1, tops, grad_sim,
):
    dim, rows = turned.shape[0], powers.shape[1]
    score_block(queries, passages, valid, embed, sent, powers, totals, scores, tops)
    log = log_sum(scores[...])
    log_out[...] = stack_rows(log_out.shape, (log,))
    back2[:dim, :] = query_gradient(passages, turned, sent, powers, totals, scores, log, grad_sim)
    back1[:dim, :] = near[...]
    tail = split(log)
    for back, lines in ((back2, tail), (back1, split(logs[1:2, :]) + tail)):
        lines = stack_rows((ROWS, rows), [line.astype(jnp.float32) for line in lines])
        back[dim:, :] = lines.astype(jnp.bfloat16)


def joined(back, dim, place):
    tail = back[dim:, :].astype(jnp.float32)
    high, middle, low = [tail[i : i + 1, :] for i in range(place, place + 3)]
    return high + (middle + low)


def pair_logs_body(logs, logs1, sent2, out):
    far = sent_log(sent2, out.shape[1])
    out[...] = stack_rows(
        out.shape, (log_add((logs1[0:1, :], logs[1:2, :])), log_add((far, logs1[1:2, :])))
    )


def grad_body(
    queries, passages, wanted, query_hidden, passage_hidden, turned,
    query_unit, query_inverse, passage_unit, passage_inverse,
    powers0, powers1, powers2, totals0, totals1, totals2, scores0, scores1, scores2,
    sent0, sent1, sent2, logs, log2, pair_logs, back1, back2,
    losses, query_pre_grad, passage_pre_grad, partial, grad_sim, query_rows,
):
    rows = powers0.shape[1]
    dim = turned.shape[0]
    second, third = joined(back1, dim, 0), joined(back2, dim, 0)
    total0 = log_add((logs[0:1, :], second, third))
    total1 = log_add((pair_logs[0:1, :], joined(back1, dim, 3)))
    total2 = log_add((pair_logs[1:2, :], log2[0:1, :]))
    scores = scores0[...]
    onehot = lax.broadcasted_iota(jnp.int32, scores.shape, 0) == wanted[...]
    loss = total0 - jnp.sum(jnp.where(onehot, scores, 0.0), axis=0, keepdims=True)
    pick = lax.broadcasted_iota(jnp.int32, (rows, LANES), 1) * (rows // queries)
    pick = (pick == lax.broadcasted_iota(jnp.int32, (rows, LANES), 0)).astype(jnp.bfloat16)
    losses[...] = sum(dot32(part, pick) for part in split(loss))[:, :queries]

    for block, (total, query, powers, totals, scores) in enumerate((
        (total0, sent0, powers0, totals0, scores0),
        (total1, sent1, powers1, totals1, scores1),
        (total2, sent2, powers2, totals2, scores2),
    )):
        dscore = jnp.exp(scores[...] - total)
        if block == 0:
            dscore = dscore - onehot.astype(jnp.float32)
        coefficient = (outer_scale * loss_scale) * dscore * sent_keep(query, rows) / totals[...]
        fill_grad_sim(passages, coefficient, powers, grad_sim, block * rows)
        query_rows[block * rows : (block + 1) * rows, :] = query[:rows, :]

    grad = dot32(grad_sim[...], query_rows[...])
    pre = back_rows(grad, passage_unit[...], passage_inverse[...])
    passage_pre_grad[...] = pre
    both = dot32(pre.T, passage_hidden[...])
    to_query = dot32(turned[...], grad_sim[:, :rows])
    to_query += back1[:dim, :].astype(jnp.float32) * jnp.exp(second - total0)
    to_query += back2[:dim, :].astype(jnp.float32) * jnp.exp(third - total0)
    pre = back_rows(to_query.T, query_unit[...], query_inverse[...])
    query_pre_grad[...] = pre
    both += dot32(pre.T, query_hidden[...])
    partial[...] = both.T.astype(jnp.bfloat16)


def sum_body(scale, copies, pieces, out):
    total = jnp.sum(pieces[...].astype(jnp.float32), axis=0) * scale
    total = total.astype(jnp.bfloat16)
    for copy in range(copies):
        out[copy] = total


def mean_over_devices(partial):
    axes = ("batch", "mp")
    devices = lax.axis_size("batch") * lax.axis_size("mp")
    rows, columns = partial.shape
    share = -(-rows // (devices * 8)) * 8
    padded = jnp.pad(partial, ((0, share * devices - rows), (0, 0)))
    pieces = lax.all_to_all(padded.reshape(devices, share, columns), axes, 0, 0)
    means = call(
        functools.partial(sum_body, 1.0 / devices, devices),
        (jax.ShapeDtypeStruct(pieces.shape, jnp.bfloat16),),
        (vmem,),
        (pieces,),
    )[0]
    whole = lax.all_to_all(means, axes, 0, 0)
    return whole.reshape(devices * share, columns)[:rows].astype(jnp.float32)


def per_device(query_hidden, passage_hidden, projection, query_lengths, passage_lengths, positives):
    queries = query_lengths.shape[0]
    passages = passage_lengths.shape[0]
    rows, width = query_hidden.shape
    slots = passage_hidden.shape[0]
    dim = projection.shape[1]
    f32, bf16 = jnp.float32, jnp.bfloat16
    of = jax.ShapeDtypeStruct
    pair = of((ROWS, rows), f32)
    pairs = pltpu.VMEM((ROWS, rows), f32)

    taken = (
        query_lengths, passage_lengths, positives, query_hidden, passage_hidden, projection
    )
    taken = tuple(pltpu.with_memory_space_constraint(x, pltpu.HBM) for x in taken)
    query_unit, query_inverse, sent0, valid, wanted, query_rows, passage_rows, weight = call(
        functools.partial(query_embed_body, queries),
        (
            of((rows, dim), f32), of((rows, dim), f32), of((rows + ROWS, dim), bf16),
            of((ROWS, rows), jnp.int32),
            of((1, rows), jnp.int32), of((rows, width), bf16), of((slots, width), bf16),
            of((width, dim), bf16),
        ),
        (hbm,) * 6,
        taken,
        scratch=(
            pltpu.SMEM((queries,), jnp.int32),
            pltpu.SMEM((passages,), jnp.int32),
            pltpu.SMEM((queries,), jnp.int32),
            pltpu.SemaphoreType.DMA((6,)),
        ),
        flops=2 * rows * width * dim,
    )
    sent1 = shifted(sent0, "batch", 1)
    (
        passage_unit, passage_inverse, embed, turned, powers0, totals0, scores0, log0, far_sent
    ) = call(
        functools.partial(own_score_body, queries, passages),
        (
            of((slots, dim), f32), of((slots, dim), f32), of((slots, dim), bf16),
            of((dim, slots), bf16), of((slots, rows), f32), pair, pair, of((8, rows), f32),
            of((rows + ROWS, dim), bf16),
        ),
        (vmem,) * 4,
        (valid, passage_rows, weight, sent0),
        scratch=(pairs,),
        flops=2 * slots * dim * (width + rows),
        trans=slots * rows,
    )
    sent2 = shifted(far_sent, "batch", 2)
    block_outs = (of((slots, rows), f32), pair, pair, of((8, rows), f32))
    message = of((dim + ROWS, rows), bf16)
    powers1, totals1, scores1, logs, near = call(
        functools.partial(near_score_body, queries, passages),
        block_outs + (of((dim, rows), bf16),),
        (vmem,) * 5,
        (valid, embed, turned, sent1, log0),
        scratch=(pairs, pltpu.VMEM((slots, rows), bf16)),
        flops=4 * slots * dim * rows,
        trans=slots * rows,
    )
    logs1 = shifted(logs, "batch", 1)
    powers2, totals2, scores2, log2, back2, back1 = call(
        functools.partial(far_score_body, queries, passages),
        block_outs + (message, message),
        (vmem,) * 6,
        (valid, embed, turned, sent2, near, logs),
        scratch=(pairs, pltpu.VMEM((slots, rows), bf16)),
        flops=4 * slots * dim * rows,
        trans=slots * rows,
    )
    back2 = shifted(back2, "batch", -2)
    back1 = shifted(back1, "batch", -1)
    pair_logs = call(
        pair_logs_body,
        (of((8, rows), f32),),
        (vmem,) * 3,
        (logs, logs1, sent2),
        flops=20 * slots * dim * rows,
    )[0]
    losses, query_pre_grad, passage_pre_grad, partial = call(
        functools.partial(grad_body, queries, passages),
        (
            of((1, queries), f32), of((rows, dim), bf16), of((slots, dim), bf16),
            of((width, dim), bf16),
        ),
        (vmem,) * 25,
        (wanted, query_rows, passage_rows, turned,
         query_unit, query_inverse, passage_unit, passage_inverse,
         powers0, powers1, powers2, totals0, totals1, totals2, scores0, scores1, scores2,
         sent0, sent1, sent2, logs, log2, pair_logs, back1, back2),
        scratch=(pltpu.VMEM((slots, 3 * rows), bf16), pltpu.VMEM((3 * rows, dim), bf16)),
        flops=8 * slots * dim * rows + 2 * (slots + rows) * width * dim,
    )
    grad_projection = mean_over_devices(partial)
    grad_query_hidden = dot32(query_pre_grad, weight, NT).astype(bf16)
    grad_passage_hidden = dot32(passage_pre_grad, weight, NT).astype(bf16)
    losses = losses.reshape(queries)
    return (losses, grad_query_hidden, grad_passage_hidden, grad_projection)


def solution(mesh):
    in_specs = (
        P(("batch", "mp"), None),
        P(("batch", "mp"), None),
        P(),
        P(("batch", "mp")),
        P(("batch", "mp")),
        P(("batch", "mp")),
    )
    out_specs = (P(("batch", "mp")), P(("batch", "mp"), None), P(("batch", "mp"), None), P())
    return jax.shard_map(
        per_device, mesh=mesh, in_specs=in_specs, out_specs=out_specs, check_vma=False
    )
```

```python
import functools
import math

import jax
import jax.numpy as jnp
from jax import lax
from jax.experimental import pallas as pl
from jax.experimental.pallas import tpu as pltpu
from jax.sharding import PartitionSpec as P

inner_scale = 128.0
outer_scale = 8.0
loss_scale = 32.0
norm_eps = 1e-06

LANES = 128
ROWS = 16
LOG2E = 1.0 / math.log(2.0)
NT = (((1,), (1,)), ((), ()))

vmem = pl.BlockSpec(memory_space=pltpu.VMEM)
hbm = pl.BlockSpec(memory_space=pltpu.HBM)


def shifted(block, axis, distance):
    devices = range(lax.axis_size(axis))
    route = [((i - distance) % len(devices), i) for i in devices]
    return lax.ppermute(block, axis, route)


def dot32(left, right, dims=(((1,), (0,)), ((), ()))):
    return lax.dot_general(left, right, dims, preferred_element_type=jnp.float32)


def call(body, outs, in_specs, args, scratch=(), flops=0, trans=0, out_specs=None):
    moved = sum(a.size * a.dtype.itemsize for a in args)
    moved += sum(math.prod(o.shape) * jnp.dtype(o.dtype).itemsize for o in outs)
    return pl.pallas_call(
        body,
        out_shape=tuple(outs),
        in_specs=list(in_specs),
        out_specs=out_specs or tuple(vmem for _ in outs),
        scratch_shapes=list(scratch),
        compiler_params=pltpu.CompilerParams(vmem_limit_bytes=24 * 2**20),
        cost_estimate=pl.CostEstimate(flops=flops, bytes_accessed=moved, transcendentals=trans),
    )(*args)


def spread(values, count, group):
    lane = lax.broadcasted_iota(jnp.int32, (1, count * group), 1) // group
    row = jnp.zeros((1, count * group), jnp.int32)
    for item in range(count):
        row = jnp.where(lane == item, values[item], row)
    return row


def keep_row(lengths, queries, tokens):
    slot = lax.broadcasted_iota(jnp.int32, (1, queries * tokens), 1) % tokens
    return (slot < spread(lengths, queries, tokens)).astype(jnp.float32)


def unit_rows(before):
    inverse = lax.rsqrt(jnp.sum(before * before, axis=1, keepdims=True) + norm_eps)
    return before * inverse, inverse


def back_rows(grad, unit, inverse):
    inner = jnp.sum(unit * grad, axis=1, keepdims=True)
    return ((grad - unit * inner) * inverse).astype(jnp.bfloat16)


def load_all(pairs, sems):
    copies = [pltpu.make_async_copy(a, b, sems.at[i]) for i, (a, b) in enumerate(pairs)]
    for copy in copies:
        copy.start()
    return copies


def query_embed_body(
    queries, query_lengths_in, passage_lengths_in, positives_in, query_hidden_in, passage_hidden_in,
    projection_in,
    unit_out, inverse_out, sent_out, slots_out, wanted_out, query_hidden, passage_hidden, projection,
    query_lengths, passage_lengths, positives, sems,
):
    pairs = [
        (projection_in, projection), (query_hidden_in, query_hidden),
        (query_lengths_in, query_lengths), (positives_in, positives),
        (passage_lengths_in, passage_lengths),
    ]
    pieces = sems.shape[0] - len(pairs)
    size = passage_hidden.shape[0] // pieces
    parts = [pl.ds(piece * size, size) for piece in range(pieces)]
    pairs += [(passage_hidden_in.at[part], passage_hidden.at[part]) for part in parts]
    copies = load_all(pairs, sems)
    copies[0].wait()
    copies[1].wait()
    rows = query_hidden.shape[0]
    before = dot32(query_hidden[...], projection[...])
    unit, inverse = unit_rows(before)
    unit_out[...] = unit
    inverse_out[...] = jnp.broadcast_to(inverse, unit.shape)
    sent_out[:rows, :] = unit.astype(jnp.bfloat16)
    copies[2].wait()
    keep = keep_row(query_lengths, queries, rows // queries)
    row = lax.broadcasted_iota(jnp.int32, (ROWS, LANES), 0)
    tail = jnp.zeros((ROWS, LANES), jnp.float32)
    for piece in range(rows // LANES):
        tail = jnp.where(row == piece, keep[:, piece * LANES : (piece + 1) * LANES], tail)
    sent_out[rows:, :] = tail.astype(jnp.bfloat16)
    copies[3].wait()
    wanted_out[...] = spread(positives, queries, rows // queries)
    copies[4].wait()
    c = lax.broadcasted_iota(jnp.int32, slots_out.shape, 0)
    valid = jnp.zeros(slots_out.shape, jnp.int32)
    for item in range(passage_lengths.shape[0]):
        valid = jnp.where(c == item, passage_lengths[item], valid)
    slots_out[...] = valid
    for copy in copies[5:]:
        copy.wait()


def sent_keep(sent, rows):
    tail = sent[rows:, :].astype(jnp.float32)
    return jnp.concatenate([tail[i : i + 1, :] for i in range(rows // LANES)], axis=1)


def split(values):
    high = values.astype(jnp.bfloat16)
    rest = values - high.astype(jnp.float32)
    middle = rest.astype(jnp.bfloat16)
    return high, middle, (rest - middle.astype(jnp.float32)).astype(jnp.bfloat16)


def score_block(queries, passages, valid, embed, sent, powers, totals, scores, tops):
    rows = sent.shape[0] - ROWS
    tokens = embed.shape[0] // passages
    query = sent[:rows, :]
    half = tokens // 2
    slot = lax.broadcasted_iota(jnp.int32, (tokens - half, rows), 0) + half
    totals[...] = jnp.ones(totals.shape, jnp.float32)
    tops[...] = jnp.zeros(tops.shape, jnp.float32)
    for c in range(passages):
        sims = dot32(embed[c * tokens : (c + 1) * tokens, :], query, NT)
        low, high = sims[:half], jnp.where(slot < valid[c : c + 1, :], sims[half:], -jnp.inf)
        top = jnp.maximum(
            jnp.max(low, axis=0, keepdims=True), jnp.max(high, axis=0, keepdims=True)
        )
        low = jnp.exp2((low - top) * (inner_scale * LOG2E))
        high = jnp.exp2((high - top) * (inner_scale * LOG2E))
        powers[c * tokens : c * tokens + half, :] = low
        powers[c * tokens + half : (c + 1) * tokens, :] = high
        tops[c : c + 1, :] = top
        totals[c : c + 1, :] = jnp.sum(low, axis=0, keepdims=True) + jnp.sum(
            high, axis=0, keepdims=True
        )
    best = tops[...] + jnp.log(totals[...]) / inner_scale
    best = best * sent_keep(sent, rows)
    group = rows // queries
    same = lax.broadcasted_iota(jnp.int32, (rows, rows), 0) // group
    same = (same == lax.broadcasted_iota(jnp.int32, (rows, rows), 1) // group).astype(jnp.bfloat16)
    total = sum(dot32(part, same) for part in split(best))
    c = lax.broadcasted_iota(jnp.int32, total.shape, 0)
    scores[...] = jnp.where(c < passages, outer_scale * total, -jnp.inf)


def own_score_body(
    queries, passages, valid, hidden, projection, sent,
    unit_out, inverse_out, embed_out, turned_out, powers, totals, scores, log_out, tops,
):
    unit, inverse = unit_rows(dot32(hidden[...], projection[...]))
    unit_out[...] = unit
    inverse_out[...] = jnp.broadcast_to(inverse, unit.shape)
    embed = unit.astype(jnp.bfloat16)
    embed_out[...] = embed
    score_block(queries, passages, valid, embed_out, sent, powers, totals, scores, tops)
    log_out[...] = stack_rows(log_out.shape, (log_sum(scores[...]),))
    turned_out[...] = embed.T


def log_sum(scores):
    top = jnp.max(scores, axis=0, keepdims=True)
    return top + jnp.log(jnp.sum(jnp.exp(scores - top), axis=0, keepdims=True))


def log_add(parts):
    top = functools.reduce(jnp.maximum, parts)
    return top + jnp.log(sum(jnp.exp(part - top) for part in parts))


def stack_rows(shape, rows):
    index = lax.broadcasted_iota(jnp.int32, shape, 0)
    tile = jnp.zeros(shape, jnp.float32)
    for place, row in enumerate(rows):
        tile = jnp.where(index == place, row, tile)
    return tile


def fill_grad_sim(passages, coefficient, powers, out, column):
    tokens = powers.shape[0] // passages
    rows = powers.shape[1]
    for c in range(passages):
        part = slice(c * tokens, (c + 1) * tokens)
        out[part, column : column + rows] = (powers[part, :] * coefficient[c : c + 1, :]).astype(
            jnp.bfloat16
        )


def send_back(passages, turned, sent, powers, totals, scores, log, tail, back, grad_sim):
    dim, rows = turned.shape[0], powers.shape[1]
    dscore = loss_scale * jnp.exp(scores[...] - log)
    coefficient = outer_scale * dscore * sent_keep(sent, rows) / totals[...]
    fill_grad_sim(passages, coefficient, powers, grad_sim, 0)
    back[:dim, :] = dot32(turned[...], grad_sim[...]).astype(jnp.bfloat16)
    tail = stack_rows((ROWS, rows), [part.astype(jnp.float32) for part in tail])
    back[dim:, :] = tail.astype(jnp.bfloat16)


def far_score_body(
    queries, passages, valid, embed, turned, sent,
    powers, totals, scores, log_out, back, tops, grad_sim,
):
    score_block(queries, passages, valid, embed, sent, powers, totals, scores, tops)
    log = log_sum(scores[...])
    log_out[...] = stack_rows(log_out.shape, (log,))
    send_back(passages, turned, sent, powers, totals, scores, log, split(log), back, grad_sim)


def near_score_body(
    queries, passages, valid, embed, turned, sent, log0, log2, far0,
    powers, totals, scores, logs, back, tops, grad_sim,
):
    score_block(queries, passages, valid, embed, sent, powers, totals, scores, tops)
    log = log_sum(scores[...])
    other = log2[0:1, :]
    logs[...] = stack_rows(logs.shape, (log0[0:1, :], log, other, far0[0:1, :]))
    tail = split(log) + split(other)
    send_back(passages, turned, sent, powers, totals, scores, log, tail, back, grad_sim)


def joined(back, dim, place):
    tail = back[dim:, :].astype(jnp.float32)
    high, middle, low = [tail[i : i + 1, :] for i in range(place, place + 3)]
    return high + (middle + low)


def grad_body(
    queries, passages, wanted, query_hidden, passage_hidden, turned,
    query_unit, query_inverse, passage_unit, passage_inverse,
    powers0, powers1, powers2, totals0, totals1, totals2, scores0, scores1, scores2,
    sent0, sent1, sent2, logs, logs1, back1, back2,
    all_logs, wanted_logs, query_pre_grad, passage_pre_grad, partial, grad_sim, query_rows,
):
    rows = powers0.shape[1]
    dim = turned.shape[0]
    second, third = joined(back1, dim, 0), joined(back2, dim, 0)
    total0 = log_add((logs[0:1, :], second, third))
    total1 = log_add((logs1[0:1, :], logs[1:2, :], joined(back1, dim, 3)))
    total2 = log_add((logs[3:4, :], logs1[1:2, :], logs[2:3, :]))
    scores = scores0[...]
    onehot = lax.broadcasted_iota(jnp.int32, scores.shape, 0) == wanted[...]
    wanted_score = jnp.sum(jnp.where(onehot, scores, 0.0), axis=0, keepdims=True)
    pick = lax.broadcasted_iota(jnp.int32, (rows, LANES), 1) * (rows // queries)
    pick = (pick == lax.broadcasted_iota(jnp.int32, (rows, LANES), 0)).astype(jnp.bfloat16)
    lines = [part.astype(jnp.float32) for part in split(total0) + split(wanted_score)]
    lines = dot32(stack_rows((ROWS, rows), lines).astype(jnp.bfloat16), pick)[:, :queries]
    all_logs[...] = lines[0:1] + (lines[1:2] + lines[2:3])
    wanted_logs[...] = lines[3:4] + (lines[4:5] + lines[5:6])

    for block, (total, query, powers, totals, scores) in enumerate((
        (total0, sent0, powers0, totals0, scores0),
        (total1, sent1, powers1, totals1, scores1),
        (total2, sent2, powers2, totals2, scores2),
    )):
        dscore = jnp.exp(scores[...] - total)
        if block == 0:
            dscore = dscore - onehot.astype(jnp.float32)
        coefficient = (outer_scale * loss_scale) * dscore * sent_keep(query, rows) / totals[...]
        fill_grad_sim(passages, coefficient, powers, grad_sim, block * rows)
        query_rows[block * rows : (block + 1) * rows, :] = query[:rows, :]

    grad = dot32(grad_sim[...], query_rows[...])
    pre = back_rows(grad, passage_unit[...], passage_inverse[...])
    passage_pre_grad[...] = pre
    both = dot32(pre.T, passage_hidden[...])
    to_query = dot32(turned[...], grad_sim[:, :rows])
    to_query += back1[:dim, :].astype(jnp.float32) * jnp.exp(second - total0)
    to_query += back2[:dim, :].astype(jnp.float32) * jnp.exp(third - total0)
    pre = back_rows(to_query.T, query_unit[...], query_inverse[...])
    query_pre_grad[...] = pre
    both += dot32(pre.T, query_hidden[...])
    partial[...] = both.T.astype(jnp.bfloat16)


def sum_body(scale, copies, pieces, out):
    total = jnp.sum(pieces[...].astype(jnp.float32), axis=0) * scale
    total = total.astype(jnp.bfloat16)
    for copy in range(copies):
        out[copy] = total


def cast_body(count, source, out, wide, sems):
    size = source.shape[0] // count
    copies = []
    for piece in range(count):
        part = pl.ds(piece * size, size)
        wide[part, :] = source[part, :].astype(jnp.float32)
        copies.append(pltpu.make_async_copy(wide.at[part], out.at[part], sems.at[piece]))
        copies[-1].start()
    for copy in copies:
        copy.wait()


def mean_over_devices(partial, later):
    axes = ("batch", "mp")
    devices = lax.axis_size("batch") * lax.axis_size("mp")
    rows, columns = partial.shape
    share = -(-rows // (devices * 8)) * 8
    padded = jnp.pad(partial, ((0, share * devices - rows), (0, 0)))
    pieces = lax.all_to_all(padded.reshape(devices, share, columns), axes, 0, 0)
    pieces, later = lax.optimization_barrier((pieces, later))
    means = call(
        functools.partial(sum_body, 1.0 / devices, devices),
        (jax.ShapeDtypeStruct(pieces.shape, jnp.bfloat16),),
        (vmem,),
        (pieces,),
    )[0]
    whole = lax.all_to_all(means, axes, 0, 0)
    whole = whole.reshape(devices * share, columns)[:rows]
    count = 4 if rows % 64 == 0 else 1
    whole = call(
        functools.partial(cast_body, count),
        (jax.ShapeDtypeStruct((rows, columns), jnp.float32),),
        (vmem,),
        (whole,),
        scratch=(pltpu.VMEM((rows, columns), jnp.float32), pltpu.SemaphoreType.DMA((count,))),
        out_specs=(hbm,),
    )[0]
    return whole, later


def per_device(query_hidden, passage_hidden, projection, query_lengths, passage_lengths, positives):
    queries = query_lengths.shape[0]
    passages = passage_lengths.shape[0]
    rows, width = query_hidden.shape
    slots = passage_hidden.shape[0]
    dim = projection.shape[1]
    f32, bf16 = jnp.float32, jnp.bfloat16
    of = jax.ShapeDtypeStruct
    pair = of((ROWS, rows), f32)
    pairs = pltpu.VMEM((ROWS, rows), f32)
    pieces = passages // 2 if passages % 2 == 0 else passages

    taken = (
        query_lengths, passage_lengths, positives, query_hidden, passage_hidden, projection
    )
    taken = tuple(pltpu.with_memory_space_constraint(x, pltpu.HBM) for x in taken)
    query_unit, query_inverse, sent0, valid, wanted, query_rows, passage_rows, weight = call(
        functools.partial(query_embed_body, queries),
        (
            of((rows, dim), f32), of((rows, dim), f32), of((rows + ROWS, dim), bf16),
            of((ROWS, rows), jnp.int32),
            of((1, rows), jnp.int32), of((rows, width), bf16), of((slots, width), bf16),
            of((width, dim), bf16),
        ),
        (hbm,) * 6,
        taken,
        scratch=(
            pltpu.SMEM((queries,), jnp.int32),
            pltpu.SMEM((passages,), jnp.int32),
            pltpu.SMEM((queries,), jnp.int32),
            pltpu.SemaphoreType.DMA((5 + pieces,)),
        ),
        flops=2 * rows * width * dim,
    )
    sent1 = shifted(sent0, "batch", 1)
    sent2 = shifted(sent0, "batch", 2)
    (
        passage_unit, passage_inverse, embed, turned, powers0, totals0, scores0, log0
    ) = call(
        functools.partial(own_score_body, queries, passages),
        (
            of((slots, dim), f32), of((slots, dim), f32), of((slots, dim), bf16),
            of((dim, slots), bf16), of((slots, rows), f32), pair, pair, of((8, rows), f32),
        ),
        (vmem,) * 4,
        (valid, passage_rows, weight, sent0),
        scratch=(pairs,),
        flops=2 * slots * dim * (width + rows),
        trans=slots * rows,
    )
    far0 = shifted(log0, "batch", 2)
    block_outs = (
        of((slots, rows), f32), pair, pair, of((8, rows), f32), of((dim + ROWS, rows), bf16)
    )
    powers2, totals2, scores2, log2, back2 = call(
        functools.partial(far_score_body, queries, passages),
        block_outs,
        (vmem,) * 4,
        (valid, embed, turned, sent2),
        scratch=(pairs, pltpu.VMEM((slots, rows), bf16)),
        flops=4 * slots * dim * rows,
        trans=slots * rows,
    )
    back2 = shifted(back2, "batch", -2)
    powers1, totals1, scores1, logs, back1 = call(
        functools.partial(near_score_body, queries, passages),
        block_outs,
        (vmem,) * 7,
        (valid, embed, turned, sent1, log0, log2, far0),
        scratch=(pairs, pltpu.VMEM((slots, rows), bf16)),
        flops=4 * slots * dim * rows,
        trans=slots * rows,
    )
    back1 = shifted(back1, "batch", -1)
    logs1 = shifted(logs, "batch", 1)
    all_logs, wanted_logs, query_pre_grad, passage_pre_grad, partial = call(
        functools.partial(grad_body, queries, passages),
        (
            of((1, queries), f32), of((1, queries), f32), of((rows, dim), bf16),
            of((slots, dim), bf16),
            of((width, dim), bf16),
        ),
        (vmem,) * 24,
        (wanted, query_rows, passage_rows, turned,
         query_unit, query_inverse, passage_unit, passage_inverse,
         powers0, powers1, powers2, totals0, totals1, totals2, scores0, scores1, scores2,
         sent0, sent1, sent2, logs, logs1, back1, back2),
        scratch=(pltpu.VMEM((slots, 3 * rows), bf16), pltpu.VMEM((3 * rows, dim), bf16)),
        flops=8 * slots * dim * rows + 2 * (slots + rows) * width * dim,
    )
    later = (query_pre_grad, passage_pre_grad, all_logs, wanted_logs)
    grad_projection, later = mean_over_devices(partial, later)
    query_pre_grad, passage_pre_grad, all_logs, wanted_logs = later
    grad_query_hidden = dot32(query_pre_grad, weight, NT).astype(bf16)
    grad_passage_hidden = dot32(passage_pre_grad, weight, NT).astype(bf16)
    losses = (all_logs - wanted_logs).reshape(queries)
    return (losses, grad_query_hidden, grad_passage_hidden, grad_projection)


def solution(mesh):
    in_specs = (
        P(("batch", "mp"), None),
        P(("batch", "mp"), None),
        P(),
        P(("batch", "mp")),
        P(("batch", "mp")),
        P(("batch", "mp")),
    )
    out_specs = (P(("batch", "mp")), P(("batch", "mp"), None), P(("batch", "mp"), None), P())
    return jax.shard_map(
        per_device, mesh=mesh, in_specs=in_specs, out_specs=out_specs, check_vma=False
    )
```

```python
import functools
import math

import jax
import jax.numpy as jnp
from jax import lax
from jax.experimental import pallas as pl
from jax.experimental.pallas import tpu as pltpu
from jax.sharding import PartitionSpec as P

inner_scale = 128.0
outer_scale = 8.0
loss_scale = 32.0
norm_eps = 1e-06

LANES = 128
ROWS = 16
LOG2E = 1.0 / math.log(2.0)
NT = (((1,), (1,)), ((), ()))

vmem = pl.BlockSpec(memory_space=pltpu.VMEM)
hbm = pl.BlockSpec(memory_space=pltpu.HBM)


def shifted(block, axis, distance):
    devices = range(lax.axis_size(axis))
    route = [((i - distance) % len(devices), i) for i in devices]
    return lax.ppermute(block, axis, route)


def dot32(left, right, dims=(((1,), (0,)), ((), ()))):
    return lax.dot_general(left, right, dims, preferred_element_type=jnp.float32)


def call(body, outs, in_specs, args, scratch=(), flops=0, trans=0, out_specs=None):
    moved = sum(a.size * a.dtype.itemsize for a in args)
    moved += sum(math.prod(o.shape) * jnp.dtype(o.dtype).itemsize for o in outs)
    return pl.pallas_call(
        body,
        out_shape=tuple(outs),
        in_specs=list(in_specs),
        out_specs=out_specs or tuple(vmem for _ in outs),
        scratch_shapes=list(scratch),
        compiler_params=pltpu.CompilerParams(vmem_limit_bytes=24 * 2**20),
        cost_estimate=pl.CostEstimate(flops=flops, bytes_accessed=moved, transcendentals=trans),
    )(*args)


def spread(values, count, group):
    lane = lax.broadcasted_iota(jnp.int32, (1, count * group), 1) // group
    row = jnp.zeros((1, count * group), jnp.int32)
    for item in range(count):
        row = jnp.where(lane == item, values[item], row)
    return row


def keep_row(lengths, queries, tokens):
    slot = lax.broadcasted_iota(jnp.int32, (1, queries * tokens), 1) % tokens
    return (slot < spread(lengths, queries, tokens)).astype(jnp.float32)


def unit_rows(before):
    inverse = lax.rsqrt(jnp.sum(before * before, axis=1, keepdims=True) + norm_eps)
    return before * inverse, inverse


def back_rows(grad, unit, inverse):
    inner = jnp.sum(unit * grad, axis=1, keepdims=True)
    return ((grad - unit * inner) * inverse).astype(jnp.bfloat16)


def load_all(pairs, sems):
    copies = [pltpu.make_async_copy(a, b, sems.at[i]) for i, (a, b) in enumerate(pairs)]
    for copy in copies:
        copy.start()
    return copies


def query_embed_body(
    queries, query_lengths_in, passage_lengths_in, positives_in, query_hidden_in, passage_hidden_in,
    projection_in,
    unit_out, inverse_out, sent_out, slots_out, wanted_out, query_hidden, passage_hidden, projection,
    query_lengths, passage_lengths, positives, sems,
):
    pairs = [
        (projection_in, projection), (query_hidden_in, query_hidden),
        (query_lengths_in, query_lengths), (positives_in, positives),
        (passage_lengths_in, passage_lengths),
    ]
    pieces = sems.shape[0] - len(pairs)
    size = passage_hidden.shape[0] // pieces
    parts = [pl.ds(piece * size, size) for piece in range(pieces)]
    pairs += [(passage_hidden_in.at[part], passage_hidden.at[part]) for part in parts]
    copies = load_all(pairs, sems)
    copies[0].wait()
    copies[1].wait()
    rows = query_hidden.shape[0]
    before = dot32(query_hidden[...], projection[...])
    unit, inverse = unit_rows(before)
    unit_out[...] = unit
    inverse_out[...] = jnp.broadcast_to(inverse, unit.shape)
    sent_out[:rows, :] = unit.astype(jnp.bfloat16)
    copies[2].wait()
    keep = keep_row(query_lengths, queries, rows // queries)
    row = lax.broadcasted_iota(jnp.int32, (ROWS, LANES), 0)
    tail = jnp.zeros((ROWS, LANES), jnp.float32)
    for piece in range(rows // LANES):
        tail = jnp.where(row == piece, keep[:, piece * LANES : (piece + 1) * LANES], tail)
    sent_out[rows:, :] = tail.astype(jnp.bfloat16)
    copies[3].wait()
    wanted_out[...] = spread(positives, queries, rows // queries)
    copies[4].wait()
    c = lax.broadcasted_iota(jnp.int32, slots_out.shape, 0)
    valid = jnp.zeros(slots_out.shape, jnp.int32)
    for item in range(passage_lengths.shape[0]):
        valid = jnp.where(c == item, passage_lengths[item], valid)
    slots_out[...] = valid
    for copy in copies[5:]:
        copy.wait()


def sent_keep(sent, rows):
    tail = sent[rows:, :].astype(jnp.float32)
    return jnp.concatenate([tail[i : i + 1, :] for i in range(rows // LANES)], axis=1)


def split(values):
    high = values.astype(jnp.bfloat16)
    rest = values - high.astype(jnp.float32)
    middle = rest.astype(jnp.bfloat16)
    return high, middle, (rest - middle.astype(jnp.float32)).astype(jnp.bfloat16)


def score_block(queries, passages, valid, embed, sent, powers, totals, scores, tops):
    rows = sent.shape[0] - ROWS
    tokens = embed.shape[0] // passages
    query = sent[:rows, :]
    half = tokens // 2
    slot = lax.broadcasted_iota(jnp.int32, (tokens - half, rows), 0) + half
    totals[...] = jnp.ones(totals.shape, jnp.float32)
    tops[...] = jnp.zeros(tops.shape, jnp.float32)
    for c in range(passages):
        sims = dot32(embed[c * tokens : (c + 1) * tokens, :], query, NT)
        low, high = sims[:half], jnp.where(slot < valid[c : c + 1, :], sims[half:], -jnp.inf)
        top = jnp.maximum(
            jnp.max(low, axis=0, keepdims=True), jnp.max(high, axis=0, keepdims=True)
        )
        low = jnp.exp2((low - top) * (inner_scale * LOG2E))
        high = jnp.exp2((high - top) * (inner_scale * LOG2E))
        powers[c * tokens : c * tokens + half, :] = low
        powers[c * tokens + half : (c + 1) * tokens, :] = high
        tops[c : c + 1, :] = top
        totals[c : c + 1, :] = jnp.sum(low, axis=0, keepdims=True) + jnp.sum(
            high, axis=0, keepdims=True
        )
    best = tops[...] + jnp.log(totals[...]) / inner_scale
    best = best * sent_keep(sent, rows)
    group = rows // queries
    same = lax.broadcasted_iota(jnp.int32, (rows, rows), 0) // group
    same = (same == lax.broadcasted_iota(jnp.int32, (rows, rows), 1) // group).astype(jnp.bfloat16)
    total = sum(dot32(part, same) for part in split(best))
    c = lax.broadcasted_iota(jnp.int32, total.shape, 0)
    scores[...] = jnp.where(c < passages, outer_scale * total, -jnp.inf)


def own_score_body(
    queries, passages, valid, hidden, projection, sent,
    unit_out, inverse_out, embed_out, turned_out, powers, totals, scores, log_out, tops,
):
    unit, inverse = unit_rows(dot32(hidden[...], projection[...]))
    unit_out[...] = unit
    inverse_out[...] = jnp.broadcast_to(inverse, unit.shape)
    embed = unit.astype(jnp.bfloat16)
    embed_out[...] = embed
    score_block(queries, passages, valid, embed_out, sent, powers, totals, scores, tops)
    log_out[...] = stack_rows(log_out.shape, (log_sum(scores[...]),))
    turned_out[...] = embed.T


def log_sum(scores):
    top = jnp.max(scores, axis=0, keepdims=True)
    return top + jnp.log(jnp.sum(jnp.exp(scores - top), axis=0, keepdims=True))


def log_add(parts):
    top = functools.reduce(jnp.maximum, parts)
    return top + jnp.log(sum(jnp.exp(part - top) for part in parts))


def stack_rows(shape, rows):
    index = lax.broadcasted_iota(jnp.int32, shape, 0)
    tile = jnp.zeros(shape, jnp.float32)
    for place, row in enumerate(rows):
        tile = jnp.where(index == place, row, tile)
    return tile


def fill_grad_sim(passages, coefficient, powers, out, column):
    tokens = powers.shape[0] // passages
    rows = powers.shape[1]
    for c in range(passages):
        part = slice(c * tokens, (c + 1) * tokens)
        out[part, column : column + rows] = (powers[part, :] * coefficient[c : c + 1, :]).astype(
            jnp.bfloat16
        )


def send_back(passages, turned, sent, powers, totals, scores, log, tail, back, grad_sim):
    dim, rows = turned.shape[0], powers.shape[1]
    dscore = loss_scale * jnp.exp(scores[...] - log)
    coefficient = outer_scale * dscore * sent_keep(sent, rows) / totals[...]
    fill_grad_sim(passages, coefficient, powers, grad_sim, 0)
    back[:dim, :] = dot32(turned[...], grad_sim[...]).astype(jnp.bfloat16)
    tail = stack_rows((ROWS, rows), [part.astype(jnp.float32) for part in tail])
    back[dim:, :] = tail.astype(jnp.bfloat16)


def far_score_body(
    queries, passages, valid, embed, turned, sent,
    powers, totals, scores, log_out, back, tops, grad_sim,
):
    score_block(queries, passages, valid, embed, sent, powers, totals, scores, tops)
    log = log_sum(scores[...])
    log_out[...] = stack_rows(log_out.shape, (log,))
    send_back(passages, turned, sent, powers, totals, scores, log, split(log), back, grad_sim)


def near_score_body(
    queries, passages, valid, embed, turned, sent, log0, log2, far0,
    powers, totals, scores, logs, back, tops, grad_sim,
):
    score_block(queries, passages, valid, embed, sent, powers, totals, scores, tops)
    log = log_sum(scores[...])
    other = log2[0:1, :]
    logs[...] = stack_rows(logs.shape, (log0[0:1, :], log, other, far0[0:1, :]))
    tail = split(log) + split(other)
    send_back(passages, turned, sent, powers, totals, scores, log, tail, back, grad_sim)


def joined(back, dim, place):
    tail = back[dim:, :].astype(jnp.float32)
    high, middle, low = [tail[i : i + 1, :] for i in range(place, place + 3)]
    return high + (middle + low)


def pair_logs_body(logs, logs1, back2, out):
    out[...] = stack_rows(out.shape, (
        log_add((logs1[0:1, :], logs[1:2, :])), log_add((logs[3:4, :], logs1[1:2, :])),
        joined(back2, back2.shape[0] - ROWS, 0),
    ))


def grad_body(
    queries, passages, wanted, query_hidden, passage_hidden, turned,
    query_unit, query_inverse, passage_unit, passage_inverse,
    powers0, powers1, powers2, totals0, totals1, totals2, scores0, scores1, scores2,
    sent0, sent1, sent2, logs, pair_logs, back1, back2,
    all_logs, wanted_logs, query_pre_grad, passage_pre_grad, partial, grad_sim, query_rows,
):
    rows = powers0.shape[1]
    dim = turned.shape[0]
    second, third = joined(back1, dim, 0), pair_logs[2:3, :]
    total0 = log_add((logs[0:1, :], second, third))
    total1 = log_add((pair_logs[0:1, :], joined(back1, dim, 3)))
    total2 = log_add((pair_logs[1:2, :], logs[2:3, :]))
    scores = scores0[...]
    onehot = lax.broadcasted_iota(jnp.int32, scores.shape, 0) == wanted[...]
    wanted_score = jnp.sum(jnp.where(onehot, scores, 0.0), axis=0, keepdims=True)
    pick = lax.broadcasted_iota(jnp.int32, (rows, LANES), 1) * (rows // queries)
    pick = (pick == lax.broadcasted_iota(jnp.int32, (rows, LANES), 0)).astype(jnp.bfloat16)
    lines = [part.astype(jnp.float32) for part in split(total0) + split(wanted_score)]
    lines = dot32(stack_rows((ROWS, rows), lines).astype(jnp.bfloat16), pick)[:, :queries]
    all_logs[...] = lines[0:1] + (lines[1:2] + lines[2:3])
    wanted_logs[...] = lines[3:4] + (lines[4:5] + lines[5:6])

    for block, (total, query, powers, totals, scores) in enumerate((
        (total0, sent0, powers0, totals0, scores0),
        (total1, sent1, powers1, totals1, scores1),
        (total2, sent2, powers2, totals2, scores2),
    )):
        dscore = jnp.exp(scores[...] - total)
        if block == 0:
            dscore = dscore - onehot.astype(jnp.float32)
        coefficient = (outer_scale * loss_scale) * dscore * sent_keep(query, rows) / totals[...]
        fill_grad_sim(passages, coefficient, powers, grad_sim, block * rows)
        query_rows[block * rows : (block + 1) * rows, :] = query[:rows, :]

    grad = dot32(grad_sim[...], query_rows[...])
    pre = back_rows(grad, passage_unit[...], passage_inverse[...])
    passage_pre_grad[...] = pre
    both = dot32(pre.T, passage_hidden[...])
    to_query = dot32(turned[...], grad_sim[:, :rows])
    to_query += back1[:dim, :].astype(jnp.float32) * jnp.exp(second - total0)
    to_query += back2[:dim, :].astype(jnp.float32) * jnp.exp(third - total0)
    pre = back_rows(to_query.T, query_unit[...], query_inverse[...])
    query_pre_grad[...] = pre
    both += dot32(pre.T, query_hidden[...])
    partial[...] = both.T.astype(jnp.bfloat16)


def sum_body(scale, copies, pieces, out):
    total = jnp.sum(pieces[...].astype(jnp.float32), axis=0) * scale
    total = total.astype(jnp.bfloat16)
    for copy in range(copies):
        out[copy] = total


def cast_body(count, source, out, wide, sems):
    size = source.shape[0] // count
    copies = []
    for piece in range(count):
        part = pl.ds(piece * size, size)
        wide[part, :] = source[part, :].astype(jnp.float32)
        copies.append(pltpu.make_async_copy(wide.at[part], out.at[part], sems.at[piece]))
        copies[-1].start()
    for copy in copies:
        copy.wait()


def mean_over_devices(partial, later):
    axes = ("batch", "mp")
    devices = lax.axis_size("batch") * lax.axis_size("mp")
    rows, columns = partial.shape
    share = -(-rows // (devices * 8)) * 8
    padded = jnp.pad(partial, ((0, share * devices - rows), (0, 0)))
    pieces = lax.all_to_all(padded.reshape(devices, share, columns), axes, 0, 0)
    pieces, later = lax.optimization_barrier((pieces, later))
    means = call(
        functools.partial(sum_body, 1.0 / devices, devices),
        (jax.ShapeDtypeStruct(pieces.shape, jnp.bfloat16),),
        (vmem,),
        (pieces,),
    )[0]
    whole = lax.all_to_all(means, axes, 0, 0)
    whole = whole.reshape(devices * share, columns)[:rows]
    count = 4 if rows % 64 == 0 else 1
    whole = call(
        functools.partial(cast_body, count),
        (jax.ShapeDtypeStruct((rows, columns), jnp.float32),),
        (vmem,),
        (whole,),
        scratch=(pltpu.VMEM((rows, columns), jnp.float32), pltpu.SemaphoreType.DMA((count,))),
        out_specs=(hbm,),
    )[0]
    return whole, later


def per_device(query_hidden, passage_hidden, projection, query_lengths, passage_lengths, positives):
    queries = query_lengths.shape[0]
    passages = passage_lengths.shape[0]
    rows, width = query_hidden.shape
    slots = passage_hidden.shape[0]
    dim = projection.shape[1]
    f32, bf16 = jnp.float32, jnp.bfloat16
    of = jax.ShapeDtypeStruct
    pair = of((ROWS, rows), f32)
    pairs = pltpu.VMEM((ROWS, rows), f32)
    pieces = passages // 2 if passages % 2 == 0 else passages

    taken = (
        query_lengths, passage_lengths, positives, query_hidden, passage_hidden, projection
    )
    taken = tuple(pltpu.with_memory_space_constraint(x, pltpu.HBM) for x in taken)
    query_unit, query_inverse, sent0, valid, wanted, query_rows, passage_rows, weight = call(
        functools.partial(query_embed_body, queries),
        (
            of((rows, dim), f32), of((rows, dim), f32), of((rows + ROWS, dim), bf16),
            of((ROWS, rows), jnp.int32),
            of((1, rows), jnp.int32), of((rows, width), bf16), of((slots, width), bf16),
            of((width, dim), bf16),
        ),
        (hbm,) * 6,
        taken,
        scratch=(
            pltpu.SMEM((queries,), jnp.int32),
            pltpu.SMEM((passages,), jnp.int32),
            pltpu.SMEM((queries,), jnp.int32),
            pltpu.SemaphoreType.DMA((5 + pieces,)),
        ),
        flops=2 * rows * width * dim,
    )
    sent1 = shifted(sent0, "batch", 1)
    sent2 = shifted(sent0, "batch", 2)
    (
        passage_unit, passage_inverse, embed, turned, powers0, totals0, scores0, log0
    ) = call(
        functools.partial(own_score_body, queries, passages),
        (
            of((slots, dim), f32), of((slots, dim), f32), of((slots, dim), bf16),
            of((dim, slots), bf16), of((slots, rows), f32), pair, pair, of((8, rows), f32),
        ),
        (vmem,) * 4,
        (valid, passage_rows, weight, sent0),
        scratch=(pairs,),
        flops=2 * slots * dim * (width + rows),
        trans=slots * rows,
    )
    far0 = shifted(log0, "batch", 2)
    block_outs = (
        of((slots, rows), f32), pair, pair, of((8, rows), f32), of((dim + ROWS, rows), bf16)
    )
    powers2, totals2, scores2, log2, back2 = call(
        functools.partial(far_score_body, queries, passages),
        block_outs,
        (vmem,) * 4,
        (valid, embed, turned, sent2),
        scratch=(pairs, pltpu.VMEM((slots, rows), bf16)),
        flops=4 * slots * dim * rows,
        trans=slots * rows,
    )
    back2 = shifted(back2, "batch", -2)
    powers1, totals1, scores1, logs, back1 = call(
        functools.partial(near_score_body, queries, passages),
        block_outs,
        (vmem,) * 7,
        (valid, embed, turned, sent1, log0, log2, far0),
        scratch=(pairs, pltpu.VMEM((slots, rows), bf16)),
        flops=4 * slots * dim * rows,
        trans=slots * rows,
    )
    back1 = shifted(back1, "batch", -1)
    logs1 = shifted(logs, "batch", 1)
    pair_logs = call(
        pair_logs_body,
        (of((8, rows), f32),),
        (vmem,) * 3,
        (logs, logs1, back2),
        flops=20 * slots * dim * rows,
    )[0]
    all_logs, wanted_logs, query_pre_grad, passage_pre_grad, partial = call(
        functools.partial(grad_body, queries, passages),
        (
            of((1, queries), f32), of((1, queries), f32), of((rows, dim), bf16),
            of((slots, dim), bf16),
            of((width, dim), bf16),
        ),
        (vmem,) * 24,
        (wanted, query_rows, passage_rows, turned,
         query_unit, query_inverse, passage_unit, passage_inverse,
         powers0, powers1, powers2, totals0, totals1, totals2, scores0, scores1, scores2,
         sent0, sent1, sent2, logs, pair_logs, back1, back2),
        scratch=(pltpu.VMEM((slots, 3 * rows), bf16), pltpu.VMEM((3 * rows, dim), bf16)),
        flops=8 * slots * dim * rows + 2 * (slots + rows) * width * dim,
    )
    later = (query_pre_grad, passage_pre_grad, all_logs, wanted_logs)
    grad_projection, later = mean_over_devices(partial, later)
    query_pre_grad, passage_pre_grad, all_logs, wanted_logs = later
    grad_query_hidden = dot32(query_pre_grad, weight, NT).astype(bf16)
    grad_passage_hidden = dot32(passage_pre_grad, weight, NT).astype(bf16)
    losses = (all_logs - wanted_logs).reshape(queries)
    return (losses, grad_query_hidden, grad_passage_hidden, grad_projection)


def solution(mesh):
    in_specs = (
        P(("batch", "mp"), None),
        P(("batch", "mp"), None),
        P(),
        P(("batch", "mp")),
        P(("batch", "mp")),
        P(("batch", "mp")),
    )
    out_specs = (P(("batch", "mp")), P(("batch", "mp"), None), P(("batch", "mp"), None), P())
    return jax.shard_map(
        per_device, mesh=mesh, in_specs=in_specs, out_specs=out_specs, check_vma=False
    )
```
